32 devices in a mesh: groups: 2 (over x), row: 16 (over z, y, core).
Axes of the slice: x: 2, y: 2, z: 4, core: 2. Of those that a mesh axis runs over, the one named last changes fastest.
Arguments:
- pair: bfloat16 [1024, 512, 128], P(('groups', 'row')), parts along dimension 0, may hold values from -6 to 6
- window_rows: int32 [256], P(('groups', 'row')), parts along dimension 0, may hold values from 0 to 511, as said below
- token_mask: int32 [1024], P('groups'), parts along dimension 0, may hold values from 0 to 1, as said below
- chain_ids: int32 [1024], P('groups'), parts along dimension 0, may hold values from 0 to 3, never falling along the last dimension, each value on 1 to 256 neighbouring positions
- ln_gain: float32 [128], replicated, may hold values from 0.1 to 1.9
- ln_shift: float32 [128], replicated, may hold values from -3 to 3
- w_project: bfloat16 [128, 512], replicated, may hold values from -0.5 to 0.5
- gate_bias: float32 [128], replicated, may hold values from -4 to 4
- w_bias: bfloat16 [128, 4], replicated
- chain_bias: float32 [4], replicated, may hold values from -8 to 8
- w_out: bfloat16 [128, 128], replicated, may hold values from -0.5 to 0.5
Outputs:
- update: bfloat16 [256, 512, 128], P('groups', 'row'), parts along dimension 0
The draws below stay inside these ranges and needn't reach their ends.
There are 2 independent parts, one for each index of `groups`. The reference program is written for one: setup_inputs(seed, part) draws one part's arguments, and reference() takes and returns one part's arrays. A program takes and returns all parts, laid end to end along the dimension named above; an argument that names none is the same for every part. Nothing has to cross between parts.
Inputs may be any that keep to these rules, and one draw needn't show every extreme that they name: `window_rows`: window slot w names a pair row from (w // 8) * 32 to (w // 8) * 32 + 31; the slots name distinct rows. `token_mask`: exactly 384 entries are 1. `chain_ids`: chain numbers never fall along the tokens.
All inputs are finite; a program needn't handle non-finite values.
Results may differ from the reference program's by a relative error of at most 0.0023.
The reference program's roundings to bfloat16 on the way (of `normed`, `bias`, `weights` and `gated`) count: a program that leaves them out, or rounds other values in their place, can miss the bound.
Values may be sent and summed in bfloat16 or wider, within the bound.
No kernel may reach another device: no remote copies, remote signals or barrier semaphores. Data moves between devices by JAX's collectives and lax.ppermute only.
A program may use at most 256 MiB of HBM per device.

```python
import math
import jax
import jax.numpy as jnp
import numpy as np
from jax import lax

C = 128
HEADS = 4
HEAD_DIM = 32
ROWS_DEV = 32
WIN_DEV = 8
CHAINS = 4
TOKENS = 512
WIN = 128
LIVE = 384


def draw_window_rows(key, part):
    blocks = WIN // WIN_DEV
    ranking = jax.random.randint(key, (blocks, ROWS_DEV), 0, 1 << 20) * ROWS_DEV + jnp.arange(ROWS_DEV, dtype=jnp.int32)[None, :]
    chosen = jnp.argsort(ranking, axis=1)[:, :WIN_DEV].astype(jnp.int32)
    starts = (jnp.arange(blocks, dtype=jnp.int32) * ROWS_DEV)[:, None]
    return (chosen + starts).reshape(WIN).astype(jnp.int32)


def draw_token_mask(key, part):
    permuted = jax.random.permutation(key, TOKENS).astype(jnp.int32)
    return (permuted < LIVE).astype(jnp.int32)


def draw_w_bias(key, part):
    base = jax.random.normal(key, (C, HEADS), jnp.float32) * C ** (-0.5)
    return base.astype(jnp.bfloat16)


def block_scale(rng, shape, split, least, high):
    factor_of = 1.0
    for axis_at, shards_of in split:
        steps = jax.random.uniform(jax.random.fold_in(jax.random.fold_in(rng, 6), axis_at), (shards_of,), jnp.float32, least / len(split), high / len(split))
        factor_of = factor_of * jnp.repeat(jnp.exp(steps), shape[axis_at] // shards_of).reshape((-1,) + (1,) * (len(shape) - 1 - axis_at))
    return factor_of


def length_profile(number_of, total, bound, lean):
    portions = [(1 << 20) // math.isqrt(rank ** lean) + 1 for rank in range(2, number_of + 1)]
    rest, holding = total - bound - (number_of - 1), [1] * (number_of - 1)
    while rest > 0:
        movable = [i for i in range(number_of - 1) if holding[i] < bound]
        whole, left = sum([portions[i] for i in movable]), rest
        for i in movable:
            more = min(bound - holding[i], max(1, left * portions[i] // whole), rest)
            holding[i] = holding[i] + more
            rest = rest - more
    return np.array([bound] + holding)


def ragged(stream_key, count, total, bound, skew):
    if count == 2:
        one = jax.random.randint(stream_key, (), max(1, total - bound), min(bound, total - 1) + 1)
        return jnp.stack([one, total - one])
    tallies = jnp.asarray(length_profile(count, total, bound, skew), jnp.int32)
    couples = (count - 1) // 2
    source_of, taker = tallies[1:1 + 2 * couples:2], tallies[2:2 + 2 * couples:2]
    slack = jnp.minimum(source_of - 1, bound - taker)
    shifted = jax.random.randint(jax.random.fold_in(stream_key, 1), (couples,), 0, 1 << 20) % (slack + 1)
    tallies = tallies.at[1:1 + 2 * couples:2].set(source_of - shifted).at[2:2 + 2 * couples:2].set(taker + shifted)
    return tallies[jax.random.permutation(jax.random.fold_in(stream_key, 2), count)]


def centred(key, extent, deviation, most, cuts=(), kind=jnp.bfloat16):
    gain = block_scale(key, extent, cuts, -0.22, 0.18) if cuts else 1.0
    drawn = jax.random.normal(key, extent, jnp.float32) * deviation * gain
    return jnp.minimum(jnp.maximum(drawn, -most), most).astype(kind)


def setup_inputs(seed: int = 0, part: int = 0) -> dict:
    seeds = jax.random.split(jax.random.key(seed), 12)
    part_keys = jax.random.split(jax.random.fold_in(seeds[11], part), 12)
    return {
        "pair": centred(part_keys[0], (TOKENS, TOKENS, C), 1.0, 6.0, ((0, 16),)),
        "window_rows": draw_window_rows(jax.random.fold_in(jax.random.fold_in(seeds[11], part), 71), part),
        "token_mask": draw_token_mask(jax.random.fold_in(jax.random.fold_in(seeds[11], part), 71), part),
        "chain_ids": jnp.searchsorted(jnp.cumsum(ragged(part_keys[3], CHAINS, TOKENS, TOKENS // 2, 1)), jnp.arange(TOKENS), side="right").astype(jnp.int32),
        "ln_gain": jnp.clip(1.0 + 0.18 * jax.random.normal(seeds[4], (C,), jnp.float32), 0.1, 1.9),
        "ln_shift": centred(seeds[5], (C,), 0.5, 3.0, (), jnp.float32),
        "w_project": centred(seeds[6], (C, 4 * HEADS * HEAD_DIM), C ** -0.5, 0.5),
        "gate_bias": centred(seeds[7], (HEADS * HEAD_DIM,), 1.0, 4.0, (), jnp.float32),
        "w_bias": draw_w_bias(jax.random.fold_in(seeds[11], 71), part),
        "chain_bias": centred(seeds[9], (HEADS,), 2.0, 8.0, (), jnp.float32),
        "w_out": centred(seeds[10], (HEADS * HEAD_DIM, C), (HEADS * HEAD_DIM) ** -0.5, 0.5),
    }


def layer_norm(field, ln_gain, ln_shift):
    field = field.astype(jnp.float32)
    mean_value = lax.optimization_barrier(jnp.mean(field, axis=-1, keepdims=True))
    variance = lax.optimization_barrier(jnp.mean((field - mean_value) ** 2, axis=-1, keepdims=True))
    return ((field - mean_value) * lax.rsqrt(variance + 1e-05) * ln_gain + ln_shift).astype(jnp.bfloat16)

def reference(pair, window_rows, token_mask, chain_ids, ln_gain, ln_shift, w_project, gate_bias, w_bias, chain_bias, w_out):
    inner_width = HEADS * HEAD_DIM
    normed = layer_norm(pair, ln_gain, ln_shift)
    bias = jnp.einsum('jkc,ch->hjk', normed.astype(jnp.float32), w_bias.astype(jnp.float32)).astype(jnp.bfloat16)
    same_chain = (chain_ids[:, None] == chain_ids[None, :]).astype(jnp.float32)
    full_bias = bias.astype(jnp.float32) + chain_bias[:, None, None] * same_chain[None]
    key_live = token_mask == 1
    row_keep = token_mask.astype(jnp.float32)

    def one_row(row_index):
        window = lax.dynamic_index_in_dim(normed, row_index, 0, keepdims=False)
        projected = jnp.dot(window, w_project, preferred_element_type=jnp.float32)
        queries = (projected[:, :inner_width] * HEAD_DIM ** (-0.5)).astype(jnp.bfloat16)
        key_rows = projected[:, inner_width:2 * inner_width].astype(jnp.bfloat16)
        value_rows = projected[:, 2 * inner_width:3 * inner_width].astype(jnp.bfloat16)
        gate_value = jax.nn.sigmoid(projected[:, 3 * inner_width:] + gate_bias)
        q_heads = queries.reshape(TOKENS, HEADS, HEAD_DIM).astype(jnp.float32)
        k_heads = key_rows.reshape(TOKENS, HEADS, HEAD_DIM).astype(jnp.float32)
        v_heads = value_rows.reshape(TOKENS, HEADS, HEAD_DIM).astype(jnp.float32)
        scores = jnp.einsum('jhd,khd->hjk', q_heads, k_heads) + full_bias
        scores = jnp.where(key_live[None, None, :], scores, -jnp.inf)
        row_max = lax.optimization_barrier(jnp.max(scores, axis=-1, keepdims=True))
        raised = jnp.where(key_live[None, None, :], jnp.exp(scores - row_max), 0.0)
        totals = lax.optimization_barrier(jnp.sum(raised, axis=-1))
        weights = raised.astype(jnp.bfloat16)
        attended = jnp.einsum('hjk,khd->jhd', weights.astype(jnp.float32), v_heads) / jnp.transpose(totals)[:, :, None]
        gated = (gate_value * attended.reshape(TOKENS, inner_width)).astype(jnp.bfloat16)
        result = jnp.dot(gated, w_out, preferred_element_type=jnp.float32) * row_keep[:, None]
        return result.astype(jnp.bfloat16)
    return lax.map(one_row, window_rows)
```

```python
import functools

import jax
import jax.numpy as jnp
from jax import lax
from jax.experimental import pallas as pl
from jax.experimental.pallas import tpu as pltpu
from jax.sharding import PartitionSpec as P

F32, BF16 = jnp.float32, jnp.bfloat16
VMEM = pl.BlockSpec(memory_space=pltpu.VMEM)
SMEM = pl.BlockSpec(memory_space=pltpu.SMEM)
ANY = pl.BlockSpec(memory_space=pl.ANY)
NT = (((1,), (1,)), ((), ()))
PARAMS = pltpu.CompilerParams(vmem_limit_bytes=48 * 1024 * 1024)


def normalised(rows, gain, shift):
    x = rows.astype(F32)
    mean = jnp.mean(x, axis=-1, keepdims=True)
    d = x - mean
    var = jnp.mean(d * d, axis=-1, keepdims=True)
    return (d * lax.rsqrt(var + 1e-05) * gain + shift).astype(BF16)


def live_ranks(mask_row):
    tokens = mask_row.shape[1]
    upper = lax.broadcasted_iota(jnp.int32, (tokens, tokens), 0) <= lax.broadcasted_iota(
        jnp.int32, (tokens, tokens), 1
    )
    ones = jnp.broadcast_to(mask_row.astype(F32), (8, tokens)).astype(BF16)
    running = jnp.dot(ones, upper.astype(F32).astype(BF16), preferred_element_type=F32)[0:1]
    return jnp.where(mask_row == 1, running - 1.0, -1.0)


def picking(mask_row, live):
    ranks = live_ranks(mask_row).astype(jnp.int32)
    wanted = lax.broadcasted_iota(jnp.int32, (live, mask_row.shape[1]), 0)
    return (wanted == ranks).astype(F32).astype(BF16)


def window_kernel(rows_ref, pair_ref, gain_ref, shift_ref, out_ref, held, sems):
    count = held.shape[0]
    rows_held = pair_ref.shape[0]
    copies = []
    for i in range(count):
        at = lax.rem(rows_ref[i], rows_held)
        copies.append(pltpu.make_async_copy(pair_ref.at[at], held.at[i], sems.at[i]))
        copies[-1].start()
    for i in range(count):
        copies[i].wait()
        out_ref[i] = normalised(held[i], gain_ref[...], shift_ref[...])


def bias_kernel(pair_ref, mask_ref, gain_ref, shift_ref, w_ref, out_ref, acc):
    step = pl.program_id(0)
    rows = pair_ref.shape[0]
    heads, held, tokens = acc.shape
    live = out_ref.shape[1]
    for i in range(rows):
        x = normalised(pair_ref[i], gain_ref[...], shift_ref[...])
        b = lax.dot_general(w_ref[...], x, NT, preferred_element_type=F32)
        for h in range(heads):
            acc[h, pl.ds(step * rows + i, 1), :] = b[h : h + 1]

    @pl.when(step == pl.num_programs(0) - 1)
    def _():
        full = acc[...].reshape(heads * held, tokens).astype(BF16)
        out_ref[...] = lax.dot_general(
            full, picking(mask_ref[...], live), NT, preferred_element_type=F32
        ).astype(BF16)


def key_value_kernel(own_ref, other_ref, mask_ref, w_ref, k_ref, v_ref, pick):
    count = own_ref.shape[0]
    live, inner = k_ref.shape[1:]
    pick[...] = picking(mask_ref[...], live)
    for i in range(count):
        both = jnp.concatenate([own_ref[i], other_ref[i]], axis=1)
        taken = jnp.dot(pick[...], both, preferred_element_type=F32).astype(BF16)
        c = own_ref.shape[2]
        for part in range(2):
            kv = jnp.dot(
                taken[:, part * c : (part + 1) * c],
                w_ref[:, inner : 3 * inner],
                preferred_element_type=F32,
            ).astype(BF16)
            k_ref[i + part * count] = kv[:, :inner]
            v_ref[i + part * count] = kv[:, inner:]


def attention_kernel(heads, blocks, place_ref, chain_bias_ref, *refs):
    bias_refs, refs = refs[:blocks], refs[blocks:]
    (own_ref, other_ref, k_ref, v_ref, mask_ref, chain_ref, w_ref, gate_bias_ref, w_out_ref), refs = (
        refs[:9],
        refs[9:],
    )
    out_refs, (q_s, gate_s, added_s, gated_s) = refs[:blocks], refs[blocks:]
    windows, live, inner = k_ref.shape
    half = windows // 2
    block = own_ref.shape[3]
    tokens = mask_ref.shape[1]
    size = inner // heads
    core = place_ref[0]
    chain_row = jnp.broadcast_to(chain_ref[...].astype(F32), (8, tokens)).astype(BF16)
    chain_live = lax.dot_general(
        chain_row, picking(mask_ref[...], live), NT, preferred_element_type=F32
    )[0:1]
    lane_head = lax.broadcasted_iota(jnp.int32, (block, inner), 1) // size
    w_q = w_ref[:, :inner]
    w_g = w_ref[:, 3 * inner :]
    for b in range(blocks):
        at = place_ref[1 + b]
        here = (
            lax.broadcasted_iota(jnp.int32, (block, tokens), 1)
            == (at * 2 + core) * block + lax.broadcasted_iota(jnp.int32, (block, tokens), 0)
        ).astype(F32)
        chain_here = jnp.sum(here * chain_ref[...].astype(F32), axis=1, keepdims=True)
        keep = jnp.sum(here * mask_ref[...].astype(F32), axis=1, keepdims=True)
        same = (chain_here == chain_live).astype(F32)
        for h in range(heads):
            rows = slice(h * block, (h + 1) * block)
            added_s[b, rows, :] = bias_refs[b][rows, :].astype(F32) + chain_bias_ref[h] * same
        for part, ref in enumerate((own_ref, other_ref)):
            x = ref[:, at, core].reshape(half * block, inner)
            span = pl.ds(part * half * block, half * block)
            q_s[b, span, :] = (
                jnp.dot(x, w_q, preferred_element_type=F32) * size ** (-0.5)
            ).astype(BF16)
            gate_s[b, span, :] = jax.nn.sigmoid(
                jnp.dot(x, w_g, preferred_element_type=F32) + gate_bias_ref[...]
            )

        def one_window(w, carry, b=b):
            span = pl.ds(pl.multiple_of(w * block, block), block)
            q = q_s[b, span, :].astype(F32)
            spread = jnp.concatenate(
                [jnp.where(lane_head == h, q, 0.0) for h in range(heads)], axis=0
            ).astype(BF16)
            scores = (
                lax.dot_general(spread, k_ref[w], NT, preferred_element_type=F32) + added_s[b]
            )
            top = jnp.max(scores, axis=1, keepdims=True)
            raised = jnp.exp(scores - top)
            totals = jnp.sum(raised, axis=1, keepdims=True)
            mixed = jnp.dot(raised.astype(BF16), v_ref[w], preferred_element_type=F32)
            mixed = mixed * (1.0 / totals)
            attended = mixed[0:block]
            for h in range(1, heads):
                attended = jnp.where(
                    lane_head == h, mixed[h * block : (h + 1) * block], attended
                )
            gated_s[b, span, :] = (gate_s[b, span, :] * attended).astype(BF16)
            return carry

        lax.fori_loop(0, windows, one_window, 0, unroll=4)
        result = jnp.dot(gated_s[b], w_out_ref[...], preferred_element_type=F32)
        result = result.reshape(windows, block, inner) * keep[None]
        result = result.astype(BF16)
        out_refs[b][pl.ds(core * half, half)] = result[:half]
        out_refs[b][pl.ds((1 - core) * half, half)] = result[half:]


def gather_kernel(place_ref, *refs):
    parts, out_ref, sems = refs[:-2], refs[-2], refs[-1]
    count = parts[0].shape[0]
    copies = []
    for i, part in enumerate(parts):
        at = place_ref[i] * count
        copies.append(pltpu.make_async_copy(part, out_ref.at[pl.ds(at, count)], sems.at[i]))
        copies[-1].start()
    for copy in copies:
        copy.wait()


def local(
    devices,
    pair,
    window_rows,
    token_mask,
    chain_ids,
    ln_gain,
    ln_shift,
    w_project,
    gate_bias,
    w_bias,
    chain_bias,
    w_out,
):
    rows_held, tokens, channels = pair.shape
    heads = w_bias.shape[1]
    inner = w_out.shape[0]
    count = window_rows.shape[0]
    live = tokens * 3 // 4
    owners = devices // 2
    me = lax.axis_index("row")
    core, chip = me % 2, me // 2
    mask_row = token_mask.reshape(1, tokens)
    chain_row = chain_ids.reshape(1, tokens)
    gain = ln_gain.reshape(1, channels)
    shift = ln_shift.reshape(1, channels)

    def swap(x, bits):
        return lax.ppermute(x, "row", [(i, i ^ bits) for i in range(devices)])

    own = pl.pallas_call(
        window_kernel,
        out_shape=jax.ShapeDtypeStruct((count, tokens, channels), BF16),
        in_specs=[SMEM, ANY, VMEM, VMEM],
        out_specs=VMEM,
        scratch_shapes=[
            pltpu.VMEM((count, tokens, channels), BF16),
            pltpu.SemaphoreType.DMA((count,)),
        ],
        compiler_params=PARAMS,
    )(window_rows, pair, gain, shift)
    other = swap(own, 1)

    step_rows = 4
    w_bias_t = jnp.pad(w_bias.T, ((0, 8 - heads), (0, 0)))
    bias = pl.pallas_call(
        bias_kernel,
        grid=(rows_held // step_rows,),
        out_shape=jax.ShapeDtypeStruct((heads * rows_held, live), BF16),
        in_specs=[
            pl.BlockSpec((step_rows, tokens, channels), lambda i: (i, 0, 0)),
            pl.BlockSpec((1, tokens), lambda i: (0, 0)),
            pl.BlockSpec((1, channels), lambda i: (0, 0)),
            pl.BlockSpec((1, channels), lambda i: (0, 0)),
            pl.BlockSpec((8, channels), lambda i: (0, 0)),
        ],
        out_specs=pl.BlockSpec((heads * rows_held, live), lambda i: (0, 0)),
        scratch_shapes=[pltpu.VMEM((heads, rows_held, tokens), F32)],
        compiler_params=PARAMS,
    )(pair, mask_row, gain, shift, w_bias_t)
    biases = [bias] + [swap(bias, 2 * m) for m in range(1, owners)]

    keys, values = pl.pallas_call(
        key_value_kernel,
        out_shape=[jax.ShapeDtypeStruct((2 * count, live, inner), BF16)] * 2,
        in_specs=[VMEM] * 4,
        out_specs=[VMEM] * 2,
        scratch_shapes=[pltpu.VMEM((live, tokens), BF16)],
        compiler_params=PARAMS,
    )(own, other, mask_row, w_project)

    split = (count, owners, 2, rows_held, channels)
    own, other = own.reshape(split), other.reshape(split)

    def attend(ms):
        blocks = len(ms)
        place = jnp.stack([core] + [chip ^ m for m in ms]).astype(jnp.int32)
        rows = 2 * count * rows_held
        return pl.pallas_call(
            functools.partial(attention_kernel, heads, blocks),
            out_shape=[jax.ShapeDtypeStruct((2 * count, rows_held, channels), BF16)] * blocks,
            in_specs=[SMEM, SMEM] + [VMEM] * (blocks + 9),
            out_specs=[VMEM] * blocks,
            scratch_shapes=[
                pltpu.VMEM((blocks, rows, inner), BF16),
                pltpu.VMEM((blocks, rows, inner), F32),
                pltpu.VMEM((blocks, heads * rows_held, live), F32),
                pltpu.VMEM((blocks, rows, inner), BF16),
            ],
            compiler_params=PARAMS,
        )(
            place,
            chain_bias,
            *[biases[m] for m in ms],
            own,
            other,
            keys,
            values,
            mask_row,
            chain_row,
            w_project,
            gate_bias.reshape(1, inner),
            w_out,
        )

    ms = list(range(owners))
    updates = attend(ms)
    received = [u if m == 0 else swap(u, 2 * m) for m, u in zip(ms, updates)]
    place = jnp.stack([chip ^ m for m in ms]).astype(jnp.int32)
    return pl.pallas_call(
        gather_kernel,
        out_shape=jax.ShapeDtypeStruct((owners * 2 * count, rows_held, channels), BF16),
        in_specs=[SMEM] + [ANY] * owners,
        out_specs=ANY,
        scratch_shapes=[pltpu.SemaphoreType.DMA((owners,))],
        compiler_params=PARAMS,
    )(place, *received)


def solution(mesh):
    placed = (
        P(("groups", "row"), None, None),
        P(("groups", "row")),
        P("groups"),
        P("groups"),
        P(),
        P(),
        P(),
        P(),
        P(),
        P(),
        P(),
    )
    return jax.shard_map(
        functools.partial(local, mesh.shape["row"]),
        mesh=mesh,
        in_specs=placed,
        out_specs=P("groups", "row", None),
        check_vma=False,
    )
```

```python
import functools

import jax
import jax.numpy as jnp
from jax import lax
from jax.experimental import pallas as pl
from jax.experimental.pallas import tpu as pltpu
from jax.sharding import PartitionSpec as P

F32, BF16 = jnp.float32, jnp.bfloat16
VMEM = pl.BlockSpec(memory_space=pltpu.VMEM)
SMEM = pl.BlockSpec(memory_space=pltpu.SMEM)
ANY = pl.BlockSpec(memory_space=pl.ANY)
NT = (((1,), (1,)), ((), ()))
PARAMS = pltpu.CompilerParams(vmem_limit_bytes=32 * 1024 * 1024)


def normalised(rows, gain, shift):
    channels = rows.shape[-1]
    x = rows.astype(F32)
    mean = jnp.dot(
        rows, jnp.full((channels, channels), 1.0 / channels, BF16), preferred_element_type=F32
    )
    d = x - mean
    var = jnp.mean(d * d, axis=-1, keepdims=True)
    return (d * lax.rsqrt(var + 1e-05) * gain + shift).astype(BF16)


def live_ranks(mask_row):
    tokens = mask_row.shape[1]
    upper = lax.broadcasted_iota(jnp.int32, (tokens, tokens), 0) <= lax.broadcasted_iota(
        jnp.int32, (tokens, tokens), 1
    )
    ones = jnp.broadcast_to(mask_row.astype(F32), (8, tokens)).astype(BF16)
    running = jnp.dot(ones, upper.astype(F32).astype(BF16), preferred_element_type=F32)[0:1]
    return jnp.where(mask_row == 1, running - 1.0, -1.0)


def picking(mask_row, live):
    ranks = live_ranks(mask_row).astype(jnp.int32)
    wanted = lax.broadcasted_iota(jnp.int32, (live, mask_row.shape[1]), 0)
    return (wanted == ranks).astype(F32).astype(BF16)


def window_kernel(rows_ref, after_ref, pair_ref, gain_ref, shift_ref, out_ref, held, sems):
    count = held.shape[0]
    rows_held = pair_ref.shape[0]
    copies = []
    for i in range(count):
        at = lax.rem(rows_ref[i], rows_held)
        copies.append(pltpu.make_async_copy(pair_ref.at[at], held.at[i], sems.at[i]))
        copies[-1].start()
    for i in range(count):
        copies[i].wait()
        out_ref[i] = normalised(held[i], gain_ref[...], shift_ref[...])


def bias_kernel(pair_ref, mask_ref, gain_ref, shift_ref, w_ref, out_ref, acc):
    step = pl.program_id(0)
    rows, tokens, channels = pair_ref.shape
    columns, live = out_ref.shape
    held = rows * pl.num_programs(0)
    heads = w_ref.shape[0]
    row_of = columns // heads
    column = lax.broadcasted_iota(jnp.int32, (heads, columns), 1)
    spread = (column // row_of == lax.broadcasted_iota(jnp.int32, (heads, columns), 0)).astype(F32)
    w = lax.dot_general(
        w_ref[...], spread.astype(BF16), (((0,), (0,)), ((), ())), preferred_element_type=F32
    )
    row_column = lax.broadcasted_iota(jnp.int32, (channels, columns), 1) % row_of
    xs, ws = [], []
    for i in range(rows):
        xs.append(normalised(pair_ref[i], gain_ref[...], shift_ref[...]))
        ws.append(jnp.where(row_column == step * rows + i, w, 0.0).astype(BF16))
    part = jnp.dot(
        jnp.concatenate(xs, axis=1), jnp.concatenate(ws, axis=0), preferred_element_type=F32
    )

    @pl.when(step == 0)
    def _():
        acc[...] = part

    @pl.when(step > 0)
    def _():
        acc[...] += part

    @pl.when(step == pl.num_programs(0) - 1)
    def _():
        full = acc[...].astype(BF16)
        taken = jnp.dot(picking(mask_ref[...], live), full, preferred_element_type=F32)
        out_ref[...] = taken.T.astype(BF16)


def key_value_kernel(own_ref, other_ref, mask_ref, w_ref, k_ref, v_ref, pick):
    count = own_ref.shape[0]
    live, inner = v_ref.shape[1:]
    pick[...] = picking(mask_ref[...], live)
    for i in range(count):
        both = jnp.concatenate([own_ref[i], other_ref[i]], axis=1)
        taken = jnp.dot(pick[...], both, preferred_element_type=F32).astype(BF16)
        c = own_ref.shape[2]
        for part in range(2):
            kv = jnp.dot(
                taken[:, part * c : (part + 1) * c],
                w_ref[:, inner : 3 * inner],
                preferred_element_type=F32,
            ).astype(BF16)
            k_ref[i + part * count] = kv[:, :inner].T
            v_ref[i + part * count] = kv[:, inner:]


def attention_kernel(heads, ms, me_ref, chain_bias_ref, *refs):
    blocks = len(ms)
    bias_refs, refs = refs[:blocks], refs[blocks:]
    own_ref, other_ref, k_ref, v_ref, mask_ref, chain_ref, w_ref, gate_bias_ref, w_out_ref = refs[:9]
    out_refs, (q_s, gate_s, added_s, gated_s) = refs[-4 - blocks : -4], refs[-4:]
    windows, inner, live = k_ref.shape
    half = windows // 2
    block = own_ref.shape[3]
    tokens = mask_ref.shape[1]
    size = inner // heads
    core, chip = lax.rem(me_ref[0], 2), lax.div(me_ref[0], 2)
    chain_row = jnp.broadcast_to(chain_ref[...].astype(F32), (8, tokens)).astype(BF16)
    chain_live = lax.dot_general(
        chain_row, picking(mask_ref[...], live), NT, preferred_element_type=F32
    )[0:1]
    lane_head = lax.broadcasted_iota(jnp.int32, (block, inner), 1) // size
    w_q = w_ref[:, :inner]
    w_g = w_ref[:, 3 * inner :]
    for b in range(blocks):
        at = lax.bitwise_xor(chip, ms[b])
        here = (
            lax.broadcasted_iota(jnp.int32, (block, tokens), 1)
            == (at * 2 + core) * block + lax.broadcasted_iota(jnp.int32, (block, tokens), 0)
        ).astype(F32)
        chain_here = jnp.sum(here * chain_ref[...].astype(F32), axis=1, keepdims=True)
        keep = jnp.sum(here * mask_ref[...].astype(F32), axis=1, keepdims=True)
        same = (chain_here == chain_live).astype(F32)
        for h in range(heads):
            rows = slice(h * block, (h + 1) * block)
            added_s[rows, :] = bias_refs[b][rows, :].astype(F32) + chain_bias_ref[h] * same
        for part, ref in enumerate((own_ref, other_ref)):
            x = ref[:, at, core].reshape(half * block, inner)
            span = pl.ds(part * half * block, half * block)
            q_s[span, :] = (
                jnp.dot(x, w_q, preferred_element_type=F32) * size ** (-0.5)
            ).astype(BF16)
            gate_s[span, :] = jax.nn.sigmoid(
                jnp.dot(x, w_g, preferred_element_type=F32) + gate_bias_ref[...]
            )

        def some_windows(g, carry):
            spans = [
                pl.ds(pl.multiple_of((g * half + i) * block, block), block) for i in range(half)
            ]
            scores = []
            for i in range(half):
                q = q_s[spans[i], :].astype(F32)
                spread = jnp.concatenate(
                    [jnp.where(lane_head == h, q, 0.0) for h in range(heads)], axis=0
                ).astype(BF16)
                scores.append(
                    jnp.dot(spread, k_ref[g * half + i], preferred_element_type=F32) + added_s[...]
                )
            tops = [jnp.max(s, axis=1, keepdims=True) for s in scores]
            raised = [jnp.exp(s - top) for s, top in zip(scores, tops)]
            shares = [1.0 / jnp.sum(r, axis=1, keepdims=True) for r in raised]
            mixed = [
                jnp.dot(r.astype(BF16), v_ref[g * half + i], preferred_element_type=F32)
                for i, r in enumerate(raised)
            ]
            for i in range(half):
                m = mixed[i] * shares[i]
                attended = m[0:block]
                for h in range(1, heads):
                    attended = jnp.where(lane_head == h, m[h * block : (h + 1) * block], attended)
                gated_s[spans[i], :] = (gate_s[spans[i], :] * attended).astype(BF16)
            return carry

        lax.fori_loop(0, 2, some_windows, 0)
        result = jnp.dot(gated_s[...], w_out_ref[...], preferred_element_type=F32)
        result = (result.reshape(windows, block, inner) * keep[None]).astype(BF16)
        out_refs[b][pl.ds(core * half, half)] = result[:half]
        out_refs[b][pl.ds((1 - core) * half, half)] = result[half:]


def gather_kernel(me_ref, *refs):
    parts, out_ref, sems = refs[:-2], refs[-2], refs[-1]
    count = parts[0].shape[0]
    chip = lax.div(me_ref[0], 2)
    copies = []
    for m, part in enumerate(parts):
        at = lax.bitwise_xor(chip, m) * count
        copies.append(pltpu.make_async_copy(part, out_ref.at[pl.ds(at, count)], sems.at[m]))
        copies[-1].start()
    for copy in copies:
        copy.wait()


def local(
    devices,
    pair,
    window_rows,
    token_mask,
    chain_ids,
    ln_gain,
    ln_shift,
    w_project,
    gate_bias,
    w_bias,
    chain_bias,
    w_out,
):
    rows_held, tokens, channels = pair.shape
    heads = w_bias.shape[1]
    inner = w_out.shape[0]
    count = window_rows.shape[0]
    live = tokens * 3 // 4
    owners = devices // 2
    me = lax.axis_index("row").astype(jnp.int32).reshape(1)
    mask_row = token_mask.reshape(1, tokens)
    chain_row = chain_ids.reshape(1, tokens)
    gain = ln_gain.reshape(1, channels)
    shift = ln_shift.reshape(1, channels)

    def swap(x, bits):
        return lax.ppermute(x, "row", [(i, i ^ bits) for i in range(devices)])

    step_rows = 8
    bias = pl.pallas_call(
        bias_kernel,
        grid=(rows_held // step_rows,),
        out_shape=jax.ShapeDtypeStruct((heads * rows_held, live), BF16),
        in_specs=[
            pl.BlockSpec((step_rows, tokens, channels), lambda i: (i, 0, 0)),
            pl.BlockSpec((1, tokens), lambda i: (0, 0)),
            pl.BlockSpec((1, channels), lambda i: (0, 0)),
            pl.BlockSpec((1, channels), lambda i: (0, 0)),
            pl.BlockSpec((heads, channels), lambda i: (0, 0)),
        ],
        out_specs=pl.BlockSpec((heads * rows_held, live), lambda i: (0, 0)),
        scratch_shapes=[pltpu.VMEM((tokens, heads * rows_held), F32)],
    )(pair, mask_row, gain, shift, w_bias.T)

    far = [m for m in range(owners // 2, owners) if m % 2 == 0]
    passed = [m + 1 for m in far]
    near = list(range(1, owners // 2))
    biases = {0: bias}
    for m in far[::-1] + near[::-1]:
        biases[m] = swap(bias, 2 * m)
    for m in passed:
        biases[m] = swap(biases[m - 1], 2)

    own = pl.pallas_call(
        window_kernel,
        out_shape=jax.ShapeDtypeStruct((count, tokens, channels), BF16),
        in_specs=[SMEM, ANY, ANY, VMEM, VMEM],
        out_specs=VMEM,
        scratch_shapes=[
            pltpu.VMEM((count, tokens, channels), BF16),
            pltpu.SemaphoreType.DMA((count,)),
        ],
        compiler_params=PARAMS,
    )(window_rows, bias, pair, gain, shift)
    other = swap(own, 1)

    keys, values = pl.pallas_call(
        key_value_kernel,
        out_shape=[
            jax.ShapeDtypeStruct((2 * count, inner, live), BF16),
            jax.ShapeDtypeStruct((2 * count, live, inner), BF16),
        ],
        in_specs=[VMEM] * 4,
        out_specs=[VMEM] * 2,
        scratch_shapes=[pltpu.VMEM((live, tokens), BF16)],
        compiler_params=PARAMS,
    )(own, other, mask_row, w_project)

    split = (count, owners, 2, rows_held, channels)
    own, other = own.reshape(split), other.reshape(split)
    updates = {}
    after = bias
    for ms in (far, [0] + near, passed):
        blocks = len(ms)
        rows = 2 * count * rows_held
        outs = pl.pallas_call(
            functools.partial(attention_kernel, heads, ms),
            out_shape=[jax.ShapeDtypeStruct((2 * count, rows_held, channels), BF16)] * blocks,
            in_specs=[SMEM, SMEM] + [VMEM] * (blocks + 9) + [ANY],
            out_specs=[VMEM] * blocks,
            scratch_shapes=[
                pltpu.VMEM((rows, inner), BF16),
                pltpu.VMEM((rows, inner), F32),
                pltpu.VMEM((heads * rows_held, live), F32),
                pltpu.VMEM((rows, inner), BF16),
            ],
            compiler_params=PARAMS,
        )(
            me,
            chain_bias,
            *[biases[m] for m in ms],
            own,
            other,
            keys,
            values,
            mask_row,
            chain_row,
            w_project,
            gate_bias.reshape(1, inner),
            w_out,
            after,
        )
        after = outs[0]
        for m, out in zip(ms, outs):
            updates[m] = out if m == 0 else swap(out, 2 * m)

    return pl.pallas_call(
        gather_kernel,
        out_shape=jax.ShapeDtypeStruct((owners * 2 * count, rows_held, channels), BF16),
        in_specs=[SMEM] + [ANY] * owners,
        out_specs=ANY,
        scratch_shapes=[pltpu.SemaphoreType.DMA((owners,))],
        compiler_params=PARAMS,
    )(me, *[updates[m] for m in range(owners)])


def solution(mesh):
    placed = (
        P(("groups", "row"), None, None),
        P(("groups", "row")),
        P("groups"),
        P("groups"),
        P(),
        P(),
        P(),
        P(),
        P(),
        P(),
        P(),
    )
    return jax.shard_map(
        functools.partial(local, mesh.shape["row"]),
        mesh=mesh,
        in_specs=placed,
        out_specs=P("groups", "row", None),
        check_vma=False,
    )
```

```python
import functools

import jax
import jax.numpy as jnp
from jax import lax
from jax.experimental import pallas as pl
from jax.experimental.pallas import tpu as pltpu
from jax.sharding import PartitionSpec as P

F32, BF16 = jnp.float32, jnp.bfloat16
VMEM = pl.BlockSpec(memory_space=pltpu.VMEM)
SMEM = pl.BlockSpec(memory_space=pltpu.SMEM)
ANY = pl.BlockSpec(memory_space=pl.ANY)
NT = (((1,), (1,)), ((), ()))
PARAMS = pltpu.CompilerParams(vmem_limit_bytes=32 * 1024 * 1024)


def measured(microseconds):
    return pl.CostEstimate(
        flops=0, transcendentals=0, bytes_accessed=int(microseconds * 3.69e6)
    )


def normalised(rows, gain, shift):
    channels = rows.shape[-1]
    square = (channels, channels)
    diagonal = lax.broadcasted_iota(jnp.int32, square, 0) == lax.broadcasted_iota(
        jnp.int32, square, 1
    )
    centring = jnp.where(diagonal, 1.0 - 1.0 / channels, -1.0 / channels).astype(BF16)
    d = jnp.dot(rows, centring, preferred_element_type=F32)
    var = jnp.mean(d * d, axis=-1, keepdims=True)
    return (d * lax.rsqrt(var + 1e-05) * gain + shift).astype(BF16)


def live_ranks(mask_row):
    tokens = mask_row.shape[1]
    upper = lax.broadcasted_iota(jnp.int32, (tokens, tokens), 0) <= lax.broadcasted_iota(
        jnp.int32, (tokens, tokens), 1
    )
    ones = jnp.broadcast_to(mask_row.astype(F32), (8, tokens)).astype(BF16)
    running = jnp.dot(ones, upper.astype(F32).astype(BF16), preferred_element_type=F32)[0:1]
    return jnp.where(mask_row == 1, running - 1.0, -1.0)


def picking(mask_row, live):
    ranks = live_ranks(mask_row).astype(jnp.int32)
    wanted = lax.broadcasted_iota(jnp.int32, (live, mask_row.shape[1]), 0)
    return (wanted == ranks).astype(F32).astype(BF16)


def bias_kernel(
    rows_ref, pair_ref, mask_ref, gain_ref, shift_ref, w_ref, out_ref, window_ref, acc, normed
):
    step = pl.program_id(0)
    rows, tokens, channels = pair_ref.shape
    columns, live = out_ref.shape
    held = rows * pl.num_programs(0)
    heads = w_ref.shape[0]
    row_of = columns // heads
    column = lax.broadcasted_iota(jnp.int32, (heads, columns), 1)
    spread = (column // row_of == lax.broadcasted_iota(jnp.int32, (heads, columns), 0)).astype(F32)
    w = lax.dot_general(
        w_ref[...], spread.astype(BF16), (((0,), (0,)), ((), ())), preferred_element_type=F32
    )
    row_column = lax.broadcasted_iota(jnp.int32, (channels, columns), 1) % row_of
    xs, ws = [], []
    for i in range(rows):
        xs.append(normalised(pair_ref[i], gain_ref[...], shift_ref[...]))
        ws.append(jnp.where(row_column == step * rows + i, w, 0.0).astype(BF16))
        normed[step * rows + i] = xs[i]
    part = jnp.dot(
        jnp.concatenate(xs, axis=1), jnp.concatenate(ws, axis=0), preferred_element_type=F32
    )

    @pl.when(step == 0)
    def _():
        acc[...] = part

    @pl.when(step > 0)
    def _():
        acc[...] += part

    @pl.when(step == pl.num_programs(0) - 1)
    def _():
        full = acc[...].astype(BF16)
        taken = jnp.dot(picking(mask_ref[...], live), full, preferred_element_type=F32)
        out_ref[...] = taken.T.astype(BF16)
        for i in range(window_ref.shape[0]):
            window_ref[i] = normed[lax.rem(rows_ref[i], held)]


def key_value_kernel(own_ref, other_ref, mask_ref, w_ref, k_ref, v_ref, pick):
    count = own_ref.shape[0]
    live, inner = v_ref.shape[1:]
    pick[...] = picking(mask_ref[...], live)
    for i in range(count):
        both = jnp.concatenate([own_ref[i], other_ref[i]], axis=1)
        taken = jnp.dot(pick[...], both, preferred_element_type=F32).astype(BF16)
        c = own_ref.shape[2]
        for part in range(2):
            kv = jnp.dot(
                taken[:, part * c : (part + 1) * c],
                w_ref[:, inner : 3 * inner],
                preferred_element_type=F32,
            ).astype(BF16)
            k_ref[i + part * count] = kv[:, :inner].T
            v_ref[i + part * count] = kv[:, inner:]


def attention_kernel(heads, ms, me_ref, chain_bias_ref, *refs):
    blocks = len(ms)
    bias_refs, refs = refs[:blocks], refs[blocks:]
    own_ref, other_ref, k_ref, v_ref, mask_ref, chain_ref, w_ref, gate_bias_ref, w_out_ref = refs[:9]
    out_refs, (q_s, gate_s, added_s, gated_s) = refs[-4 - blocks : -4], refs[-4:]
    windows, inner, live = k_ref.shape
    half = windows // 2
    block = own_ref.shape[3]
    tokens = mask_ref.shape[1]
    size = inner // heads
    core, chip = lax.rem(me_ref[0], 2), lax.div(me_ref[0], 2)
    chain_row = jnp.broadcast_to(chain_ref[...].astype(F32), (8, tokens)).astype(BF16)
    chain_live = lax.dot_general(
        chain_row, picking(mask_ref[...], live), NT, preferred_element_type=F32
    )[0:1]
    lane_head = lax.broadcasted_iota(jnp.int32, (block, inner), 1) // size
    w_q = w_ref[:, :inner]
    w_g = w_ref[:, 3 * inner :]
    for b in range(blocks):
        at = lax.bitwise_xor(chip, ms[b])
        here = (
            lax.broadcasted_iota(jnp.int32, (block, tokens), 1)
            == (at * 2 + core) * block + lax.broadcasted_iota(jnp.int32, (block, tokens), 0)
        ).astype(F32)
        chain_here = jnp.sum(here * chain_ref[...].astype(F32), axis=1, keepdims=True)
        keep = jnp.sum(here * mask_ref[...].astype(F32), axis=1, keepdims=True)
        same = (chain_here == chain_live).astype(F32)
        for h in range(heads):
            rows = slice(h * block, (h + 1) * block)
            added_s[rows, :] = bias_refs[b][rows, :].astype(F32) + chain_bias_ref[h] * same
        for part, ref in enumerate((own_ref, other_ref)):
            x = ref[:, at, core].reshape(half * block, inner)
            span = pl.ds(part * half * block, half * block)
            q_s[span, :] = (
                jnp.dot(x, w_q, preferred_element_type=F32) * size ** (-0.5)
            ).astype(BF16)
            gate_s[span, :] = jax.nn.sigmoid(
                jnp.dot(x, w_g, preferred_element_type=F32) + gate_bias_ref[...]
            )

        def some_windows(g, carry):
            spans = [
                pl.ds(pl.multiple_of((g * half + i) * block, block), block) for i in range(half)
            ]
            scores = []
            for i in range(half):
                q = q_s[spans[i], :].astype(F32)
                spread = jnp.concatenate(
                    [jnp.where(lane_head == h, q, 0.0) for h in range(heads)], axis=0
                ).astype(BF16)
                scores.append(
                    jnp.dot(spread, k_ref[g * half + i], preferred_element_type=F32) + added_s[...]
                )
            tops = [jnp.max(s, axis=1, keepdims=True) for s in scores]
            raised = [jnp.exp(s - top) for s, top in zip(scores, tops)]
            shares = [1.0 / jnp.sum(r, axis=1, keepdims=True) for r in raised]
            mixed = [
                jnp.dot(r.astype(BF16), v_ref[g * half + i], preferred_element_type=F32)
                for i, r in enumerate(raised)
            ]
            for i in range(half):
                m = mixed[i] * shares[i]
                attended = m[0:block]
                for h in range(1, heads):
                    attended = jnp.where(lane_head == h, m[h * block : (h + 1) * block], attended)
                gated_s[spans[i], :] = (gate_s[spans[i], :] * attended).astype(BF16)
            return carry

        lax.fori_loop(0, 2, some_windows, 0)
        result = jnp.dot(gated_s[...], w_out_ref[...], preferred_element_type=F32)
        result = (result.reshape(windows, block, inner) * keep[None]).astype(BF16)
        out_refs[b][pl.ds(core * half, half)] = result[:half]
        out_refs[b][pl.ds((1 - core) * half, half)] = result[half:]


def gather_kernel(me_ref, *refs):
    parts, out_ref, sems = refs[:-2], refs[-2], refs[-1]
    count = parts[0].shape[0]
    chip = lax.div(me_ref[0], 2)
    copies = []
    for m, part in enumerate(parts):
        at = lax.bitwise_xor(chip, m) * count
        copies.append(pltpu.make_async_copy(part, out_ref.at[pl.ds(at, count)], sems.at[m]))
        copies[-1].start()
    for copy in copies:
        copy.wait()


def local(
    devices,
    pair,
    window_rows,
    token_mask,
    chain_ids,
    ln_gain,
    ln_shift,
    w_project,
    gate_bias,
    w_bias,
    chain_bias,
    w_out,
):
    rows_held, tokens, channels = pair.shape
    heads = w_bias.shape[1]
    inner = w_out.shape[0]
    count = window_rows.shape[0]
    live = tokens * 3 // 4
    owners = devices // 2
    me = lax.axis_index("row").astype(jnp.int32).reshape(1)
    mask_row = token_mask.reshape(1, tokens)
    chain_row = chain_ids.reshape(1, tokens)
    gain = ln_gain.reshape(1, channels)
    shift = ln_shift.reshape(1, channels)

    def swap(x, bits):
        return lax.ppermute(x, "row", [(i, i ^ bits) for i in range(devices)])

    step_rows = 8
    bias, own = pl.pallas_call(
        bias_kernel,
        grid=(rows_held // step_rows,),
        out_shape=[
            jax.ShapeDtypeStruct((heads * rows_held, live), BF16),
            jax.ShapeDtypeStruct((count, tokens, channels), BF16),
        ],
        in_specs=[
            SMEM,
            pl.BlockSpec((step_rows, tokens, channels), lambda i: (i, 0, 0)),
            pl.BlockSpec((1, tokens), lambda i: (0, 0)),
            pl.BlockSpec((1, channels), lambda i: (0, 0)),
            pl.BlockSpec((1, channels), lambda i: (0, 0)),
            pl.BlockSpec((heads, channels), lambda i: (0, 0)),
        ],
        out_specs=[
            pl.BlockSpec((heads * rows_held, live), lambda i: (0, 0)),
            pl.BlockSpec((count, tokens, channels), lambda i: (0, 0, 0)),
        ],
        scratch_shapes=[
            pltpu.VMEM((tokens, heads * rows_held), F32),
            pltpu.VMEM((rows_held, tokens, channels), BF16),
        ],
        compiler_params=pltpu.CompilerParams(vmem_limit_bytes=60 * 1024 * 1024),
        cost_estimate=measured(6),
    )(window_rows, pair, mask_row, gain, shift, w_bias.T)

    far = [m for m in range(owners // 2, owners) if m % 2 == 0]
    passed = [m + 1 for m in far]
    near = list(range(1, owners // 2))
    biases = {0: bias}
    for m in far[::-1] + near[::-1]:
        biases[m] = swap(bias, 2 * m)
    for m in passed:
        biases[m] = swap(biases[m - 1], 2)

    other = swap(own, 1)

    keys, values = pl.pallas_call(
        key_value_kernel,
        out_shape=[
            jax.ShapeDtypeStruct((2 * count, inner, live), BF16),
            jax.ShapeDtypeStruct((2 * count, live, inner), BF16),
        ],
        in_specs=[VMEM] * 4,
        out_specs=[VMEM] * 2,
        scratch_shapes=[pltpu.VMEM((live, tokens), BF16)],
        compiler_params=PARAMS,
        cost_estimate=measured(2.2),
    )(own, other, mask_row, w_project)

    split = (count, owners, 2, rows_held, channels)
    own, other = own.reshape(split), other.reshape(split)
    updates = {}
    calls = ((far, []), ([0] + near[:1], far[:1]), (passed, near[:1]), (near[1:], far))
    sent = {}
    for ms, earlier in calls:
        after = [sent[m] if ms == near[1:] else updates[m] for m in earlier]
        blocks = len(ms)
        rows = 2 * count * rows_held
        outs = pl.pallas_call(
            functools.partial(attention_kernel, heads, ms),
            out_shape=[jax.ShapeDtypeStruct((2 * count, rows_held, channels), BF16)] * blocks,
            in_specs=[SMEM, SMEM] + [VMEM] * (blocks + 9) + [ANY] * len(after),
            out_specs=[VMEM] * blocks,
            scratch_shapes=[
                pltpu.VMEM((rows, inner), BF16),
                pltpu.VMEM((rows, inner), F32),
                pltpu.VMEM((heads * rows_held, live), F32),
                pltpu.VMEM((rows, inner), BF16),
            ],
            compiler_params=PARAMS,
            cost_estimate=measured(2.2 * blocks),
        )(
            me,
            chain_bias,
            *[biases[m] for m in ms],
            own,
            other,
            keys,
            values,
            mask_row,
            chain_row,
            w_project,
            gate_bias.reshape(1, inner),
            w_out,
            *after,
        )
        for m, out in zip(ms, outs):
            updates[m] = out
            sent[m] = out if m == 0 else swap(out, 2 * m)

    return pl.pallas_call(
        gather_kernel,
        out_shape=jax.ShapeDtypeStruct((owners * 2 * count, rows_held, channels), BF16),
        in_specs=[SMEM] + [ANY] * owners,
        out_specs=ANY,
        scratch_shapes=[pltpu.SemaphoreType.DMA((owners,))],
        compiler_params=PARAMS,
    )(me, *[sent[m] for m in range(owners)])


def solution(mesh):
    placed = (
        P(("groups", "row"), None, None),
        P(("groups", "row")),
        P("groups"),
        P("groups"),
        P(),
        P(),
        P(),
        P(),
        P(),
        P(),
        P(),
    )
    return jax.shard_map(
        functools.partial(local, mesh.shape["row"]),
        mesh=mesh,
        in_specs=placed,
        out_specs=P("groups", "row", None),
        check_vma=False,
    )
```

```python
import functools

import jax
import jax.numpy as jnp
from jax import lax
from jax.experimental import pallas as pl
from jax.experimental.pallas import tpu as pltpu
from jax.sharding import PartitionSpec as P

F32, BF16 = jnp.float32, jnp.bfloat16
VMEM = pl.BlockSpec(memory_space=pltpu.VMEM)
SMEM = pl.BlockSpec(memory_space=pltpu.SMEM)
ANY = pl.BlockSpec(memory_space=pl.ANY)
NT = (((1,), (1,)), ((), ()))
PARAMS = pltpu.CompilerParams(vmem_limit_bytes=32 * 1024 * 1024)


def measured(microseconds):
    return pl.CostEstimate(
        flops=0, transcendentals=0, bytes_accessed=int(microseconds * 3.69e6)
    )


def normalised(rows, gain, shift):
    channels = rows.shape[-1]
    square = (channels, channels)
    diagonal = lax.broadcasted_iota(jnp.int32, square, 0) == lax.broadcasted_iota(
        jnp.int32, square, 1
    )
    centring = jnp.where(diagonal, 1.0 - 1.0 / channels, -1.0 / channels).astype(BF16)
    d = jnp.dot(rows, centring, preferred_element_type=F32)
    var = jnp.mean(d * d, axis=-1, keepdims=True)
    return (d * lax.rsqrt(var + 1e-05) * gain + shift).astype(BF16)


def live_ranks(mask_row):
    tokens = mask_row.shape[1]
    upper = lax.broadcasted_iota(jnp.int32, (tokens, tokens), 0) <= lax.broadcasted_iota(
        jnp.int32, (tokens, tokens), 1
    )
    ones = jnp.broadcast_to(mask_row.astype(F32), (8, tokens)).astype(BF16)
    running = jnp.dot(ones, upper.astype(F32).astype(BF16), preferred_element_type=F32)[0:1]
    return jnp.where(mask_row == 1, running - 1.0, -1.0)


def picking(mask_row, live):
    ranks = live_ranks(mask_row).astype(jnp.int32)
    wanted = lax.broadcasted_iota(jnp.int32, (live, mask_row.shape[1]), 0)
    return (wanted == ranks).astype(F32).astype(BF16)


def bias_kernel(
    rows_ref,
    pair_ref,
    mask_ref,
    chain_ref,
    gain_ref,
    shift_ref,
    w_ref,
    out_ref,
    window_ref,
    pick_ref,
    chain_live_ref,
    acc,
    normed,
):
    step = pl.program_id(0)
    rows, tokens, channels = pair_ref.shape
    columns, live = out_ref.shape
    held = rows * pl.num_programs(0)
    heads = w_ref.shape[0]
    row_of = columns // heads
    column = lax.broadcasted_iota(jnp.int32, (heads, columns), 1)
    spread = (column // row_of == lax.broadcasted_iota(jnp.int32, (heads, columns), 0)).astype(F32)
    w = lax.dot_general(
        w_ref[...], spread.astype(BF16), (((0,), (0,)), ((), ())), preferred_element_type=F32
    )
    row_column = lax.broadcasted_iota(jnp.int32, (channels, columns), 1) % row_of
    xs, ws = [], []
    for i in range(rows):
        xs.append(normalised(pair_ref[i], gain_ref[...], shift_ref[...]))
        ws.append(jnp.where(row_column == step * rows + i, w, 0.0).astype(BF16))
        normed[step * rows + i] = xs[i]
    part = jnp.dot(
        jnp.concatenate(xs, axis=1), jnp.concatenate(ws, axis=0), preferred_element_type=F32
    )

    @pl.when(step == 0)
    def _():
        acc[...] = part
        pick = picking(mask_ref[...], live)
        pick_ref[...] = pick
        chain_row = jnp.broadcast_to(chain_ref[...].astype(F32), (8, tokens)).astype(BF16)
        chain_live_ref[...] = lax.dot_general(chain_row, pick, NT, preferred_element_type=F32)

    @pl.when(step > 0)
    def _():
        acc[...] += part

    @pl.when(step == pl.num_programs(0) - 1)
    def _():
        full = acc[...].astype(BF16)
        taken = jnp.dot(pick_ref[...], full, preferred_element_type=F32)
        out_ref[...] = taken.T.astype(BF16)
        for i in range(window_ref.shape[0]):
            window_ref[i] = normed[lax.rem(rows_ref[i], held)]


def key_value_kernel(own_ref, other_ref, pick_ref, w_ref, k_ref, v_ref):
    count = own_ref.shape[0]
    live, inner = v_ref.shape[1:]
    for i in range(count):
        both = jnp.concatenate([own_ref[i], other_ref[i]], axis=1)
        taken = jnp.dot(pick_ref[...], both, preferred_element_type=F32).astype(BF16)
        c = own_ref.shape[2]
        for part in range(2):
            kv = jnp.dot(
                taken[:, part * c : (part + 1) * c],
                w_ref[:, inner : 3 * inner],
                preferred_element_type=F32,
            ).astype(BF16)
            k_ref[i + part * count] = kv[:, :inner].T
            v_ref[i + part * count] = kv[:, inner:]


def attention_kernel(heads, ms, first, me_ref, chain_bias_ref, *refs):
    blocks = len(ms)
    bias_refs, refs = refs[:blocks], refs[blocks:]
    own_ref, other_ref, k_ref, v_ref, mask_ref, chain_ref, chain_live_ref = refs[:7]
    w_ref, gate_bias_ref, w_out_ref = refs[7:10]
    out_refs, (q_s, gate_s, added_s, gated_s) = refs[-4 - blocks : -4], refs[-4:]
    windows, inner, live = k_ref.shape
    half = windows // 2
    block = own_ref.shape[3]
    tokens = mask_ref.shape[1]
    size = inner // heads
    core, chip = lax.rem(me_ref[0], 2), lax.div(me_ref[0], 2)
    chain_live = chain_live_ref[0:1, :]
    lane_head = lax.broadcasted_iota(jnp.int32, (block, inner), 1) // size
    w_q = w_ref[:, :inner]
    w_g = w_ref[:, 3 * inner :]
    for b in range(blocks):
        at = lax.bitwise_xor(chip, ms[b])
        here = (
            lax.broadcasted_iota(jnp.int32, (block, tokens), 1)
            == (at * 2 + core) * block + lax.broadcasted_iota(jnp.int32, (block, tokens), 0)
        ).astype(F32)
        chain_here = jnp.sum(here * chain_ref[...].astype(F32), axis=1, keepdims=True)
        keep = jnp.sum(here * mask_ref[...].astype(F32), axis=1, keepdims=True)
        same = (chain_here == chain_live).astype(F32)
        for h in range(heads):
            rows = slice(h * block, (h + 1) * block)
            taken = pl.ds(first[b] + h * block, block)
            added_s[rows, :] = bias_refs[b][taken, :].astype(F32) + chain_bias_ref[h] * same
        for part, ref in enumerate((own_ref, other_ref)):
            x = ref[:, at, core].reshape(half * block, inner)
            span = pl.ds(part * half * block, half * block)
            q_s[span, :] = (
                jnp.dot(x, w_q, preferred_element_type=F32) * size ** (-0.5)
            ).astype(BF16)
            gate_s[span, :] = jax.nn.sigmoid(
                jnp.dot(x, w_g, preferred_element_type=F32) + gate_bias_ref[...]
            )

        def some_windows(g, carry):
            spans = [
                pl.ds(pl.multiple_of((g * half + i) * block, block), block) for i in range(half)
            ]
            scores = []
            for i in range(half):
                q = q_s[spans[i], :].astype(F32)
                spread = jnp.concatenate(
                    [jnp.where(lane_head == h, q, 0.0) for h in range(heads)], axis=0
                ).astype(BF16)
                scores.append(
                    jnp.dot(spread, k_ref[g * half + i], preferred_element_type=F32) + added_s[...]
                )
            tops = [jnp.max(s, axis=1, keepdims=True) for s in scores]
            raised = [jnp.exp(s - top) for s, top in zip(scores, tops)]
            shares = [1.0 / jnp.sum(r, axis=1, keepdims=True) for r in raised]
            mixed = [
                jnp.dot(r.astype(BF16), v_ref[g * half + i], preferred_element_type=F32)
                for i, r in enumerate(raised)
            ]
            for i in range(half):
                m = mixed[i] * shares[i]
                attended = m[0:block]
                for h in range(1, heads):
                    attended = jnp.where(lane_head == h, m[h * block : (h + 1) * block], attended)
                gated_s[spans[i], :] = (gate_s[spans[i], :] * attended).astype(BF16)
            return carry

        lax.fori_loop(0, 2, some_windows, 0)
        result = jnp.dot(gated_s[...], w_out_ref[...], preferred_element_type=F32)
        result = (result.reshape(windows, block, inner) * keep[None]).astype(BF16)
        out_refs[b][pl.ds(core * half, half)] = result[:half]
        out_refs[b][pl.ds((1 - core) * half, half)] = result[half:]


def gather_kernel(order, me_ref, *refs):
    parts, out_ref, sems = refs[: len(order)], refs[-2], refs[-1]
    count = parts[0].shape[0]
    chip = lax.div(me_ref[0], 2)
    copies = []
    for i, part in enumerate(parts):
        at = lax.bitwise_xor(chip, order[i]) * count
        copies.append(pltpu.make_async_copy(part, out_ref.at[pl.ds(at, count)], sems.at[i]))
        copies[-1].start()
    for copy in copies:
        copy.wait()


def local(
    devices,
    pair,
    window_rows,
    token_mask,
    chain_ids,
    ln_gain,
    ln_shift,
    w_project,
    gate_bias,
    w_bias,
    chain_bias,
    w_out,
):
    rows_held, tokens, channels = pair.shape
    heads = w_bias.shape[1]
    inner = w_out.shape[0]
    count = window_rows.shape[0]
    live = tokens * 3 // 4
    owners = devices // 2
    me = lax.axis_index("row").astype(jnp.int32).reshape(1)
    mask_row = token_mask.reshape(1, tokens)
    chain_row = chain_ids.reshape(1, tokens)
    gain = ln_gain.reshape(1, channels)
    shift = ln_shift.reshape(1, channels)

    def swap(x, bits):
        return lax.ppermute(x, "row", [(i, i ^ bits) for i in range(devices)])

    step_rows = 16
    bias, own, pick, chain_live = pl.pallas_call(
        bias_kernel,
        grid=(rows_held // step_rows,),
        out_shape=[
            jax.ShapeDtypeStruct((heads * rows_held, live), BF16),
            jax.ShapeDtypeStruct((count, tokens, channels), BF16),
            jax.ShapeDtypeStruct((live, tokens), BF16),
            jax.ShapeDtypeStruct((8, live), F32),
        ],
        in_specs=[
            SMEM,
            pl.BlockSpec((step_rows, tokens, channels), lambda i: (i, 0, 0)),
            pl.BlockSpec((1, tokens), lambda i: (0, 0)),
            pl.BlockSpec((1, tokens), lambda i: (0, 0)),
            pl.BlockSpec((1, channels), lambda i: (0, 0)),
            pl.BlockSpec((1, channels), lambda i: (0, 0)),
            pl.BlockSpec((heads, channels), lambda i: (0, 0)),
        ],
        out_specs=[
            pl.BlockSpec((heads * rows_held, live), lambda i: (0, 0)),
            pl.BlockSpec((count, tokens, channels), lambda i: (0, 0, 0)),
            pl.BlockSpec((live, tokens), lambda i: (0, 0)),
            pl.BlockSpec((8, live), lambda i: (0, 0)),
        ],
        scratch_shapes=[
            pltpu.VMEM((tokens, heads * rows_held), F32),
            pltpu.VMEM((rows_held, tokens, channels), BF16),
        ],
        compiler_params=pltpu.CompilerParams(vmem_limit_bytes=60 * 1024 * 1024),
        cost_estimate=measured(6),
    )(window_rows, pair, mask_row, chain_row, gain, shift, w_bias.T)

    far = [m for m in range(owners // 2, owners) if m % 2 == 0]
    passed = [m + 1 for m in far]
    near = list(range(1, owners // 2))
    biases = {0: bias}
    for m in far[::-1] + near[::-1]:
        biases[m] = swap(bias, 2 * m)
    other = swap(own, 1)

    keys, values = pl.pallas_call(
        key_value_kernel,
        out_shape=[
            jax.ShapeDtypeStruct((2 * count, inner, live), BF16),
            jax.ShapeDtypeStruct((2 * count, live, inner), BF16),
        ],
        in_specs=[VMEM] * 4,
        out_specs=[VMEM] * 2,
        compiler_params=PARAMS,
        cost_estimate=measured(2),
    )(own, other, pick, w_project)

    split = (count, owners, 2, rows_held, channels)
    own, other = own.reshape(split), other.reshape(split)
    updates = {}
    sent = {}
    for ms in ([0] + near[:1], far, passed, near[1:]):
        if ms == far:
            after = [updates[0]] + [biases[m] for m in near[1:]]
        elif ms == passed:
            after = [updates[far[0]]]
        elif ms == near[1:]:
            after = [updates[passed[0]]] + [sent[m] for m in far]
        else:
            after = []
        blocks = len(ms)
        first = [i * heads * rows_held if ms == passed else 0 for i in range(blocks)]
        rows = 2 * count * rows_held
        outs = pl.pallas_call(
            functools.partial(attention_kernel, heads, ms, first),
            out_shape=[jax.ShapeDtypeStruct((2 * count, rows_held, channels), BF16)] * blocks,
            in_specs=[SMEM, SMEM] + [VMEM] * (blocks + 10) + [ANY] * len(after),
            out_specs=[VMEM] * blocks,
            scratch_shapes=[
                pltpu.VMEM((rows, inner), BF16),
                pltpu.VMEM((rows, inner), F32),
                pltpu.VMEM((heads * rows_held, live), F32),
                pltpu.VMEM((rows, inner), BF16),
            ],
            compiler_params=PARAMS,
            cost_estimate=measured(2.2 * blocks),
        )(
            me,
            chain_bias,
            *[biases[m] for m in ms],
            own,
            other,
            keys,
            values,
            mask_row,
            chain_row,
            chain_live,
            w_project,
            gate_bias.reshape(1, inner),
            w_out,
            *after,
        )
        for m, out in zip(ms, outs):
            updates[m] = out
        if 0 in ms:
            *straight, _ = lax.optimization_barrier((*[biases[m] for m in far], outs[0]))
            straight = swap(jnp.concatenate(straight), 2)
            for i, m in enumerate(passed):
                biases[m] = straight
        for m, out in zip(ms, outs):
            sent[m] = out if m == 0 else swap(out, 2 * m)

    whole = []
    for order in ([0] + near[:1] + far + passed, near[1:]):
        placed = len(order)
        whole = [
            pl.pallas_call(
                functools.partial(gather_kernel, order),
                out_shape=jax.ShapeDtypeStruct((owners * 2 * count, rows_held, channels), BF16),
                in_specs=[SMEM] + [ANY] * (placed + len(whole)),
                out_specs=ANY,
                scratch_shapes=[pltpu.SemaphoreType.DMA((placed,))],
                input_output_aliases={placed + 1: 0} if whole else {},
                compiler_params=PARAMS,
                cost_estimate=measured(1),
            )(me, *[sent[m] for m in order], *whole)
        ]
    return whole[0]


def solution(mesh):
    placed = (
        P(("groups", "row"), None, None),
        P(("groups", "row")),
        P("groups"),
        P("groups"),
        P(),
        P(),
        P(),
        P(),
        P(),
        P(),
        P(),
    )
    return jax.shard_map(
        functools.partial(local, mesh.shape["row"]),
        mesh=mesh,
        in_specs=placed,
        out_specs=P("groups", "row", None),
        check_vma=False,
    )
```

```python
import functools

import jax
import jax.numpy as jnp
from jax import lax
from jax.experimental import pallas as pl
from jax.experimental.pallas import tpu as pltpu
from jax.sharding import PartitionSpec as P

F32, BF16 = jnp.float32, jnp.bfloat16
VMEM = pl.BlockSpec(memory_space=pltpu.VMEM)
SMEM = pl.BlockSpec(memory_space=pltpu.SMEM)
ANY = pl.BlockSpec(memory_space=pl.ANY)
NT = (((1,), (1,)), ((), ()))
PARAMS = pltpu.CompilerParams(vmem_limit_bytes=32 * 1024 * 1024)


def measured(microseconds):
    return pl.CostEstimate(
        flops=0, transcendentals=0, bytes_accessed=int(microseconds * 3.69e6)
    )


def normalised(rows, gain, shift):
    channels = rows.shape[-1]
    square = (channels, channels)
    diagonal = lax.broadcasted_iota(jnp.int32, square, 0) == lax.broadcasted_iota(
        jnp.int32, square, 1
    )
    centring = jnp.where(diagonal, 1.0 - 1.0 / channels, -1.0 / channels).astype(BF16)
    d = jnp.dot(rows, centring, preferred_element_type=F32)
    var = jnp.mean(d * d, axis=-1, keepdims=True)
    return (d * lax.rsqrt(var + 1e-05) * gain + shift).astype(BF16)


def live_ranks(mask_row):
    tokens = mask_row.shape[1]
    upper = lax.broadcasted_iota(jnp.int32, (tokens, tokens), 0) <= lax.broadcasted_iota(
        jnp.int32, (tokens, tokens), 1
    )
    ones = jnp.broadcast_to(mask_row.astype(F32), (8, tokens)).astype(BF16)
    running = jnp.dot(ones, upper.astype(F32).astype(BF16), preferred_element_type=F32)[0:1]
    return jnp.where(mask_row == 1, running - 1.0, -1.0)


def picking(mask_row, live):
    ranks = live_ranks(mask_row).astype(jnp.int32)
    wanted = lax.broadcasted_iota(jnp.int32, (live, mask_row.shape[1]), 0)
    return (wanted == ranks).astype(F32).astype(BF16)


def bias_kernel(
    rows_ref,
    pair_ref,
    mask_ref,
    chain_ref,
    gain_ref,
    shift_ref,
    w_ref,
    out_ref,
    window_ref,
    pick_ref,
    chain_live_ref,
    acc,
    normed,
):
    step = pl.program_id(0)
    rows, tokens, channels = pair_ref.shape
    columns, live = out_ref.shape
    held = rows * pl.num_programs(0)
    heads = w_ref.shape[0]
    row_of = columns // heads
    column = lax.broadcasted_iota(jnp.int32, (heads, columns), 1)
    spread = (column // row_of == lax.broadcasted_iota(jnp.int32, (heads, columns), 0)).astype(F32)
    w = lax.dot_general(
        w_ref[...], spread.astype(BF16), (((0,), (0,)), ((), ())), preferred_element_type=F32
    )
    row_column = lax.broadcasted_iota(jnp.int32, (channels, columns), 1) % row_of
    xs, ws = [], []
    for i in range(rows):
        xs.append(normalised(pair_ref[i], gain_ref[...], shift_ref[...]))
        ws.append(jnp.where(row_column == step * rows + i, w, 0.0).astype(BF16))
        normed[step * rows + i] = xs[i]
    part = jnp.dot(
        jnp.concatenate(xs, axis=1), jnp.concatenate(ws, axis=0), preferred_element_type=F32
    )

    @pl.when(step == 0)
    def _():
        acc[...] = part
        pick = picking(mask_ref[...], live)
        pick_ref[...] = pick
        chain_row = jnp.broadcast_to(chain_ref[...].astype(F32), (8, tokens)).astype(BF16)
        chain_live_ref[...] = lax.dot_general(chain_row, pick, NT, preferred_element_type=F32)

    @pl.when(step > 0)
    def _():
        acc[...] += part

    @pl.when(step == pl.num_programs(0) - 1)
    def _():
        full = acc[...].astype(BF16)
        taken = jnp.dot(pick_ref[...], full, preferred_element_type=F32)
        out_ref[...] = taken.T.astype(BF16)
        for i in range(window_ref.shape[0]):
            window_ref[i] = normed[lax.rem(rows_ref[i], held)]


def key_value_kernel(own_ref, other_ref, pick_ref, w_ref, k_ref, v_ref):
    count = own_ref.shape[0]
    live, inner = v_ref.shape[1:]
    for i in range(count):
        both = jnp.concatenate([own_ref[i], other_ref[i]], axis=1)
        taken = jnp.dot(pick_ref[...], both, preferred_element_type=F32).astype(BF16)
        c = own_ref.shape[2]
        for part in range(2):
            kv = jnp.dot(
                taken[:, part * c : (part + 1) * c],
                w_ref[:, inner : 3 * inner],
                preferred_element_type=F32,
            ).astype(BF16)
            k_ref[i + part * count] = kv[:, :inner].T
            v_ref[i + part * count] = kv[:, inner:]


def attention_kernel(heads, ms, first, me_ref, chain_bias_ref, *refs):
    blocks = len(ms)
    bias_refs, refs = refs[:blocks], refs[blocks:]
    own_ref, other_ref, k_ref, v_ref, mask_ref, chain_ref, chain_live_ref = refs[:7]
    w_ref, gate_bias_ref, w_out_ref = refs[7:10]
    out_refs, (q_s, gate_s, added_s, gated_s) = refs[-4 - blocks : -4], refs[-4:]
    windows, inner, live = k_ref.shape
    half = windows // 2
    block = own_ref.shape[3]
    tokens = mask_ref.shape[1]
    size = inner // heads
    core, chip = lax.rem(me_ref[0], 2), lax.div(me_ref[0], 2)
    chain_live = chain_live_ref[0:1, :]
    lane_head = lax.broadcasted_iota(jnp.int32, (block, inner), 1) // size
    w_q = w_ref[:, :inner]
    w_g = w_ref[:, 3 * inner :]
    for b in range(blocks):
        at = lax.bitwise_xor(chip, ms[b])
        here = (
            lax.broadcasted_iota(jnp.int32, (block, tokens), 1)
            == (at * 2 + core) * block + lax.broadcasted_iota(jnp.int32, (block, tokens), 0)
        ).astype(F32)
        chain_here = jnp.sum(here * chain_ref[...].astype(F32), axis=1, keepdims=True)
        keep = jnp.sum(here * mask_ref[...].astype(F32), axis=1, keepdims=True)
        same = (chain_here == chain_live).astype(F32)
        for h in range(heads):
            rows = slice(h * block, (h + 1) * block)
            taken = pl.ds(first[b] + h * block, block)
            added_s[rows, :] = bias_refs[b][taken, :].astype(F32) + chain_bias_ref[h] * same
        for part, ref in enumerate((own_ref, other_ref)):
            x = ref[:, at, core].reshape(half * block, inner)
            span = pl.ds(part * half * block, half * block)
            q_s[span, :] = (
                jnp.dot(x, w_q, preferred_element_type=F32) * size ** (-0.5)
            ).astype(BF16)
            gate_s[span, :] = jax.nn.sigmoid(
                jnp.dot(x, w_g, preferred_element_type=F32) + gate_bias_ref[...]
            )

        def some_windows(g, carry):
            spans = [
                pl.ds(pl.multiple_of((g * half + i) * block, block), block) for i in range(half)
            ]
            scores = []
            for i in range(half):
                q = q_s[spans[i], :].astype(F32)
                spread = jnp.concatenate(
                    [jnp.where(lane_head == h, q, 0.0) for h in range(heads)], axis=0
                ).astype(BF16)
                scores.append(
                    jnp.dot(spread, k_ref[g * half + i], preferred_element_type=F32) + added_s[...]
                )
            tops = [jnp.max(s, axis=1, keepdims=True) for s in scores]
            raised = [jnp.exp(s - top) for s, top in zip(scores, tops)]
            shares = [1.0 / jnp.sum(r, axis=1, keepdims=True) for r in raised]
            mixed = [
                jnp.dot(r.astype(BF16), v_ref[g * half + i], preferred_element_type=F32)
                for i, r in enumerate(raised)
            ]
            for i in range(half):
                m = mixed[i] * shares[i]
                attended = m[0:block]
                for h in range(1, heads):
                    attended = jnp.where(lane_head == h, m[h * block : (h + 1) * block], attended)
                gated_s[spans[i], :] = (gate_s[spans[i], :] * attended).astype(BF16)
            return carry

        lax.fori_loop(0, 2, some_windows, 0)
        result = jnp.dot(gated_s[...], w_out_ref[...], preferred_element_type=F32)
        result = (result.reshape(windows, block, inner) * keep[None]).astype(BF16)
        out_refs[b][pl.ds(core * half, half)] = result[:half]
        out_refs[b][pl.ds((1 - core) * half, half)] = result[half:]


def gather_kernel(order, me_ref, *refs):
    parts, out_ref, sems = refs[: len(order)], refs[-2], refs[-1]
    count = parts[0].shape[0]
    chip = lax.div(me_ref[0], 2)
    copies = []
    for i, part in enumerate(parts):
        at = lax.bitwise_xor(chip, order[i]) * count
        copies.append(pltpu.make_async_copy(part, out_ref.at[pl.ds(at, count)], sems.at[i]))
        copies[-1].start()
    for copy in copies:
        copy.wait()


def local(
    devices,
    pair,
    window_rows,
    token_mask,
    chain_ids,
    ln_gain,
    ln_shift,
    w_project,
    gate_bias,
    w_bias,
    chain_bias,
    w_out,
):
    rows_held, tokens, channels = pair.shape
    heads = w_bias.shape[1]
    inner = w_out.shape[0]
    count = window_rows.shape[0]
    live = tokens * 3 // 4
    owners = devices // 2
    me = lax.axis_index("row").astype(jnp.int32).reshape(1)
    mask_row = token_mask.reshape(1, tokens)
    chain_row = chain_ids.reshape(1, tokens)
    gain = ln_gain.reshape(1, channels)
    shift = ln_shift.reshape(1, channels)

    def swap(x, bits):
        return lax.ppermute(x, "row", [(i, i ^ bits) for i in range(devices)])

    step_rows = 16
    bias, own, pick, chain_live = pl.pallas_call(
        bias_kernel,
        grid=(rows_held // step_rows,),
        out_shape=[
            jax.ShapeDtypeStruct((heads * rows_held, live), BF16),
            jax.ShapeDtypeStruct((count, tokens, channels), BF16),
            jax.ShapeDtypeStruct((live, tokens), BF16),
            jax.ShapeDtypeStruct((8, live), F32),
        ],
        in_specs=[
            SMEM,
            pl.BlockSpec((step_rows, tokens, channels), lambda i: (i, 0, 0)),
            pl.BlockSpec((1, tokens), lambda i: (0, 0)),
            pl.BlockSpec((1, tokens), lambda i: (0, 0)),
            pl.BlockSpec((1, channels), lambda i: (0, 0)),
            pl.BlockSpec((1, channels), lambda i: (0, 0)),
            pl.BlockSpec((heads, channels), lambda i: (0, 0)),
        ],
        out_specs=[
            pl.BlockSpec((heads * rows_held, live), lambda i: (0, 0)),
            pl.BlockSpec((count, tokens, channels), lambda i: (0, 0, 0)),
            pl.BlockSpec((live, tokens), lambda i: (0, 0)),
            pl.BlockSpec((8, live), lambda i: (0, 0)),
        ],
        scratch_shapes=[
            pltpu.VMEM((tokens, heads * rows_held), F32),
            pltpu.VMEM((rows_held, tokens, channels), BF16),
        ],
        compiler_params=PARAMS,
        cost_estimate=measured(6),
    )(window_rows, pltpu.with_memory_space_constraint(pair, pltpu.HBM), mask_row, chain_row, gain, shift, w_bias.T)

    far = [m for m in range(owners // 2, owners) if m % 2 == 0]
    passed = [m + 1 for m in far]
    near = list(range(1, owners // 2))
    biases = {0: bias}
    for m in far[::-1] + near[::-1]:
        biases[m] = swap(bias, 2 * m)
    other = swap(own, 1)

    keys, values = pl.pallas_call(
        key_value_kernel,
        out_shape=[
            jax.ShapeDtypeStruct((2 * count, inner, live), BF16),
            jax.ShapeDtypeStruct((2 * count, live, inner), BF16),
        ],
        in_specs=[VMEM] * 4,
        out_specs=[VMEM] * 2,
        compiler_params=PARAMS,
        cost_estimate=measured(2),
    )(own, other, pick, w_project)

    split = (count, owners, 2, rows_held, channels)
    own, other = own.reshape(split), other.reshape(split)
    updates = {}
    *straight, _ = lax.optimization_barrier((*[biases[m] for m in far], keys))
    straight = swap(jnp.concatenate(straight), 2)
    for m in passed:
        biases[m] = straight
    sent = {}
    for ms in (far, [0] + near[:1], passed, near[1:]):
        if ms == far:
            after = []
        elif ms == near[1:]:
            after = [updates[passed[0]]] + [sent[m] for m in far]
        else:
            after = [updates[far[0] if 0 in ms else 0]]
            if ms == passed:
                after += [biases[m] for m in near[1:]]
        blocks = len(ms)
        first = [i * heads * rows_held if ms == passed else 0 for i in range(blocks)]
        rows = 2 * count * rows_held
        outs = pl.pallas_call(
            functools.partial(attention_kernel, heads, ms, first),
            out_shape=[jax.ShapeDtypeStruct((2 * count, rows_held, channels), BF16)] * blocks,
            in_specs=[SMEM, SMEM] + [VMEM] * (blocks + 10) + [ANY] * len(after),
            out_specs=[VMEM] * blocks,
            scratch_shapes=[
                pltpu.VMEM((rows, inner), BF16),
                pltpu.VMEM((rows, inner), F32),
                pltpu.VMEM((heads * rows_held, live), F32),
                pltpu.VMEM((rows, inner), BF16),
            ],
            compiler_params=PARAMS,
            cost_estimate=measured(2.2 * blocks),
        )(
            me,
            chain_bias,
            *[biases[m] for m in ms],
            own,
            other,
            keys,
            values,
            mask_row,
            chain_row,
            chain_live,
            w_project,
            gate_bias.reshape(1, inner),
            w_out,
            *after,
        )
        for m, out in zip(ms, outs):
            updates[m] = out
        for m, out in zip(ms, outs):
            sent[m] = out if m == 0 else swap(out, 2 * m)

    whole = []
    for order in ([0] + near[:1] + far + passed, near[1:]):
        placed = len(order)
        whole = [
            pl.pallas_call(
                functools.partial(gather_kernel, order),
                out_shape=jax.ShapeDtypeStruct((owners * 2 * count, rows_held, channels), BF16),
                in_specs=[SMEM] + [ANY] * (placed + len(whole)),
                out_specs=ANY,
                scratch_shapes=[pltpu.SemaphoreType.DMA((placed,))],
                input_output_aliases={placed + 1: 0} if whole else {},
                compiler_params=PARAMS,
                cost_estimate=measured(1),
            )(me, *[sent[m] for m in order], *whole)
        ]
    return whole[0]


def solution(mesh):
    placed = (
        P(("groups", "row"), None, None),
        P(("groups", "row")),
        P("groups"),
        P("groups"),
        P(),
        P(),
        P(),
        P(),
        P(),
        P(),
        P(),
    )
    return jax.shard_map(
        functools.partial(local, mesh.shape["row"]),
        mesh=mesh,
        in_specs=placed,
        out_specs=P("groups", "row", None),
        check_vma=False,
    )
```

```python
import functools

import jax
import jax.numpy as jnp
from jax import lax
from jax.experimental import pallas as pl
from jax.experimental.pallas import tpu as pltpu
from jax.sharding import PartitionSpec as P

F32, BF16 = jnp.float32, jnp.bfloat16
VMEM = pl.BlockSpec(memory_space=pltpu.VMEM)
SMEM = pl.BlockSpec(memory_space=pltpu.SMEM)
ANY = pl.BlockSpec(memory_space=pl.ANY)
NT = (((1,), (1,)), ((), ()))
PARAMS = pltpu.CompilerParams(vmem_limit_bytes=32 * 1024 * 1024)


def measured(microseconds):
    return pl.CostEstimate(
        flops=0, transcendentals=0, bytes_accessed=int(microseconds * 3.69e6)
    )


def normalised(rows, gain, shift):
    channels = rows.shape[-1]
    square = (channels, channels)
    diagonal = lax.broadcasted_iota(jnp.int32, square, 0) == lax.broadcasted_iota(
        jnp.int32, square, 1
    )
    centring = jnp.where(diagonal, 1.0 - 1.0 / channels, -1.0 / channels).astype(BF16)
    d = jnp.dot(rows, centring, preferred_element_type=F32)
    var = jnp.mean(d * d, axis=-1, keepdims=True)
    return (d * lax.rsqrt(var + 1e-05) * gain + shift).astype(BF16)


def live_ranks(mask_row):
    tokens = mask_row.shape[1]
    upper = lax.broadcasted_iota(jnp.int32, (tokens, tokens), 0) <= lax.broadcasted_iota(
        jnp.int32, (tokens, tokens), 1
    )
    ones = jnp.broadcast_to(mask_row.astype(F32), (8, tokens)).astype(BF16)
    running = jnp.dot(ones, upper.astype(F32).astype(BF16), preferred_element_type=F32)[0:1]
    return jnp.where(mask_row == 1, running - 1.0, -1.0)


def picking(mask_row, live):
    ranks = live_ranks(mask_row).astype(jnp.int32)
    wanted = lax.broadcasted_iota(jnp.int32, (live, mask_row.shape[1]), 0)
    return (wanted == ranks).astype(F32).astype(BF16)


def bias_kernel(
    rows_ref,
    pair_ref,
    mask_ref,
    chain_ref,
    gain_ref,
    shift_ref,
    w_ref,
    out_ref,
    window_ref,
    pick_ref,
    chain_live_ref,
    acc,
    normed,
    rows_s,
    rows_sem,
):
    step = pl.program_id(0)
    rows, tokens, channels = pair_ref.shape
    columns, live = out_ref.shape
    held = rows * pl.num_programs(0)
    heads = w_ref.shape[0]
    row_of = columns // heads
    column = lax.broadcasted_iota(jnp.int32, (heads, columns), 1)
    spread = (column // row_of == lax.broadcasted_iota(jnp.int32, (heads, columns), 0)).astype(F32)
    w = lax.dot_general(
        w_ref[...], spread.astype(BF16), (((0,), (0,)), ((), ())), preferred_element_type=F32
    )
    row_column = lax.broadcasted_iota(jnp.int32, (channels, columns), 1) % row_of
    xs, ws = [], []
    for i in range(rows):
        xs.append(normalised(pair_ref[i], gain_ref[...], shift_ref[...]))
        ws.append(jnp.where(row_column == step * rows + i, w, 0.0).astype(BF16))
        normed[step * rows + i] = xs[i]
    part = jnp.dot(
        jnp.concatenate(xs, axis=1), jnp.concatenate(ws, axis=0), preferred_element_type=F32
    )

    @pl.when(step == 0)
    def _():
        pltpu.make_async_copy(rows_ref, rows_s, rows_sem).start()
        acc[...] = part
        pick = picking(mask_ref[...], live)
        pick_ref[...] = pick
        chain_row = jnp.broadcast_to(chain_ref[...].astype(F32), (8, tokens)).astype(BF16)
        chain_live_ref[...] = lax.dot_general(chain_row, pick, NT, preferred_element_type=F32)

    @pl.when(step > 0)
    def _():
        acc[...] += part

    @pl.when(step == pl.num_programs(0) - 1)
    def _():
        full = acc[...].astype(BF16)
        taken = jnp.dot(pick_ref[...], full, preferred_element_type=F32)
        out_ref[...] = taken.T.astype(BF16)
        pltpu.make_async_copy(rows_ref, rows_s, rows_sem).wait()
        for i in range(window_ref.shape[0]):
            window_ref[i] = normed[lax.rem(rows_s[i], held)]


def key_value_kernel(own_ref, other_ref, pick_ref, w_ref, after_ref, k_ref, v_ref, done_ref):
    done_ref[...] = jnp.zeros_like(done_ref)
    count = own_ref.shape[0]
    live, inner = v_ref.shape[1:]
    for i in range(count):
        both = jnp.concatenate([own_ref[i], other_ref[i]], axis=1)
        taken = jnp.dot(pick_ref[...], both, preferred_element_type=F32).astype(BF16)
        c = own_ref.shape[2]
        for part in range(2):
            kv = jnp.dot(
                taken[:, part * c : (part + 1) * c],
                w_ref[:, inner : 3 * inner],
                preferred_element_type=F32,
            ).astype(BF16)
            k_ref[i + part * count] = kv[:, :inner].T
            v_ref[i + part * count] = kv[:, inner:]


def attention_kernel(heads, ms, first, me_ref, chain_bias_ref, *refs):
    blocks = len(ms)
    bias_refs, refs = refs[:blocks], refs[blocks:]
    own_ref, other_ref, k_ref, v_ref, mask_ref, chain_ref, chain_live_ref = refs[:7]
    w_ref, gate_bias_ref, w_out_ref = refs[7:10]
    out_refs, (q_s, gate_s, added_s, gated_s) = refs[-4 - blocks : -4], refs[-4:]
    windows, inner, live = k_ref.shape
    half = windows // 2
    block = own_ref.shape[3]
    tokens = mask_ref.shape[1]
    size = inner // heads
    core, chip = lax.rem(me_ref[0], 2), lax.div(me_ref[0], 2)
    chain_live = chain_live_ref[0:1, :]
    lane_head = lax.broadcasted_iota(jnp.int32, (block, inner), 1) // size
    w_q = w_ref[:, :inner]
    w_g = w_ref[:, 3 * inner :]
    for b in range(blocks):
        at = lax.bitwise_xor(chip, ms[b])
        here = (
            lax.broadcasted_iota(jnp.int32, (block, tokens), 1)
            == (at * 2 + core) * block + lax.broadcasted_iota(jnp.int32, (block, tokens), 0)
        ).astype(F32)
        chain_here = jnp.sum(here * chain_ref[...].astype(F32), axis=1, keepdims=True)
        keep = jnp.sum(here * mask_ref[...].astype(F32), axis=1, keepdims=True)
        same = (chain_here == chain_live).astype(F32)
        for h in range(heads):
            rows = slice(h * block, (h + 1) * block)
            taken = pl.ds(first[b] + h * block, block)
            added_s[rows, :] = bias_refs[b][taken, :].astype(F32) + chain_bias_ref[h] * same
        for part, ref in enumerate((own_ref, other_ref)):
            x = ref[:, at, core].reshape(half * block, inner)
            span = pl.ds(part * half * block, half * block)
            q_s[span, :] = (
                jnp.dot(x, w_q, preferred_element_type=F32) * size ** (-0.5)
            ).astype(BF16)
            gate_s[span, :] = jax.nn.sigmoid(
                jnp.dot(x, w_g, preferred_element_type=F32) + gate_bias_ref[...]
            )

        def some_windows(g, carry):
            spans = [
                pl.ds(pl.multiple_of((g * half + i) * block, block), block) for i in range(half)
            ]
            scores = []
            for i in range(half):
                q = q_s[spans[i], :].astype(F32)
                spread = jnp.concatenate(
                    [jnp.where(lane_head == h, q, 0.0) for h in range(heads)], axis=0
                ).astype(BF16)
                scores.append(
                    jnp.dot(spread, k_ref[g * half + i], preferred_element_type=F32) + added_s[...]
                )
            tops = [jnp.max(s, axis=1, keepdims=True) for s in scores]
            raised = [jnp.exp(s - top) for s, top in zip(scores, tops)]
            shares = [1.0 / jnp.sum(r, axis=1, keepdims=True) for r in raised]
            mixed = [
                jnp.dot(r.astype(BF16), v_ref[g * half + i], preferred_element_type=F32)
                for i, r in enumerate(raised)
            ]
            for i in range(half):
                m = mixed[i] * shares[i]
                attended = m[0:block]
                for h in range(1, heads):
                    attended = jnp.where(lane_head == h, m[h * block : (h + 1) * block], attended)
                gated_s[spans[i], :] = (gate_s[spans[i], :] * attended).astype(BF16)
            return carry

        lax.fori_loop(0, 2, some_windows, 0)
        result = jnp.dot(gated_s[...], w_out_ref[...], preferred_element_type=F32)
        result = (result.reshape(windows, block, inner) * keep[None]).astype(BF16)
        out_refs[b][pl.ds(core * half, half)] = result[:half]
        out_refs[b][pl.ds((1 - core) * half, half)] = result[half:]


def gather_kernel(order, me_ref, *refs):
    parts, out_ref, sems = refs[: len(order)], refs[-2], refs[-1]
    count = parts[0].shape[0]
    chip = lax.div(me_ref[0], 2)
    copies = []
    for i, part in enumerate(parts):
        at = lax.bitwise_xor(chip, order[i]) * count
        copies.append(pltpu.make_async_copy(part, out_ref.at[pl.ds(at, count)], sems.at[i]))
        copies[-1].start()
    for copy in copies:
        copy.wait()


def local(
    devices,
    pair,
    window_rows,
    token_mask,
    chain_ids,
    ln_gain,
    ln_shift,
    w_project,
    gate_bias,
    w_bias,
    chain_bias,
    w_out,
):
    rows_held, tokens, channels = pair.shape
    heads = w_bias.shape[1]
    inner = w_out.shape[0]
    count = window_rows.shape[0]
    live = tokens * 3 // 4
    owners = devices // 2
    me = lax.axis_index("row").astype(jnp.int32).reshape(1)
    mask_row = token_mask.reshape(1, tokens)
    chain_row = chain_ids.reshape(1, tokens)
    gain = ln_gain.reshape(1, channels)
    shift = ln_shift.reshape(1, channels)

    def swap(x, bits):
        return lax.ppermute(x, "row", [(i, i ^ bits) for i in range(devices)])

    step_rows = 16
    bias, own, pick, chain_live = pl.pallas_call(
        bias_kernel,
        grid=(rows_held // step_rows,),
        out_shape=[
            jax.ShapeDtypeStruct((heads * rows_held, live), BF16),
            jax.ShapeDtypeStruct((count, tokens, channels), BF16),
            jax.ShapeDtypeStruct((live, tokens), BF16),
            jax.ShapeDtypeStruct((8, live), F32),
        ],
        in_specs=[
            ANY,
            pl.BlockSpec((step_rows, tokens, channels), lambda i: (i, 0, 0)),
            pl.BlockSpec((1, tokens), lambda i: (0, 0)),
            pl.BlockSpec((1, tokens), lambda i: (0, 0)),
            pl.BlockSpec((1, channels), lambda i: (0, 0)),
            pl.BlockSpec((1, channels), lambda i: (0, 0)),
            pl.BlockSpec((heads, channels), lambda i: (0, 0)),
        ],
        out_specs=[
            pl.BlockSpec((heads * rows_held, live), lambda i: (0, 0)),
            pl.BlockSpec((count, tokens, channels), lambda i: (0, 0, 0)),
            pl.BlockSpec((live, tokens), lambda i: (0, 0)),
            pl.BlockSpec((8, live), lambda i: (0, 0)),
        ],
        scratch_shapes=[
            pltpu.VMEM((tokens, heads * rows_held), F32),
            pltpu.VMEM((rows_held, tokens, channels), BF16),
            pltpu.SMEM((count,), jnp.int32),
            pltpu.SemaphoreType.DMA(()),
        ],
        compiler_params=PARAMS,
        cost_estimate=measured(6),
    )(
        *[
            pltpu.with_memory_space_constraint(x, pltpu.HBM)
            for x in (window_rows, pair, mask_row, chain_row, gain, shift, w_bias.T)
        ]
    )

    far = [m for m in range(owners // 2, owners) if m % 2 == 0]
    passed = [m + 1 for m in far]
    near = list(range(1, owners // 2))
    biases = {0: bias}
    for m in far[::-1] + near[::-1]:
        biases[m] = swap(bias, 2 * m)
    other = swap(own, 1)

    keys, values, done = pl.pallas_call(
        key_value_kernel,
        out_shape=[
            jax.ShapeDtypeStruct((2 * count, inner, live), BF16),
            jax.ShapeDtypeStruct((2 * count, live, inner), BF16),
            jax.ShapeDtypeStruct((8, channels), F32),
        ],
        in_specs=[VMEM] * 4 + [ANY],
        out_specs=[VMEM] * 3,
        compiler_params=PARAMS,
        cost_estimate=measured(2),
    )(own, other, pick, w_project, biases[near[0]])

    split = (count, owners, 2, rows_held, channels)
    own, other = own.reshape(split), other.reshape(split)
    updates = {}
    straight = jnp.concatenate([biases[m] for m in far]) + done[:1, :1].astype(BF16)
    straight = swap(straight, 2)
    for m in passed:
        biases[m] = straight
    sent = {}
    for ms in (far, [0] + near[:1], passed, near[1:]):
        if ms == far:
            after = [biases[near[1]]]
        elif ms == near[1:]:
            after = [updates[passed[0]]] + [sent[m] for m in far]
        else:
            after = [updates[far[0] if 0 in ms else 0]]
        blocks = len(ms)
        first = [i * heads * rows_held if ms == passed else 0 for i in range(blocks)]
        rows = 2 * count * rows_held
        outs = pl.pallas_call(
            functools.partial(attention_kernel, heads, ms, first),
            out_shape=[jax.ShapeDtypeStruct((2 * count, rows_held, channels), BF16)] * blocks,
            in_specs=[SMEM, SMEM] + [VMEM] * (blocks + 10) + [ANY] * len(after),
            out_specs=[VMEM] * blocks,
            scratch_shapes=[
                pltpu.VMEM((rows, inner), BF16),
                pltpu.VMEM((rows, inner), F32),
                pltpu.VMEM((heads * rows_held, live), F32),
                pltpu.VMEM((rows, inner), BF16),
            ],
            compiler_params=PARAMS,
            cost_estimate=measured(2.2 * blocks),
        )(
            me,
            chain_bias,
            *[biases[m] for m in ms],
            own,
            other,
            keys,
            values,
            mask_row,
            chain_row,
            chain_live,
            w_project,
            gate_bias.reshape(1, inner),
            w_out,
            *after,
        )
        for m, out in zip(ms, outs):
            updates[m] = out
        for m, out in zip(ms, outs):
            sent[m] = out if m == 0 else swap(out, 2 * m)

    whole = []
    for order in ([0] + near[:1] + far + passed, near[1:]):
        placed = len(order)
        whole = [
            pl.pallas_call(
                functools.partial(gather_kernel, order),
                out_shape=jax.ShapeDtypeStruct((owners * 2 * count, rows_held, channels), BF16),
                in_specs=[SMEM] + [ANY] * (placed + len(whole)),
                out_specs=ANY,
                scratch_shapes=[pltpu.SemaphoreType.DMA((placed,))],
                input_output_aliases={placed + 1: 0} if whole else {},
                compiler_params=PARAMS,
                cost_estimate=measured(1),
            )(me, *[sent[m] for m in order], *whole)
        ]
    return whole[0]


def solution(mesh):
    placed = (
        P(("groups", "row"), None, None),
        P(("groups", "row")),
        P("groups"),
        P("groups"),
        P(),
        P(),
        P(),
        P(),
        P(),
        P(),
        P(),
    )
    return jax.shard_map(
        functools.partial(local, mesh.shape["row"]),
        mesh=mesh,
        in_specs=placed,
        out_specs=P("groups", "row", None),
        check_vma=False,
    )
```

```python
import functools

import jax
import jax.numpy as jnp
from jax import lax
from jax.experimental import pallas as pl
from jax.experimental.pallas import tpu as pltpu
from jax.sharding import PartitionSpec as P

F32, BF16 = jnp.float32, jnp.bfloat16
VMEM = pl.BlockSpec(memory_space=pltpu.VMEM)
SMEM = pl.BlockSpec(memory_space=pltpu.SMEM)
ANY = pl.BlockSpec(memory_space=pl.ANY)
NT = (((1,), (1,)), ((), ()))
PARAMS = pltpu.CompilerParams(vmem_limit_bytes=32 * 1024 * 1024)


def measured(microseconds):
    return pl.CostEstimate(
        flops=0, transcendentals=0, bytes_accessed=int(microseconds * 3.69e6)
    )


def normalised(rows, gain, shift):
    channels = rows.shape[-1]
    square = (channels, channels)
    diagonal = lax.broadcasted_iota(jnp.int32, square, 0) == lax.broadcasted_iota(
        jnp.int32, square, 1
    )
    centring = jnp.where(diagonal, 1.0 - 1.0 / channels, -1.0 / channels).astype(BF16)
    d = jnp.dot(rows, centring, preferred_element_type=F32)
    var = jnp.mean(d * d, axis=-1, keepdims=True)
    return (d * lax.rsqrt(var + 1e-05) * gain + shift).astype(BF16)


def live_ranks(mask_row):
    tokens = mask_row.shape[1]
    upper = lax.broadcasted_iota(jnp.int32, (tokens, tokens), 0) <= lax.broadcasted_iota(
        jnp.int32, (tokens, tokens), 1
    )
    ones = jnp.broadcast_to(mask_row.astype(F32), (8, tokens)).astype(BF16)
    running = jnp.dot(ones, upper.astype(F32).astype(BF16), preferred_element_type=F32)[0:1]
    return jnp.where(mask_row == 1, running - 1.0, -1.0)


def picking(mask_row, live):
    ranks = live_ranks(mask_row).astype(jnp.int32)
    wanted = lax.broadcasted_iota(jnp.int32, (live, mask_row.shape[1]), 0)
    return (wanted == ranks).astype(F32).astype(BF16)


def bias_kernel(
    rows_ref,
    pair_ref,
    mask_ref,
    chain_ref,
    gain_ref,
    shift_ref,
    w_ref,
    out_ref,
    window_ref,
    pick_ref,
    chain_live_ref,
    acc,
    normed,
    rows_s,
    rows_sem,
):
    step = pl.program_id(0)
    rows, tokens, channels = pair_ref.shape
    columns, live = out_ref.shape
    held = rows * pl.num_programs(0)
    heads = w_ref.shape[0]
    row_of = columns // heads
    column = lax.broadcasted_iota(jnp.int32, (heads, columns), 1)
    spread = (column // row_of == lax.broadcasted_iota(jnp.int32, (heads, columns), 0)).astype(F32)
    w = lax.dot_general(
        w_ref[...], spread.astype(BF16), (((0,), (0,)), ((), ())), preferred_element_type=F32
    )
    row_column = lax.broadcasted_iota(jnp.int32, (channels, columns), 1) % row_of
    xs, ws = [], []
    for i in range(rows):
        xs.append(normalised(pair_ref[i], gain_ref[...], shift_ref[...]))
        ws.append(jnp.where(row_column == step * rows + i, w, 0.0).astype(BF16))
        normed[step * rows + i] = xs[i]
    part = jnp.dot(
        jnp.concatenate(xs, axis=1), jnp.concatenate(ws, axis=0), preferred_element_type=F32
    )

    @pl.when(step == 0)
    def _():
        pltpu.make_async_copy(rows_ref, rows_s, rows_sem).start()
        acc[...] = part
        pick = picking(mask_ref[...], live)
        pick_ref[...] = pick
        chain_row = jnp.broadcast_to(chain_ref[...].astype(F32), (8, tokens)).astype(BF16)
        chain_live_ref[...] = lax.dot_general(chain_row, pick, NT, preferred_element_type=F32)

    @pl.when(step > 0)
    def _():
        acc[...] += part

    @pl.when(step == pl.num_programs(0) - 1)
    def _():
        full = acc[...].astype(BF16)
        taken = jnp.dot(pick_ref[...], full, preferred_element_type=F32)
        out_ref[...] = taken.T.astype(BF16)
        pltpu.make_async_copy(rows_ref, rows_s, rows_sem).wait()
        for i in range(window_ref.shape[0]):
            window_ref[i] = normed[lax.rem(rows_s[i], held)]


def key_value_kernel(own_ref, other_ref, pick_ref, w_ref, k_ref, v_ref):
    count = own_ref.shape[0]
    live, inner = v_ref.shape[1:]
    for i in range(count):
        both = jnp.concatenate([own_ref[i], other_ref[i]], axis=1)
        taken = jnp.dot(pick_ref[...], both, preferred_element_type=F32).astype(BF16)
        c = own_ref.shape[2]
        for part in range(2):
            kv = jnp.dot(
                taken[:, part * c : (part + 1) * c],
                w_ref[:, inner : 3 * inner],
                preferred_element_type=F32,
            ).astype(BF16)
            k_ref[i + part * count] = kv[:, :inner].T
            v_ref[i + part * count] = kv[:, inner:]


def attention_kernel(heads, ms, first, me_ref, chain_bias_ref, *refs):
    blocks = len(ms)
    bias_refs, refs = refs[:blocks], refs[blocks:]
    own_ref, other_ref, k_ref, v_ref, mask_ref, chain_ref, chain_live_ref = refs[:7]
    w_ref, gate_bias_ref, w_out_ref = refs[7:10]
    out_refs, (q_s, gate_s, added_s, gated_s) = refs[-4 - blocks : -4], refs[-4:]
    windows, inner, live = k_ref.shape
    half = windows // 2
    block = own_ref.shape[3]
    tokens = mask_ref.shape[1]
    size = inner // heads
    core, chip = lax.rem(me_ref[0], 2), lax.div(me_ref[0], 2)
    chain_live = chain_live_ref[0:1, :]
    lane_head = lax.broadcasted_iota(jnp.int32, (block, inner), 1) // size
    w_q = w_ref[:, :inner]
    w_g = w_ref[:, 3 * inner :]
    for b in range(blocks):
        at = lax.bitwise_xor(chip, ms[b])
        here = (
            lax.broadcasted_iota(jnp.int32, (block, tokens), 1)
            == (at * 2 + core) * block + lax.broadcasted_iota(jnp.int32, (block, tokens), 0)
        ).astype(F32)
        chain_here = jnp.sum(here * chain_ref[...].astype(F32), axis=1, keepdims=True)
        keep = jnp.sum(here * mask_ref[...].astype(F32), axis=1, keepdims=True)
        same = (chain_here == chain_live).astype(F32)
        for h in range(heads):
            rows = slice(h * block, (h + 1) * block)
            taken = pl.ds(first[b] + h * block, block)
            added_s[rows, :] = bias_refs[b][taken, :].astype(F32) + chain_bias_ref[h] * same
        for part, ref in enumerate((own_ref, other_ref)):
            x = ref[:, at, core].reshape(half * block, inner)
            span = pl.ds(part * half * block, half * block)
            q_s[span, :] = (
                jnp.dot(x, w_q, preferred_element_type=F32) * size ** (-0.5)
            ).astype(BF16)
            gate_s[span, :] = jax.nn.sigmoid(
                jnp.dot(x, w_g, preferred_element_type=F32) + gate_bias_ref[...]
            )

        def some_windows(g, carry):
            spans = [
                pl.ds(pl.multiple_of((g * half + i) * block, block), block) for i in range(half)
            ]
            scores = []
            for i in range(half):
                q = q_s[spans[i], :].astype(F32)
                spread = jnp.concatenate(
                    [jnp.where(lane_head == h, q, 0.0) for h in range(heads)], axis=0
                ).astype(BF16)
                scores.append(
                    jnp.dot(spread, k_ref[g * half + i], preferred_element_type=F32) + added_s[...]
                )
            tops = [jnp.max(s, axis=1, keepdims=True) for s in scores]
            raised = [jnp.exp(s - top) for s, top in zip(scores, tops)]
            shares = [1.0 / jnp.sum(r, axis=1, keepdims=True) for r in raised]
            mixed = [
                jnp.dot(r.astype(BF16), v_ref[g * half + i], preferred_element_type=F32)
                for i, r in enumerate(raised)
            ]
            for i in range(half):
                m = mixed[i] * shares[i]
                attended = m[0:block]
                for h in range(1, heads):
                    attended = jnp.where(lane_head == h, m[h * block : (h + 1) * block], attended)
                gated_s[spans[i], :] = (gate_s[spans[i], :] * attended).astype(BF16)
            return carry

        lax.fori_loop(0, 2, some_windows, 0)
        result = jnp.dot(gated_s[...], w_out_ref[...], preferred_element_type=F32)
        result = (result.reshape(windows, block, inner) * keep[None]).astype(BF16)
        out_refs[b][pl.ds(core * half, half)] = result[:half]
        out_refs[b][pl.ds((1 - core) * half, half)] = result[half:]


def join_kernel(*refs):
    parts, out_ref = refs[:-2], refs[-1]
    rows = parts[0].shape[0]
    for i, part in enumerate(parts):
        out_ref[i * rows : (i + 1) * rows, :] = part[...]


def gather_kernel(order, me_ref, *refs):
    parts, out_ref, sems = refs[: len(order)], refs[-2], refs[-1]
    count = parts[0].shape[0]
    chip = lax.div(me_ref[0], 2)
    copies = []
    for i, part in enumerate(parts):
        at = lax.bitwise_xor(chip, order[i]) * count
        copies.append(pltpu.make_async_copy(part, out_ref.at[pl.ds(at, count)], sems.at[i]))
        copies[-1].start()
    for copy in copies:
        copy.wait()


def local(
    devices,
    pair,
    window_rows,
    token_mask,
    chain_ids,
    ln_gain,
    ln_shift,
    w_project,
    gate_bias,
    w_bias,
    chain_bias,
    w_out,
):
    rows_held, tokens, channels = pair.shape
    heads = w_bias.shape[1]
    inner = w_out.shape[0]
    count = window_rows.shape[0]
    live = tokens * 3 // 4
    owners = devices // 2
    me = lax.axis_index("row").astype(jnp.int32).reshape(1)
    mask_row = token_mask.reshape(1, tokens)
    chain_row = chain_ids.reshape(1, tokens)
    gain = ln_gain.reshape(1, channels)
    shift = ln_shift.reshape(1, channels)

    def swap(x, bits):
        return lax.ppermute(x, "row", [(i, i ^ bits) for i in range(devices)])

    step_rows = 16
    bias, own, pick, chain_live = pl.pallas_call(
        bias_kernel,
        grid=(rows_held // step_rows,),
        out_shape=[
            jax.ShapeDtypeStruct((heads * rows_held, live), BF16),
            jax.ShapeDtypeStruct((count, tokens, channels), BF16),
            jax.ShapeDtypeStruct((live, tokens), BF16),
            jax.ShapeDtypeStruct((8, live), F32),
        ],
        in_specs=[
            ANY,
            pl.BlockSpec((step_rows, tokens, channels), lambda i: (i, 0, 0)),
            pl.BlockSpec((1, tokens), lambda i: (0, 0)),
            pl.BlockSpec((1, tokens), lambda i: (0, 0)),
            pl.BlockSpec((1, channels), lambda i: (0, 0)),
            pl.BlockSpec((1, channels), lambda i: (0, 0)),
            pl.BlockSpec((heads, channels), lambda i: (0, 0)),
        ],
        out_specs=[
            pl.BlockSpec((heads * rows_held, live), lambda i: (0, 0)),
            pl.BlockSpec((count, tokens, channels), lambda i: (0, 0, 0)),
            pl.BlockSpec((live, tokens), lambda i: (0, 0)),
            pl.BlockSpec((8, live), lambda i: (0, 0)),
        ],
        scratch_shapes=[
            pltpu.VMEM((tokens, heads * rows_held), F32),
            pltpu.VMEM((rows_held, tokens, channels), BF16),
            pltpu.SMEM((count,), jnp.int32),
            pltpu.SemaphoreType.DMA(()),
        ],
        compiler_params=PARAMS,
        cost_estimate=measured(6),
    )(
        *[
            pltpu.with_memory_space_constraint(x, pltpu.HBM)
            for x in (window_rows, pair, mask_row, chain_row, gain, shift, w_bias.T)
        ]
    )

    far = [m for m in range(owners // 2, owners) if m % 2 == 0]
    passed = [m + 1 for m in far]
    near = list(range(1, owners // 2))
    biases = {0: bias}
    for m in far[::-1] + near[::-1]:
        biases[m] = swap(bias, 2 * m)
    other = swap(own, 1)

    keys, values = pl.pallas_call(
        key_value_kernel,
        out_shape=[
            jax.ShapeDtypeStruct((2 * count, inner, live), BF16),
            jax.ShapeDtypeStruct((2 * count, live, inner), BF16),
        ],
        in_specs=[VMEM] * 4,
        out_specs=[VMEM] * 2,
        compiler_params=PARAMS,
        cost_estimate=measured(2),
    )(own, other, pick, w_project)

    split = (count, owners, 2, rows_held, channels)
    own, other = own.reshape(split), other.reshape(split)
    updates = {}
    straight = pl.pallas_call(
        join_kernel,
        out_shape=jax.ShapeDtypeStruct((len(far) * heads * rows_held, live), BF16),
        in_specs=[VMEM] * len(far) + [ANY],
        out_specs=VMEM,
        compiler_params=PARAMS,
        cost_estimate=measured(0.5),
    )(*[biases[m] for m in far], keys)
    straight = swap(straight, 2)
    for m in passed:
        biases[m] = straight
    sent = {}
    for ms in (far, [0] + near[:1], passed, near[1:]):
        if ms == far:
            after = [biases[m] for m in near]
        elif ms == near[1:]:
            after = [updates[passed[0]]] + [sent[m] for m in far]
        else:
            after = [updates[far[0] if 0 in ms else 0]]
        blocks = len(ms)
        first = [i * heads * rows_held if ms == passed else 0 for i in range(blocks)]
        rows = 2 * count * rows_held
        outs = pl.pallas_call(
            functools.partial(attention_kernel, heads, ms, first),
            out_shape=[jax.ShapeDtypeStruct((2 * count, rows_held, channels), BF16)] * blocks,
            in_specs=[SMEM, SMEM] + [VMEM] * (blocks + 10) + [ANY] * len(after),
            out_specs=[VMEM] * blocks,
            scratch_shapes=[
                pltpu.VMEM((rows, inner), BF16),
                pltpu.VMEM((rows, inner), F32),
                pltpu.VMEM((heads * rows_held, live), F32),
                pltpu.VMEM((rows, inner), BF16),
            ],
            compiler_params=PARAMS,
            cost_estimate=measured(2.2 * blocks),
        )(
            me,
            chain_bias,
            *[biases[m] for m in ms],
            own,
            other,
            keys,
            values,
            mask_row,
            chain_row,
            chain_live,
            w_project,
            gate_bias.reshape(1, inner),
            w_out,
            *after,
        )
        for m, out in zip(ms, outs):
            updates[m] = out
        for m, out in zip(ms, outs):
            sent[m] = out if m == 0 else swap(out, 2 * m)

    whole = []
    for order in ([0] + near[:1] + far + passed, near[1:]):
        placed = len(order)
        whole = [
            pl.pallas_call(
                functools.partial(gather_kernel, order),
                out_shape=jax.ShapeDtypeStruct((owners * 2 * count, rows_held, channels), BF16),
                in_specs=[SMEM] + [ANY] * (placed + len(whole)),
                out_specs=ANY,
                scratch_shapes=[pltpu.SemaphoreType.DMA((placed,))],
                input_output_aliases={placed + 1: 0} if whole else {},
                compiler_params=PARAMS,
                cost_estimate=measured(1),
            )(me, *[sent[m] for m in order], *whole)
        ]
    return whole[0]


def solution(mesh):
    placed = (
        P(("groups", "row"), None, None),
        P(("groups", "row")),
        P("groups"),
        P("groups"),
        P(),
        P(),
        P(),
        P(),
        P(),
        P(),
        P(),
    )
    return jax.shard_map(
        functools.partial(local, mesh.shape["row"]),
        mesh=mesh,
        in_specs=placed,
        out_specs=P("groups", "row", None),
        check_vma=False,
    )
```

```python
import functools

import jax
import jax.numpy as jnp
from jax import lax
from jax.experimental import pallas as pl
from jax.experimental.pallas import tpu as pltpu
from jax.sharding import PartitionSpec as P

F32, BF16 = jnp.float32, jnp.bfloat16
VMEM = pl.BlockSpec(memory_space=pltpu.VMEM)
SMEM = pl.BlockSpec(memory_space=pltpu.SMEM)
ANY = pl.BlockSpec(memory_space=pl.ANY)
NT = (((1,), (1,)), ((), ()))
PARAMS = pltpu.CompilerParams(vmem_limit_bytes=32 * 1024 * 1024)


def measured(microseconds):
    return pl.CostEstimate(
        flops=0, transcendentals=0, bytes_accessed=int(microseconds * 3.69e6)
    )


def normalised(rows, gain, shift):
    channels = rows.shape[-1]
    square = (channels, channels)
    diagonal = lax.broadcasted_iota(jnp.int32, square, 0) == lax.broadcasted_iota(
        jnp.int32, square, 1
    )
    centring = jnp.where(diagonal, 1.0 - 1.0 / channels, -1.0 / channels).astype(BF16)
    d = jnp.dot(rows, centring, preferred_element_type=F32)
    var = jnp.mean(d * d, axis=-1, keepdims=True)
    return (d * lax.rsqrt(var + 1e-05) * gain + shift).astype(BF16)


def live_ranks(mask_row):
    tokens = mask_row.shape[1]
    upper = lax.broadcasted_iota(jnp.int32, (tokens, tokens), 0) <= lax.broadcasted_iota(
        jnp.int32, (tokens, tokens), 1
    )
    ones = jnp.broadcast_to(mask_row.astype(F32), (8, tokens)).astype(BF16)
    running = jnp.dot(ones, upper.astype(F32).astype(BF16), preferred_element_type=F32)[0:1]
    return jnp.where(mask_row == 1, running - 1.0, -1.0)


def picking(mask_row, live):
    ranks = live_ranks(mask_row).astype(jnp.int32)
    wanted = lax.broadcasted_iota(jnp.int32, (live, mask_row.shape[1]), 0)
    return (wanted == ranks).astype(F32).astype(BF16)


def bias_kernel(
    me_ref,
    rows_ref,
    pair_ref,
    mask_ref,
    chain_ref,
    gain_ref,
    shift_ref,
    w_ref,
    out_ref,
    window_ref,
    pick_ref,
    chain_live_ref,
    acc,
    normed,
    rows_s,
    rows_sem,
):
    step = pl.program_id(0)
    rows, tokens, channels = pair_ref.shape
    columns, live = out_ref.shape
    held = rows * pl.num_programs(0)
    heads = w_ref.shape[0]
    row_of = columns // heads
    column = lax.broadcasted_iota(jnp.int32, (heads, columns), 1)
    spread = (column // row_of == lax.broadcasted_iota(jnp.int32, (heads, columns), 0)).astype(F32)
    w = lax.dot_general(
        w_ref[...], spread.astype(BF16), (((0,), (0,)), ((), ())), preferred_element_type=F32
    )
    row_column = lax.broadcasted_iota(jnp.int32, (channels, columns), 1) % row_of
    xs, ws = [], []
    for i in range(rows):
        xs.append(normalised(pair_ref[i], gain_ref[...], shift_ref[...]))
        ws.append(jnp.where(row_column == step * rows + i, w, 0.0).astype(BF16))
        normed[step * rows + i] = xs[i]
    part = jnp.dot(
        jnp.concatenate(xs, axis=1), jnp.concatenate(ws, axis=0), preferred_element_type=F32
    )

    @pl.when(step == 0)
    def _():
        pltpu.make_async_copy(rows_ref, rows_s, rows_sem).start()
        acc[...] = part
        pick = picking(mask_ref[...], live)
        pick_ref[...] = pick
        chain_row = jnp.broadcast_to(chain_ref[...].astype(F32), (8, tokens)).astype(BF16)
        chain_live_ref[...] = lax.dot_general(chain_row, pick, NT, preferred_element_type=F32)

    @pl.when(step > 0)
    def _():
        acc[...] += part

    @pl.when(step == pl.num_programs(0) - 1)
    def _():
        full = acc[...].astype(BF16)
        taken = jnp.dot(pick_ref[...], full, preferred_element_type=F32)
        out_ref[...] = taken.T.astype(BF16)
        pltpu.make_async_copy(rows_ref, rows_s, rows_sem).wait()
        for i in range(window_ref.shape[0]):
            window_ref[i] = normed[lax.rem(rows_s[i], held)]


def key_value_kernel(own_ref, other_ref, pick_ref, w_ref, k_ref, v_ref):
    count = own_ref.shape[0]
    live, inner = v_ref.shape[1:]
    for i in range(count):
        both = jnp.concatenate([own_ref[i], other_ref[i]], axis=1)
        taken = jnp.dot(pick_ref[...], both, preferred_element_type=F32).astype(BF16)
        c = own_ref.shape[2]
        for part in range(2):
            kv = jnp.dot(
                taken[:, part * c : (part + 1) * c],
                w_ref[:, inner : 3 * inner],
                preferred_element_type=F32,
            ).astype(BF16)
            k_ref[i + part * count] = kv[:, :inner].T
            v_ref[i + part * count] = kv[:, inner:]


def attention_kernel(heads, ms, first, me_ref, chain_bias_ref, *refs):
    blocks = len(ms)
    bias_refs, refs = refs[:blocks], refs[blocks:]
    own_ref, other_ref, k_ref, v_ref, mask_ref, chain_ref, chain_live_ref = refs[:7]
    w_ref, gate_bias_ref, w_out_ref = refs[7:10]
    out_refs, (q_s, gate_s, added_s, gated_s) = refs[-4 - blocks : -4], refs[-4:]
    windows, inner, live = k_ref.shape
    half = windows // 2
    block = own_ref.shape[3]
    tokens = mask_ref.shape[1]
    size = inner // heads
    core, chip = lax.rem(me_ref[0], 2), lax.div(me_ref[0], 2)
    chain_live = chain_live_ref[0:1, :]
    lane_head = lax.broadcasted_iota(jnp.int32, (block, inner), 1) // size
    w_q = w_ref[:, :inner]
    w_g = w_ref[:, 3 * inner :]
    for b in range(blocks):
        at = lax.bitwise_xor(chip, ms[b])
        here = (
            lax.broadcasted_iota(jnp.int32, (block, tokens), 1)
            == (at * 2 + core) * block + lax.broadcasted_iota(jnp.int32, (block, tokens), 0)
        ).astype(F32)
        chain_here = jnp.sum(here * chain_ref[...].astype(F32), axis=1, keepdims=True)
        keep = jnp.sum(here * mask_ref[...].astype(F32), axis=1, keepdims=True)
        same = (chain_here == chain_live).astype(F32)
        for h in range(heads):
            rows = slice(h * block, (h + 1) * block)
            taken = pl.ds(first[b] + h * block, block)
            added_s[rows, :] = bias_refs[b][taken, :].astype(F32) + chain_bias_ref[h] * same
        for part, ref in enumerate((own_ref, other_ref)):
            x = ref[:, at, core].reshape(half * block, inner)
            span = pl.ds(part * half * block, half * block)
            q_s[span, :] = (
                jnp.dot(x, w_q, preferred_element_type=F32) * size ** (-0.5)
            ).astype(BF16)
            gate_s[span, :] = jax.nn.sigmoid(
                jnp.dot(x, w_g, preferred_element_type=F32) + gate_bias_ref[...]
            )

        def some_windows(g, carry):
            spans = [
                pl.ds(pl.multiple_of((g * half + i) * block, block), block) for i in range(half)
            ]
            scores = []
            for i in range(half):
                q = q_s[spans[i], :].astype(F32)
                spread = jnp.concatenate(
                    [jnp.where(lane_head == h, q, 0.0) for h in range(heads)], axis=0
                ).astype(BF16)
                scores.append(
                    jnp.dot(spread, k_ref[g * half + i], preferred_element_type=F32) + added_s[...]
                )
            tops = [jnp.max(s, axis=1, keepdims=True) for s in scores]
            raised = [jnp.exp(s - top) for s, top in zip(scores, tops)]
            shares = [1.0 / jnp.sum(r, axis=1, keepdims=True) for r in raised]
            mixed = [
                jnp.dot(r.astype(BF16), v_ref[g * half + i], preferred_element_type=F32)
                for i, r in enumerate(raised)
            ]
            for i in range(half):
                m = mixed[i] * shares[i]
                attended = m[0:block]
                for h in range(1, heads):
                    attended = jnp.where(lane_head == h, m[h * block : (h + 1) * block], attended)
                gated_s[spans[i], :] = (gate_s[spans[i], :] * attended).astype(BF16)
            return carry

        lax.fori_loop(0, 2, some_windows, 0)
        result = jnp.dot(gated_s[...], w_out_ref[...], preferred_element_type=F32)
        result = (result.reshape(windows, block, inner) * keep[None]).astype(BF16)
        out_refs[b][pl.ds(core * half, half)] = result[:half]
        out_refs[b][pl.ds((1 - core) * half, half)] = result[half:]


def join_kernel(*refs):
    parts, out_ref = refs[:-2], refs[-1]
    rows = parts[0].shape[0]
    for i, part in enumerate(parts):
        out_ref[i * rows : (i + 1) * rows, :] = part[...]


def gather_kernel(order, me_ref, *refs):
    parts, out_ref, sems = refs[: len(order)], refs[-2], refs[-1]
    count = parts[0].shape[0]
    chip = lax.div(me_ref[0], 2)
    copies = []
    for i, part in enumerate(parts):
        at = lax.bitwise_xor(chip, order[i]) * count
        copies.append(pltpu.make_async_copy(part, out_ref.at[pl.ds(at, count)], sems.at[i]))
        copies[-1].start()
    for copy in copies:
        copy.wait()


def local(
    devices,
    pair,
    window_rows,
    token_mask,
    chain_ids,
    ln_gain,
    ln_shift,
    w_project,
    gate_bias,
    w_bias,
    chain_bias,
    w_out,
):
    rows_held, tokens, channels = pair.shape
    heads = w_bias.shape[1]
    inner = w_out.shape[0]
    count = window_rows.shape[0]
    live = tokens * 3 // 4
    owners = devices // 2
    me = lax.axis_index("row").astype(jnp.int32).reshape(1)
    mask_row = token_mask.reshape(1, tokens)
    chain_row = chain_ids.reshape(1, tokens)
    gain = ln_gain.reshape(1, channels)
    shift = ln_shift.reshape(1, channels)

    def swap(x, bits):
        return lax.ppermute(x, "row", [(i, i ^ bits) for i in range(devices)])

    step_rows = 16
    bias, own, pick, chain_live = pl.pallas_call(
        bias_kernel,
        grid=(rows_held // step_rows,),
        out_shape=[
            jax.ShapeDtypeStruct((heads * rows_held, live), BF16),
            jax.ShapeDtypeStruct((count, tokens, channels), BF16),
            jax.ShapeDtypeStruct((live, tokens), BF16),
            jax.ShapeDtypeStruct((8, live), F32),
        ],
        in_specs=[
            ANY,
            ANY,
            pl.BlockSpec((step_rows, tokens, channels), lambda i: (i, 0, 0)),
            pl.BlockSpec((1, tokens), lambda i: (0, 0)),
            pl.BlockSpec((1, tokens), lambda i: (0, 0)),
            pl.BlockSpec((1, channels), lambda i: (0, 0)),
            pl.BlockSpec((1, channels), lambda i: (0, 0)),
            pl.BlockSpec((heads, channels), lambda i: (0, 0)),
        ],
        out_specs=[
            pl.BlockSpec((heads * rows_held, live), lambda i: (0, 0)),
            pl.BlockSpec((count, tokens, channels), lambda i: (0, 0, 0)),
            pl.BlockSpec((live, tokens), lambda i: (0, 0)),
            pl.BlockSpec((8, live), lambda i: (0, 0)),
        ],
        scratch_shapes=[
            pltpu.VMEM((tokens, heads * rows_held), F32),
            pltpu.VMEM((rows_held, tokens, channels), BF16),
            pltpu.SMEM((count,), jnp.int32),
            pltpu.SemaphoreType.DMA(()),
        ],
        compiler_params=PARAMS,
        cost_estimate=measured(6),
    )(
        me,
        *[
            pltpu.with_memory_space_constraint(x, pltpu.HBM)
            for x in (window_rows, pair, mask_row, chain_row, gain, shift, w_bias.T)
        ]
    )

    far = [m for m in range(owners // 2, owners) if m % 2 == 0]
    passed = [m + 1 for m in far]
    near = list(range(1, owners // 2))
    biases = {0: bias}
    for m in far[::-1] + near[::-1]:
        biases[m] = swap(bias, 2 * m)
    other = swap(own, 1)

    keys, values = pl.pallas_call(
        key_value_kernel,
        out_shape=[
            jax.ShapeDtypeStruct((2 * count, inner, live), BF16),
            jax.ShapeDtypeStruct((2 * count, live, inner), BF16),
        ],
        in_specs=[VMEM] * 4,
        out_specs=[VMEM] * 2,
        compiler_params=PARAMS,
        cost_estimate=measured(2),
    )(own, other, pick, w_project)

    split = (count, owners, 2, rows_held, channels)
    own, other = own.reshape(split), other.reshape(split)
    updates = {}
    straight = pl.pallas_call(
        join_kernel,
        out_shape=jax.ShapeDtypeStruct((len(far) * heads * rows_held, live), BF16),
        in_specs=[VMEM] * len(far) + [ANY],
        out_specs=VMEM,
        compiler_params=PARAMS,
        cost_estimate=measured(0.5),
    )(*[biases[m] for m in far], keys)
    straight = swap(straight, 2)
    for m in passed:
        biases[m] = straight
    sent = {}
    for ms in (far, [0] + near[:1], passed, near[1:]):
        if ms == far:
            after = [biases[m] for m in near]
        elif ms == near[1:]:
            after = [updates[passed[0]]] + [sent[m] for m in far]
        else:
            after = [updates[far[0] if 0 in ms else 0]]
        blocks = len(ms)
        first = [i * heads * rows_held if ms == passed else 0 for i in range(blocks)]
        rows = 2 * count * rows_held
        outs = pl.pallas_call(
            functools.partial(attention_kernel, heads, ms, first),
            out_shape=[jax.ShapeDtypeStruct((2 * count, rows_held, channels), BF16)] * blocks,
            in_specs=[SMEM, SMEM] + [VMEM] * (blocks + 10) + [ANY] * len(after),
            out_specs=[VMEM] * blocks,
            scratch_shapes=[
                pltpu.VMEM((rows, inner), BF16),
                pltpu.VMEM((rows, inner), F32),
                pltpu.VMEM((heads * rows_held, live), F32),
                pltpu.VMEM((rows, inner), BF16),
            ],
            compiler_params=PARAMS,
            cost_estimate=measured(2.2 * blocks),
        )(
            me,
            chain_bias,
            *[biases[m] for m in ms],
            own,
            other,
            keys,
            values,
            mask_row,
            chain_row,
            chain_live,
            w_project,
            gate_bias.reshape(1, inner),
            w_out,
            *after,
        )
        for m, out in zip(ms, outs):
            updates[m] = out
        for m, out in zip(ms, outs):
            sent[m] = out if m == 0 else swap(out, 2 * m)

    whole = []
    for order in ([0] + near[:1] + far + passed, near[1:]):
        placed = len(order)
        whole = [
            pl.pallas_call(
                functools.partial(gather_kernel, order),
                out_shape=jax.ShapeDtypeStruct((owners * 2 * count, rows_held, channels), BF16),
                in_specs=[SMEM] + [ANY] * (placed + len(whole)),
                out_specs=ANY,
                scratch_shapes=[pltpu.SemaphoreType.DMA((placed,))],
                input_output_aliases={placed + 1: 0} if whole else {},
                compiler_params=PARAMS,
                cost_estimate=measured(1),
            )(me, *[sent[m] for m in order], *whole)
        ]
    return whole[0]


def solution(mesh):
    placed = (
        P(("groups", "row"), None, None),
        P(("groups", "row")),
        P("groups"),
        P("groups"),
        P(),
        P(),
        P(),
        P(),
        P(),
        P(),
        P(),
    )
    return jax.shard_map(
        functools.partial(local, mesh.shape["row"]),
        mesh=mesh,
        in_specs=placed,
        out_specs=P("groups", "row", None),
        check_vma=False,
    )
```

```python
import functools

import jax
import jax.numpy as jnp
from jax import lax
from jax.experimental import pallas as pl
from jax.experimental.pallas import tpu as pltpu
from jax.sharding import PartitionSpec as P

F32, BF16 = jnp.float32, jnp.bfloat16
VMEM = pl.BlockSpec(memory_space=pltpu.VMEM)
SMEM = pl.BlockSpec(memory_space=pltpu.SMEM)
ANY = pl.BlockSpec(memory_space=pl.ANY)
NT = (((1,), (1,)), ((), ()))
PARAMS = pltpu.CompilerParams(vmem_limit_bytes=32 * 1024 * 1024)


def measured(microseconds):
    return pl.CostEstimate(
        flops=0, transcendentals=0, bytes_accessed=int(microseconds * 3.69e6)
    )


def normalised(rows, gain, shift):
    channels = rows.shape[-1]
    square = (channels, channels)
    diagonal = lax.broadcasted_iota(jnp.int32, square, 0) == lax.broadcasted_iota(
        jnp.int32, square, 1
    )
    centring = jnp.where(diagonal, 1.0 - 1.0 / channels, -1.0 / channels).astype(BF16)
    d = jnp.dot(rows, centring, preferred_element_type=F32)
    var = jnp.mean(d * d, axis=-1, keepdims=True)
    return (d * lax.rsqrt(var + 1e-05) * gain + shift).astype(BF16)


def live_ranks(mask_row):
    tokens = mask_row.shape[1]
    upper = lax.broadcasted_iota(jnp.int32, (tokens, tokens), 0) <= lax.broadcasted_iota(
        jnp.int32, (tokens, tokens), 1
    )
    ones = jnp.broadcast_to(mask_row.astype(F32), (8, tokens)).astype(BF16)
    running = jnp.dot(ones, upper.astype(F32).astype(BF16), preferred_element_type=F32)[0:1]
    return jnp.where(mask_row == 1, running - 1.0, -1.0)


def picking(mask_row, live):
    ranks = live_ranks(mask_row).astype(jnp.int32)
    wanted = lax.broadcasted_iota(jnp.int32, (live, mask_row.shape[1]), 0)
    return (wanted == ranks).astype(F32).astype(BF16)


def bias_kernel(
    me_ref,
    rows_ref,
    pair_ref,
    mask_ref,
    chain_ref,
    gain_ref,
    shift_ref,
    w_ref,
    out_ref,
    window_ref,
    pick_ref,
    chain_live_ref,
    acc,
    normed,
    rows_s,
    rows_sem,
):
    step = pl.program_id(0)
    rows, tokens, channels = pair_ref.shape
    columns, live = out_ref.shape
    held = rows * pl.num_programs(0)
    heads = w_ref.shape[0]
    row_of = columns // heads
    column = lax.broadcasted_iota(jnp.int32, (heads, columns), 1)
    spread = (column // row_of == lax.broadcasted_iota(jnp.int32, (heads, columns), 0)).astype(F32)
    w = lax.dot_general(
        w_ref[...], spread.astype(BF16), (((0,), (0,)), ((), ())), preferred_element_type=F32
    )
    row_column = lax.broadcasted_iota(jnp.int32, (channels, columns), 1) % row_of
    xs, ws = [], []
    for i in range(rows):
        xs.append(normalised(pair_ref[i], gain_ref[...], shift_ref[...]))
        ws.append(jnp.where(row_column == step * rows + i, w, 0.0).astype(BF16))
        normed[step * rows + i] = xs[i]
    part = jnp.dot(
        jnp.concatenate(xs, axis=1), jnp.concatenate(ws, axis=0), preferred_element_type=F32
    )

    @pl.when(step == 0)
    def _():
        pltpu.make_async_copy(rows_ref, rows_s, rows_sem).start()
        acc[...] = part
        pick = picking(mask_ref[...], live)
        pick_ref[...] = pick
        chain_row = jnp.broadcast_to(chain_ref[...].astype(F32), (8, tokens)).astype(BF16)
        chain_live_ref[...] = lax.dot_general(chain_row, pick, NT, preferred_element_type=F32)

    @pl.when(step > 0)
    def _():
        acc[...] += part

    @pl.when(step == pl.num_programs(0) - 1)
    def _():
        full = acc[...].astype(BF16)
        taken = jnp.dot(pick_ref[...], full, preferred_element_type=F32)
        out_ref[...] = taken.T.astype(BF16)
        pltpu.make_async_copy(rows_ref, rows_s, rows_sem).wait()
        for i in range(window_ref.shape[0]):
            window_ref[i] = normed[lax.rem(rows_s[i], held)]


def key_value_kernel(own_ref, other_ref, pick_ref, w_ref, k_ref, v_ref):
    count = own_ref.shape[0]
    live, inner = v_ref.shape[1:]
    for i in range(count):
        both = jnp.concatenate([own_ref[i], other_ref[i]], axis=1)
        taken = jnp.dot(pick_ref[...], both, preferred_element_type=F32).astype(BF16)
        c = own_ref.shape[2]
        for part in range(2):
            kv = jnp.dot(
                taken[:, part * c : (part + 1) * c],
                w_ref[:, inner : 3 * inner],
                preferred_element_type=F32,
            ).astype(BF16)
            k_ref[i + part * count] = kv[:, :inner].T
            v_ref[i + part * count] = kv[:, inner:]


def attention_kernel(heads, ms, first, me_ref, chain_bias_ref, *refs):
    blocks = len(ms)
    bias_refs, refs = refs[:blocks], refs[blocks:]
    own_ref, other_ref, k_ref, v_ref, mask_ref, chain_ref, chain_live_ref = refs[:7]
    w_ref, gate_bias_ref, w_out_ref = refs[7:10]
    out_refs, (q_s, gate_s, added_s, gated_s) = refs[-4 - blocks : -4], refs[-4:]
    windows, inner, live = k_ref.shape
    half = windows // 2
    block = own_ref.shape[3]
    tokens = mask_ref.shape[1]
    size = inner // heads
    core, chip = lax.rem(me_ref[0], 2), lax.div(me_ref[0], 2)
    chain_live = chain_live_ref[0:1, :]
    lane_head = lax.broadcasted_iota(jnp.int32, (block, inner), 1) // size
    w_q = w_ref[:, :inner]
    w_g = w_ref[:, 3 * inner :]
    for b in range(blocks):
        at = lax.bitwise_xor(chip, ms[b])
        here = (
            lax.broadcasted_iota(jnp.int32, (block, tokens), 1)
            == (at * 2 + core) * block + lax.broadcasted_iota(jnp.int32, (block, tokens), 0)
        ).astype(F32)
        chain_here = jnp.sum(here * chain_ref[...].astype(F32), axis=1, keepdims=True)
        keep = jnp.sum(here * mask_ref[...].astype(F32), axis=1, keepdims=True)
        same = (chain_here == chain_live).astype(F32)
        for h in range(heads):
            rows = slice(h * block, (h + 1) * block)
            taken = pl.ds(first[b] + h * block, block)
            added_s[rows, :] = bias_refs[b][taken, :].astype(F32) + chain_bias_ref[h] * same
        for part, ref in enumerate((own_ref, other_ref)):
            x = ref[:, at, core].reshape(half * block, inner)
            span = pl.ds(part * half * block, half * block)
            q_s[span, :] = (
                jnp.dot(x, w_q, preferred_element_type=F32) * size ** (-0.5)
            ).astype(BF16)
            gate_s[span, :] = jax.nn.sigmoid(
                jnp.dot(x, w_g, preferred_element_type=F32) + gate_bias_ref[...]
            )

        def some_windows(g, carry):
            spans = [
                pl.ds(pl.multiple_of((g * half + i) * block, block), block) for i in range(half)
            ]
            scores = []
            for i in range(half):
                q = q_s[spans[i], :].astype(F32)
                spread = jnp.concatenate(
                    [jnp.where(lane_head == h, q, 0.0) for h in range(heads)], axis=0
                ).astype(BF16)
                scores.append(
                    jnp.dot(spread, k_ref[g * half + i], preferred_element_type=F32) + added_s[...]
                )
            tops = [jnp.max(s, axis=1, keepdims=True) for s in scores]
            raised = [jnp.exp(s - top) for s, top in zip(scores, tops)]
            shares = [1.0 / jnp.sum(r, axis=1, keepdims=True) for r in raised]
            mixed = [
                jnp.dot(r.astype(BF16), v_ref[g * half + i], preferred_element_type=F32)
                for i, r in enumerate(raised)
            ]
            for i in range(half):
                m = mixed[i] * shares[i]
                attended = m[0:block]
                for h in range(1, heads):
                    attended = jnp.where(lane_head == h, m[h * block : (h + 1) * block], attended)
                gated_s[spans[i], :] = (gate_s[spans[i], :] * attended).astype(BF16)
            return carry

        lax.fori_loop(0, 2, some_windows, 0)
        result = jnp.dot(gated_s[...], w_out_ref[...], preferred_element_type=F32)
        result = (result.reshape(windows, block, inner) * keep[None]).astype(BF16)
        out_refs[b][pl.ds(core * half, half)] = result[:half]
        out_refs[b][pl.ds((1 - core) * half, half)] = result[half:]


def join_kernel(*refs):
    parts, out_ref = refs[:-2], refs[-1]
    rows = parts[0].shape[0]
    for i, part in enumerate(parts):
        out_ref[i * rows : (i + 1) * rows, :] = part[...]


def gather_kernel(order, me_ref, *refs):
    parts, out_ref, sems = refs[: len(order)], refs[-2], refs[-1]
    count = parts[0].shape[0]
    chip = lax.div(me_ref[0], 2)
    copies = []
    for i, part in enumerate(parts):
        at = lax.bitwise_xor(chip, order[i]) * count
        copies.append(pltpu.make_async_copy(part, out_ref.at[pl.ds(at, count)], sems.at[i]))
        copies[-1].start()
    for copy in copies:
        copy.wait()


def local(
    devices,
    pair,
    window_rows,
    token_mask,
    chain_ids,
    ln_gain,
    ln_shift,
    w_project,
    gate_bias,
    w_bias,
    chain_bias,
    w_out,
):
    rows_held, tokens, channels = pair.shape
    heads = w_bias.shape[1]
    inner = w_out.shape[0]
    count = window_rows.shape[0]
    live = tokens * 3 // 4
    owners = devices // 2
    me = lax.axis_index("row").astype(jnp.int32).reshape(1)
    mask_row = token_mask.reshape(1, tokens)
    chain_row = chain_ids.reshape(1, tokens)
    gain = ln_gain.reshape(1, channels)
    shift = ln_shift.reshape(1, channels)

    def swap(x, bits):
        return lax.ppermute(x, "row", [(i, i ^ bits) for i in range(devices)])

    step_rows = 16
    bias, own, pick, chain_live = pl.pallas_call(
        bias_kernel,
        grid=(rows_held // step_rows,),
        out_shape=[
            jax.ShapeDtypeStruct((heads * rows_held, live), BF16),
            jax.ShapeDtypeStruct((count, tokens, channels), BF16),
            jax.ShapeDtypeStruct((live, tokens), BF16),
            jax.ShapeDtypeStruct((8, live), F32),
        ],
        in_specs=[
            ANY,
            ANY,
            pl.BlockSpec((step_rows, tokens, channels), lambda i: (i, 0, 0)),
            pl.BlockSpec((1, tokens), lambda i: (0, 0)),
            pl.BlockSpec((1, tokens), lambda i: (0, 0)),
            pl.BlockSpec((1, channels), lambda i: (0, 0)),
            pl.BlockSpec((1, channels), lambda i: (0, 0)),
            pl.BlockSpec((heads, channels), lambda i: (0, 0)),
        ],
        out_specs=[
            pl.BlockSpec((heads * rows_held, live), lambda i: (0, 0)),
            pl.BlockSpec((count, tokens, channels), lambda i: (0, 0, 0)),
            pl.BlockSpec((live, tokens), lambda i: (0, 0)),
            pl.BlockSpec((8, live), lambda i: (0, 0)),
        ],
        scratch_shapes=[
            pltpu.VMEM((tokens, heads * rows_held), F32),
            pltpu.VMEM((rows_held, tokens, channels), BF16),
            pltpu.SMEM((count,), jnp.int32),
            pltpu.SemaphoreType.DMA(()),
        ],
        compiler_params=PARAMS,
        cost_estimate=measured(6),
    )(
        me,
        *[
            pltpu.with_memory_space_constraint(x, pltpu.HBM)
            for x in (window_rows, pair, mask_row, chain_row, gain, shift, w_bias.T)
        ]
    )

    far = [m for m in range(owners // 2, owners) if m % 2 == 0]
    passed = [m + 1 for m in far]
    near = list(range(1, owners // 2))
    biases = {0: bias}
    for m in far[::-1] + near[::-1]:
        biases[m] = swap(bias, 2 * m)
    other = swap(own, 1)

    keys, values = pl.pallas_call(
        key_value_kernel,
        out_shape=[
            jax.ShapeDtypeStruct((2 * count, inner, live), BF16),
            jax.ShapeDtypeStruct((2 * count, live, inner), BF16),
        ],
        in_specs=[VMEM] * 4,
        out_specs=[VMEM] * 2,
        compiler_params=PARAMS,
        cost_estimate=measured(2),
    )(own, other, pick, w_project)

    split = (count, owners, 2, rows_held, channels)
    own, other = own.reshape(split), other.reshape(split)
    updates = {}
    straight = pl.pallas_call(
        join_kernel,
        out_shape=jax.ShapeDtypeStruct((len(far) * heads * rows_held, live), BF16),
        in_specs=[VMEM] * len(far) + [ANY],
        out_specs=VMEM,
        compiler_params=PARAMS,
        cost_estimate=measured(0.5),
    )(*[biases[m] for m in far], keys)
    straight = swap(straight, 2)
    for m in passed:
        biases[m] = straight
    sent = {}
    for ms in (far, passed, near[1:], [0] + near[:1]):
        if ms == far:
            after = [biases[near[0]]]
        elif ms == passed:
            after = [updates[far[0]]]
        elif ms == near[1:]:
            after = [updates[m] for m in passed]
        else:
            after = [updates[near[1]], sent[far[0]]]
        blocks = len(ms)
        first = [i * heads * rows_held if ms == passed else 0 for i in range(blocks)]
        rows = 2 * count * rows_held
        outs = pl.pallas_call(
            functools.partial(attention_kernel, heads, ms, first),
            out_shape=[jax.ShapeDtypeStruct((2 * count, rows_held, channels), BF16)] * blocks,
            in_specs=[SMEM, SMEM] + [VMEM] * (blocks + 10) + [ANY] * len(after),
            out_specs=[VMEM] * blocks,
            scratch_shapes=[
                pltpu.VMEM((rows, inner), BF16),
                pltpu.VMEM((rows, inner), F32),
                pltpu.VMEM((heads * rows_held, live), F32),
                pltpu.VMEM((rows, inner), BF16),
            ],
            compiler_params=PARAMS,
            cost_estimate=measured(2.2 * blocks),
        )(
            me,
            chain_bias,
            *[biases[m] for m in ms],
            own,
            other,
            keys,
            values,
            mask_row,
            chain_row,
            chain_live,
            w_project,
            gate_bias.reshape(1, inner),
            w_out,
            *after,
        )
        for m, out in zip(ms, outs):
            updates[m] = out
        for m, out in zip(ms, outs):
            sent[m] = out if m == 0 else swap(out, 2 * m)

    whole = []
    for order in (near[1:] + far + passed, [0] + near[:1]):
        placed = len(order)
        whole = [
            pl.pallas_call(
                functools.partial(gather_kernel, order),
                out_shape=jax.ShapeDtypeStruct((owners * 2 * count, rows_held, channels), BF16),
                in_specs=[SMEM] + [ANY] * (placed + len(whole)),
                out_specs=ANY,
                scratch_shapes=[pltpu.SemaphoreType.DMA((placed,))],
                input_output_aliases={placed + 1: 0} if whole else {},
                compiler_params=PARAMS,
                cost_estimate=measured(1),
            )(me, *[sent[m] for m in order], *whole)
        ]
    return whole[0]


def solution(mesh):
    placed = (
        P(("groups", "row"), None, None),
        P(("groups", "row")),
        P("groups"),
        P("groups"),
        P(),
        P(),
        P(),
        P(),
        P(),
        P(),
        P(),
    )
    return jax.shard_map(
        functools.partial(local, mesh.shape["row"]),
        mesh=mesh,
        in_specs=placed,
        out_specs=P("groups", "row", None),
        check_vma=False,
    )
```

```python
import functools

import jax
import jax.numpy as jnp
from jax import lax
from jax.experimental import pallas as pl
from jax.experimental.pallas import tpu as pltpu
from jax.sharding import PartitionSpec as P

F32, BF16 = jnp.float32, jnp.bfloat16
VMEM = pl.BlockSpec(memory_space=pltpu.VMEM)
SMEM = pl.BlockSpec(memory_space=pltpu.SMEM)
ANY = pl.BlockSpec(memory_space=pl.ANY)
NT = (((1,), (1,)), ((), ()))
PARAMS = pltpu.CompilerParams(vmem_limit_bytes=32 * 1024 * 1024)


def measured(microseconds):
    return pl.CostEstimate(
        flops=0, transcendentals=0, bytes_accessed=int(microseconds * 3.69e6)
    )


def normalised(rows, gain, shift):
    channels = rows.shape[-1]
    square = (channels, channels)
    diagonal = lax.broadcasted_iota(jnp.int32, square, 0) == lax.broadcasted_iota(
        jnp.int32, square, 1
    )
    centring = jnp.where(diagonal, 1.0 - 1.0 / channels, -1.0 / channels).astype(BF16)
    d = jnp.dot(rows, centring, preferred_element_type=F32)
    var = jnp.mean(d * d, axis=-1, keepdims=True)
    return (d * lax.rsqrt(var + 1e-05) * gain + shift).astype(BF16)


def live_ranks(mask_row):
    tokens = mask_row.shape[1]
    upper = lax.broadcasted_iota(jnp.int32, (tokens, tokens), 0) <= lax.broadcasted_iota(
        jnp.int32, (tokens, tokens), 1
    )
    ones = jnp.broadcast_to(mask_row.astype(F32), (8, tokens)).astype(BF16)
    running = jnp.dot(ones, upper.astype(F32).astype(BF16), preferred_element_type=F32)[0:1]
    return jnp.where(mask_row == 1, running - 1.0, -1.0)


def picking(mask_row, live):
    ranks = live_ranks(mask_row).astype(jnp.int32)
    wanted = lax.broadcasted_iota(jnp.int32, (live, mask_row.shape[1]), 0)
    return (wanted == ranks).astype(F32).astype(BF16)


def bias_kernel(
    me_ref,
    rows_ref,
    pair_ref,
    mask_ref,
    chain_ref,
    gain_ref,
    shift_ref,
    w_ref,
    out_ref,
    window_ref,
    pick_ref,
    chain_live_ref,
    acc,
    normed,
    rows_s,
    rows_sem,
):
    step = pl.program_id(0)
    rows, tokens, channels = pair_ref.shape
    columns, live = out_ref.shape
    held = rows * pl.num_programs(0)
    heads = w_ref.shape[0]
    row_of = columns // heads
    column = lax.broadcasted_iota(jnp.int32, (heads, columns), 1)
    spread = (column // row_of == lax.broadcasted_iota(jnp.int32, (heads, columns), 0)).astype(F32)
    w = lax.dot_general(
        w_ref[...], spread.astype(BF16), (((0,), (0,)), ((), ())), preferred_element_type=F32
    )
    row_column = lax.broadcasted_iota(jnp.int32, (channels, columns), 1) % row_of
    xs, ws = [], []
    for i in range(rows):
        xs.append(normalised(pair_ref[i], gain_ref[...], shift_ref[...]))
        ws.append(jnp.where(row_column == step * rows + i, w, 0.0).astype(BF16))
        normed[step * rows + i] = xs[i]
    part = jnp.dot(
        jnp.concatenate(xs, axis=1), jnp.concatenate(ws, axis=0), preferred_element_type=F32
    )

    @pl.when(step == 0)
    def _():
        pltpu.make_async_copy(rows_ref, rows_s, rows_sem).start()
        acc[...] = part
        pick = picking(mask_ref[...], live)
        pick_ref[...] = pick
        chain_row = jnp.broadcast_to(chain_ref[...].astype(F32), (8, tokens)).astype(BF16)
        chain_live_ref[...] = lax.dot_general(chain_row, pick, NT, preferred_element_type=F32)

    @pl.when(step > 0)
    def _():
        acc[...] += part

    @pl.when(step == pl.num_programs(0) - 1)
    def _():
        full = acc[...].astype(BF16)
        taken = jnp.dot(pick_ref[...], full, preferred_element_type=F32)
        out_ref[...] = taken.T.astype(BF16)
        pltpu.make_async_copy(rows_ref, rows_s, rows_sem).wait()
        for i in range(window_ref.shape[0]):
            window_ref[i] = normed[lax.rem(rows_s[i], held)]


def key_value_kernel(own_ref, other_ref, pick_ref, w_ref, k_ref, v_ref):
    count = own_ref.shape[0]
    live, inner = v_ref.shape[1:]
    for i in range(count):
        both = jnp.concatenate([own_ref[i], other_ref[i]], axis=1)
        taken = jnp.dot(pick_ref[...], both, preferred_element_type=F32).astype(BF16)
        c = own_ref.shape[2]
        for part in range(2):
            kv = jnp.dot(
                taken[:, part * c : (part + 1) * c],
                w_ref[:, inner : 3 * inner],
                preferred_element_type=F32,
            ).astype(BF16)
            k_ref[i + part * count] = kv[:, :inner].T
            v_ref[i + part * count] = kv[:, inner:]


def attention_kernel(heads, ms, first, me_ref, chain_bias_ref, *refs):
    blocks = len(ms)
    bias_refs, refs = refs[:blocks], refs[blocks:]
    own_ref, other_ref, k_ref, v_ref, mask_ref, chain_ref, chain_live_ref = refs[:7]
    w_ref, gate_bias_ref, w_out_ref = refs[7:10]
    out_refs, (q_s, gate_s, added_s, gated_s) = refs[-4 - blocks : -4], refs[-4:]
    windows, inner, live = k_ref.shape
    half = windows // 2
    block = own_ref.shape[3]
    tokens = mask_ref.shape[1]
    size = inner // heads
    core, chip = lax.rem(me_ref[0], 2), lax.div(me_ref[0], 2)
    chain_live = chain_live_ref[0:1, :]
    lane_head = lax.broadcasted_iota(jnp.int32, (block, inner), 1) // size
    w_q = w_ref[:, :inner]
    w_g = w_ref[:, 3 * inner :]
    for b in range(blocks):
        at = lax.bitwise_xor(chip, ms[b])
        here = (
            lax.broadcasted_iota(jnp.int32, (block, tokens), 1)
            == (at * 2 + core) * block + lax.broadcasted_iota(jnp.int32, (block, tokens), 0)
        ).astype(F32)
        chain_here = jnp.sum(here * chain_ref[...].astype(F32), axis=1, keepdims=True)
        keep = jnp.sum(here * mask_ref[...].astype(F32), axis=1, keepdims=True)
        same = (chain_here == chain_live).astype(F32)
        for h in range(heads):
            rows = slice(h * block, (h + 1) * block)
            taken = pl.ds(first[b] + h * block, block)
            added_s[rows, :] = bias_refs[b][taken, :].astype(F32) + chain_bias_ref[h] * same
        for part, ref in enumerate((own_ref, other_ref)):
            x = ref[:, at, core].reshape(half * block, inner)
            span = pl.ds(part * half * block, half * block)
            q_s[span, :] = (
                jnp.dot(x, w_q, preferred_element_type=F32) * size ** (-0.5)
            ).astype(BF16)
            gate_s[span, :] = jax.nn.sigmoid(
                jnp.dot(x, w_g, preferred_element_type=F32) + gate_bias_ref[...]
            )

        def some_windows(g, carry):
            spans = [
                pl.ds(pl.multiple_of((g * half + i) * block, block), block) for i in range(half)
            ]
            scores = []
            for i in range(half):
                q = q_s[spans[i], :].astype(F32)
                spread = jnp.concatenate(
                    [jnp.where(lane_head == h, q, 0.0) for h in range(heads)], axis=0
                ).astype(BF16)
                scores.append(
                    jnp.dot(spread, k_ref[g * half + i], preferred_element_type=F32) + added_s[...]
                )
            tops = [jnp.max(s, axis=1, keepdims=True) for s in scores]
            raised = [jnp.exp(s - top) for s, top in zip(scores, tops)]
            shares = [1.0 / jnp.sum(r, axis=1, keepdims=True) for r in raised]
            mixed = [
                jnp.dot(r.astype(BF16), v_ref[g * half + i], preferred_element_type=F32)
                for i, r in enumerate(raised)
            ]
            for i in range(half):
                m = mixed[i] * shares[i]
                attended = m[0:block]
                for h in range(1, heads):
                    attended = jnp.where(lane_head == h, m[h * block : (h + 1) * block], attended)
                gated_s[spans[i], :] = (gate_s[spans[i], :] * attended).astype(BF16)
            return carry

        lax.fori_loop(0, 2, some_windows, 0)
        result = jnp.dot(gated_s[...], w_out_ref[...], preferred_element_type=F32)
        result = (result.reshape(windows, block, inner) * keep[None]).astype(BF16)
        out_refs[b][pl.ds(core * half, half)] = result[:half]
        out_refs[b][pl.ds((1 - core) * half, half)] = result[half:]


def join_kernel(*refs):
    parts, out_ref = refs[:-2], refs[-1]
    rows = parts[0].shape[0]
    for i, part in enumerate(parts):
        out_ref[i * rows : (i + 1) * rows, :] = part[...]


def gather_kernel(order, me_ref, *refs):
    parts, out_ref, sems = refs[: len(order)], refs[-2], refs[-1]
    count = parts[0].shape[0]
    chip = lax.div(me_ref[0], 2)
    copies = []
    for i, part in enumerate(parts):
        at = lax.bitwise_xor(chip, order[i]) * count
        copies.append(pltpu.make_async_copy(part, out_ref.at[pl.ds(at, count)], sems.at[i]))
        copies[-1].start()
    for copy in copies:
        copy.wait()


def local(
    devices,
    pair,
    window_rows,
    token_mask,
    chain_ids,
    ln_gain,
    ln_shift,
    w_project,
    gate_bias,
    w_bias,
    chain_bias,
    w_out,
):
    rows_held, tokens, channels = pair.shape
    heads = w_bias.shape[1]
    inner = w_out.shape[0]
    count = window_rows.shape[0]
    live = tokens * 3 // 4
    owners = devices // 2
    me = lax.axis_index("row").astype(jnp.int32).reshape(1)
    mask_row = token_mask.reshape(1, tokens)
    chain_row = chain_ids.reshape(1, tokens)
    gain = ln_gain.reshape(1, channels)
    shift = ln_shift.reshape(1, channels)

    def swap(x, bits):
        return lax.ppermute(x, "row", [(i, i ^ bits) for i in range(devices)])

    step_rows = 16
    bias, own, pick, chain_live = pl.pallas_call(
        bias_kernel,
        grid=(rows_held // step_rows,),
        out_shape=[
            jax.ShapeDtypeStruct((heads * rows_held, live), BF16),
            jax.ShapeDtypeStruct((count, tokens, channels), BF16),
            jax.ShapeDtypeStruct((live, tokens), BF16),
            jax.ShapeDtypeStruct((8, live), F32),
        ],
        in_specs=[
            ANY,
            ANY,
            pl.BlockSpec((step_rows, tokens, channels), lambda i: (i, 0, 0)),
            pl.BlockSpec((1, tokens), lambda i: (0, 0)),
            pl.BlockSpec((1, tokens), lambda i: (0, 0)),
            pl.BlockSpec((1, channels), lambda i: (0, 0)),
            pl.BlockSpec((1, channels), lambda i: (0, 0)),
            pl.BlockSpec((heads, channels), lambda i: (0, 0)),
        ],
        out_specs=[
            pl.BlockSpec((heads * rows_held, live), lambda i: (0, 0)),
            pl.BlockSpec((count, tokens, channels), lambda i: (0, 0, 0)),
            pl.BlockSpec((live, tokens), lambda i: (0, 0)),
            pl.BlockSpec((8, live), lambda i: (0, 0)),
        ],
        scratch_shapes=[
            pltpu.VMEM((tokens, heads * rows_held), F32),
            pltpu.VMEM((rows_held, tokens, channels), BF16),
            pltpu.SMEM((count,), jnp.int32),
            pltpu.SemaphoreType.DMA(()),
        ],
        compiler_params=PARAMS,
        cost_estimate=measured(6),
    )(
        me,
        *[
            pltpu.with_memory_space_constraint(x, pltpu.HBM)
            for x in (window_rows, pair, mask_row, chain_row, gain, shift, w_bias.T)
        ]
    )

    far = [m for m in range(owners // 2, owners) if m % 2 == 0]
    passed = [m + 1 for m in far]
    near = list(range(1, owners // 2))
    biases = {0: bias}
    for m in far[::-1] + near[::-1]:
        biases[m] = swap(bias, 2 * m)
    other = swap(own, 1)

    keys, values = pl.pallas_call(
        key_value_kernel,
        out_shape=[
            jax.ShapeDtypeStruct((2 * count, inner, live), BF16),
            jax.ShapeDtypeStruct((2 * count, live, inner), BF16),
        ],
        in_specs=[VMEM] * 4,
        out_specs=[VMEM] * 2,
        compiler_params=PARAMS,
        cost_estimate=measured(2),
    )(own, other, pick, w_project)

    split = (count, owners, 2, rows_held, channels)
    own, other = own.reshape(split), other.reshape(split)
    updates = {}
    straight = pl.pallas_call(
        join_kernel,
        out_shape=jax.ShapeDtypeStruct((len(far) * heads * rows_held, live), BF16),
        in_specs=[VMEM] * len(far) + [ANY],
        out_specs=VMEM,
        compiler_params=PARAMS,
        cost_estimate=measured(0.5),
    )(*[biases[m] for m in far], keys)
    straight = swap(straight, 2)
    for m in passed:
        biases[m] = straight
    sent = {}
    for ms in (far, passed, near[1:], [0] + near[:1]):
        if ms == far:
            after = [biases[m] for m in near]
        elif ms == passed:
            after = [updates[far[0]]]
        elif ms == near[1:]:
            after = [updates[m] for m in passed]
        else:
            after = [updates[near[1]], sent[far[0]]]
        blocks = len(ms)
        first = [i * heads * rows_held if ms == passed else 0 for i in range(blocks)]
        rows = 2 * count * rows_held
        outs = pl.pallas_call(
            functools.partial(attention_kernel, heads, ms, first),
            out_shape=[jax.ShapeDtypeStruct((2 * count, rows_held, channels), BF16)] * blocks,
            in_specs=[SMEM, SMEM] + [VMEM] * (blocks + 10) + [ANY] * len(after),
            out_specs=[VMEM] * blocks,
            scratch_shapes=[
                pltpu.VMEM((rows, inner), BF16),
                pltpu.VMEM((rows, inner), F32),
                pltpu.VMEM((heads * rows_held, live), F32),
                pltpu.VMEM((rows, inner), BF16),
            ],
            compiler_params=PARAMS,
            cost_estimate=measured(2.2 * blocks),
        )(
            me,
            chain_bias,
            *[biases[m] for m in ms],
            own,
            other,
            keys,
            values,
            mask_row,
            chain_row,
            chain_live,
            w_project,
            gate_bias.reshape(1, inner),
            w_out,
            *after,
        )
        for m, out in zip(ms, outs):
            updates[m] = out
        for m, out in zip(ms, outs):
            sent[m] = out if m == 0 else swap(out, 2 * m)

    whole = []
    for order in (near[1:] + far + passed, [0] + near[:1]):
        placed = len(order)
        whole = [
            pl.pallas_call(
                functools.partial(gather_kernel, order),
                out_shape=jax.ShapeDtypeStruct((owners * 2 * count, rows_held, channels), BF16),
                in_specs=[SMEM] + [ANY] * (placed + len(whole)),
                out_specs=ANY,
                scratch_shapes=[pltpu.SemaphoreType.DMA((placed,))],
                input_output_aliases={placed + 1: 0} if whole else {},
                compiler_params=PARAMS,
                cost_estimate=measured(1),
            )(me, *[sent[m] for m in order], *whole)
        ]
    return whole[0]


def solution(mesh):
    placed = (
        P(("groups", "row"), None, None),
        P(("groups", "row")),
        P("groups"),
        P("groups"),
        P(),
        P(),
        P(),
        P(),
        P(),
        P(),
        P(),
    )
    return jax.shard_map(
        functools.partial(local, mesh.shape["row"]),
        mesh=mesh,
        in_specs=placed,
        out_specs=P("groups", "row", None),
        check_vma=False,
    )
```

```python
import functools

import jax
import jax.numpy as jnp
from jax import lax
from jax.experimental import pallas as pl
from jax.experimental.pallas import tpu as pltpu
from jax.sharding import PartitionSpec as P

F32, BF16 = jnp.float32, jnp.bfloat16
VMEM = pl.BlockSpec(memory_space=pltpu.VMEM)
SMEM = pl.BlockSpec(memory_space=pltpu.SMEM)
ANY = pl.BlockSpec(memory_space=pl.ANY)
NT = (((1,), (1,)), ((), ()))
PARAMS = pltpu.CompilerParams(vmem_limit_bytes=32 * 1024 * 1024)


def measured(microseconds):
    return pl.CostEstimate(
        flops=0, transcendentals=0, bytes_accessed=int(microseconds * 3.69e6)
    )


def normalised(rows, gain, shift):
    channels = rows.shape[-1]
    square = (channels, channels)
    diagonal = lax.broadcasted_iota(jnp.int32, square, 0) == lax.broadcasted_iota(
        jnp.int32, square, 1
    )
    centring = jnp.where(diagonal, 1.0 - 1.0 / channels, -1.0 / channels).astype(BF16)
    d = jnp.dot(rows, centring, preferred_element_type=F32)
    var = jnp.mean(d * d, axis=-1, keepdims=True)
    return (d * lax.rsqrt(var + 1e-05) * gain + shift).astype(BF16)


def live_ranks(mask_row):
    tokens = mask_row.shape[1]
    upper = lax.broadcasted_iota(jnp.int32, (tokens, tokens), 0) <= lax.broadcasted_iota(
        jnp.int32, (tokens, tokens), 1
    )
    ones = jnp.broadcast_to(mask_row.astype(F32), (8, tokens)).astype(BF16)
    running = jnp.dot(ones, upper.astype(F32).astype(BF16), preferred_element_type=F32)[0:1]
    return jnp.where(mask_row == 1, running - 1.0, -1.0)


def picking(mask_row, live):
    ranks = live_ranks(mask_row).astype(jnp.int32)
    wanted = lax.broadcasted_iota(jnp.int32, (live, mask_row.shape[1]), 0)
    return (wanted == ranks).astype(F32).astype(BF16)


def bias_kernel(
    me_ref,
    rows_ref,
    pair_ref,
    mask_ref,
    chain_ref,
    gain_ref,
    shift_ref,
    w_ref,
    out_ref,
    window_ref,
    pick_ref,
    chain_live_ref,
    acc,
    normed,
    rows_s,
    rows_sem,
):
    step = pl.program_id(0)
    rows, tokens, channels = pair_ref.shape
    columns, live = out_ref.shape
    held = rows * pl.num_programs(0)
    heads = w_ref.shape[0]
    row_of = columns // heads
    column = lax.broadcasted_iota(jnp.int32, (heads, columns), 1)
    spread = (column // row_of == lax.broadcasted_iota(jnp.int32, (heads, columns), 0)).astype(F32)
    w = lax.dot_general(
        w_ref[...], spread.astype(BF16), (((0,), (0,)), ((), ())), preferred_element_type=F32
    )
    row_column = lax.broadcasted_iota(jnp.int32, (channels, columns), 1) % row_of
    xs, ws = [], []
    for i in range(rows):
        xs.append(normalised(pair_ref[i], gain_ref[...], shift_ref[...]))
        ws.append(jnp.where(row_column == step * rows + i, w, 0.0).astype(BF16))
        normed[step * rows + i] = xs[i]
    part = jnp.dot(
        jnp.concatenate(xs, axis=1), jnp.concatenate(ws, axis=0), preferred_element_type=F32
    )

    @pl.when(step == 0)
    def _():
        pltpu.make_async_copy(rows_ref, rows_s, rows_sem).start()
        acc[...] = part
        pick = picking(mask_ref[...], live)
        pick_ref[...] = pick
        chain_row = jnp.broadcast_to(chain_ref[...].astype(F32), (8, tokens)).astype(BF16)
        chain_live_ref[...] = lax.dot_general(chain_row, pick, NT, preferred_element_type=F32)

    @pl.when(step > 0)
    def _():
        acc[...] += part

    @pl.when(step == pl.num_programs(0) - 1)
    def _():
        full = acc[...].astype(BF16)
        taken = jnp.dot(pick_ref[...], full, preferred_element_type=F32)
        out_ref[...] = taken.T.astype(BF16)
        pltpu.make_async_copy(rows_ref, rows_s, rows_sem).wait()
        for i in range(window_ref.shape[0]):
            window_ref[i] = normed[lax.rem(rows_s[i], held)]


def key_value_kernel(own_ref, other_ref, pick_ref, w_ref, k_ref, v_ref):
    count = own_ref.shape[0]
    live, inner = v_ref.shape[1:]
    for i in range(count):
        both = jnp.concatenate([own_ref[i], other_ref[i]], axis=1)
        taken = jnp.dot(pick_ref[...], both, preferred_element_type=F32).astype(BF16)
        c = own_ref.shape[2]
        for part in range(2):
            kv = jnp.dot(
                taken[:, part * c : (part + 1) * c],
                w_ref[:, inner : 3 * inner],
                preferred_element_type=F32,
            ).astype(BF16)
            k_ref[i + part * count] = kv[:, :inner].T
            v_ref[i + part * count] = kv[:, inner:]


def attention_kernel(heads, ms, first, me_ref, chain_bias_ref, *refs):
    blocks = len(ms)
    bias_refs, refs = refs[:blocks], refs[blocks:]
    own_ref, other_ref, k_ref, v_ref, mask_ref, chain_ref, chain_live_ref = refs[:7]
    w_ref, gate_bias_ref, w_out_ref = refs[7:10]
    out_refs, (q_s, gate_s, added_s, gated_s) = refs[-4 - blocks : -4], refs[-4:]
    windows, inner, live = k_ref.shape
    half = windows // 2
    block = own_ref.shape[3]
    tokens = mask_ref.shape[1]
    size = inner // heads
    core, chip = lax.rem(me_ref[0], 2), lax.div(me_ref[0], 2)
    chain_live = chain_live_ref[0:1, :]
    lane_head = lax.broadcasted_iota(jnp.int32, (block, inner), 1) // size
    w_q = w_ref[:, :inner]
    w_g = w_ref[:, 3 * inner :]
    for b in range(blocks):
        at = lax.bitwise_xor(chip, ms[b])
        here = (
            lax.broadcasted_iota(jnp.int32, (block, tokens), 1)
            == (at * 2 + core) * block + lax.broadcasted_iota(jnp.int32, (block, tokens), 0)
        ).astype(F32)
        chain_here = jnp.sum(here * chain_ref[...].astype(F32), axis=1, keepdims=True)
        keep = jnp.sum(here * mask_ref[...].astype(F32), axis=1, keepdims=True)
        same = (chain_here == chain_live).astype(F32)
        for h in range(heads):
            rows = slice(h * block, (h + 1) * block)
            taken = pl.ds(first[b] + h * block, block)
            added_s[rows, :] = bias_refs[b][taken, :].astype(F32) + chain_bias_ref[h] * same
        for part, ref in enumerate((own_ref, other_ref)):
            x = ref[:, at, core].reshape(half * block, inner)
            span = pl.ds(part * half * block, half * block)
            q_s[span, :] = (
                jnp.dot(x, w_q, preferred_element_type=F32) * size ** (-0.5)
            ).astype(BF16)
            gate_s[span, :] = jax.nn.sigmoid(
                jnp.dot(x, w_g, preferred_element_type=F32) + gate_bias_ref[...]
            )

        def some_windows(g, carry):
            spans = [
                pl.ds(pl.multiple_of((g * half + i) * block, block), block) for i in range(half)
            ]
            scores = []
            for i in range(half):
                q = q_s[spans[i], :].astype(F32)
                spread = jnp.concatenate(
                    [jnp.where(lane_head == h, q, 0.0) for h in range(heads)], axis=0
                ).astype(BF16)
                scores.append(
                    jnp.dot(spread, k_ref[g * half + i], preferred_element_type=F32) + added_s[...]
                )
            tops = [jnp.max(s, axis=1, keepdims=True) for s in scores]
            raised = [jnp.exp(s - top) for s, top in zip(scores, tops)]
            shares = [1.0 / jnp.sum(r, axis=1, keepdims=True) for r in raised]
            mixed = [
                jnp.dot(r.astype(BF16), v_ref[g * half + i], preferred_element_type=F32)
                for i, r in enumerate(raised)
            ]
            for i in range(half):
                m = mixed[i] * shares[i]
                attended = m[0:block]
                for h in range(1, heads):
                    attended = jnp.where(lane_head == h, m[h * block : (h + 1) * block], attended)
                gated_s[spans[i], :] = (gate_s[spans[i], :] * attended).astype(BF16)
            return carry

        lax.fori_loop(0, 2, some_windows, 0)
        result = jnp.dot(gated_s[...], w_out_ref[...], preferred_element_type=F32)
        result = (result.reshape(windows, block, inner) * keep[None]).astype(BF16)
        out_refs[b][pl.ds(core * half, half)] = result[:half]
        out_refs[b][pl.ds((1 - core) * half, half)] = result[half:]


def join_kernel(*refs):
    parts, out_ref = refs[:-2], refs[-1]
    rows = parts[0].shape[0]
    for i, part in enumerate(parts):
        out_ref[i * rows : (i + 1) * rows, :] = part[...]


def gather_kernel(order, me_ref, *refs):
    parts, out_ref, sems = refs[: len(order)], refs[-2], refs[-1]
    count = parts[0].shape[0]
    chip = lax.div(me_ref[0], 2)
    copies = []
    for i, part in enumerate(parts):
        at = lax.bitwise_xor(chip, order[i]) * count
        copies.append(pltpu.make_async_copy(part, out_ref.at[pl.ds(at, count)], sems.at[i]))
        copies[-1].start()
    for copy in copies:
        copy.wait()


def local(
    devices,
    pair,
    window_rows,
    token_mask,
    chain_ids,
    ln_gain,
    ln_shift,
    w_project,
    gate_bias,
    w_bias,
    chain_bias,
    w_out,
):
    rows_held, tokens, channels = pair.shape
    heads = w_bias.shape[1]
    inner = w_out.shape[0]
    count = window_rows.shape[0]
    live = tokens * 3 // 4
    owners = devices // 2
    me = lax.axis_index("row").astype(jnp.int32).reshape(1)
    mask_row = token_mask.reshape(1, tokens)
    chain_row = chain_ids.reshape(1, tokens)
    gain = ln_gain.reshape(1, channels)
    shift = ln_shift.reshape(1, channels)

    def swap(x, bits):
        return lax.ppermute(x, "row", [(i, i ^ bits) for i in range(devices)])

    step_rows = 16
    bias, own, pick, chain_live = pl.pallas_call(
        bias_kernel,
        grid=(rows_held // step_rows,),
        out_shape=[
            jax.ShapeDtypeStruct((heads * rows_held, live), BF16),
            jax.ShapeDtypeStruct((count, tokens, channels), BF16),
            jax.ShapeDtypeStruct((live, tokens), BF16),
            jax.ShapeDtypeStruct((8, live), F32),
        ],
        in_specs=[
            ANY,
            ANY,
            pl.BlockSpec((step_rows, tokens, channels), lambda i: (i, 0, 0)),
            pl.BlockSpec((1, tokens), lambda i: (0, 0)),
            pl.BlockSpec((1, tokens), lambda i: (0, 0)),
            pl.BlockSpec((1, channels), lambda i: (0, 0)),
            pl.BlockSpec((1, channels), lambda i: (0, 0)),
            pl.BlockSpec((heads, channels), lambda i: (0, 0)),
        ],
        out_specs=[
            pl.BlockSpec((heads * rows_held, live), lambda i: (0, 0)),
            pl.BlockSpec((count, tokens, channels), lambda i: (0, 0, 0)),
            pl.BlockSpec((live, tokens), lambda i: (0, 0)),
            pl.BlockSpec((8, live), lambda i: (0, 0)),
        ],
        scratch_shapes=[
            pltpu.VMEM((tokens, heads * rows_held), F32),
            pltpu.VMEM((rows_held, tokens, channels), BF16),
            pltpu.SMEM((count,), jnp.int32),
            pltpu.SemaphoreType.DMA(()),
        ],
        compiler_params=PARAMS,
        cost_estimate=measured(6),
    )(
        me,
        *[
            pltpu.with_memory_space_constraint(x, pltpu.HBM)
            for x in (window_rows, pair, mask_row, chain_row, gain, shift, w_bias.T)
        ]
    )

    far = [m for m in range(owners // 2, owners) if m % 2 == 0]
    passed = [m + 1 for m in far]
    near = list(range(1, owners // 2))
    biases = {0: bias}
    for m in far[::-1] + near[::-1]:
        biases[m] = swap(bias, 2 * m)
    other = swap(own, 1)

    keys, values = pl.pallas_call(
        key_value_kernel,
        out_shape=[
            jax.ShapeDtypeStruct((2 * count, inner, live), BF16),
            jax.ShapeDtypeStruct((2 * count, live, inner), BF16),
        ],
        in_specs=[VMEM] * 4,
        out_specs=[VMEM] * 2,
        compiler_params=PARAMS,
        cost_estimate=measured(2),
    )(own, other, pick, w_project)

    split = (count, owners, 2, rows_held, channels)
    own, other = own.reshape(split), other.reshape(split)
    updates = {}
    sent = {}
    head, rest = far[-1:], far[:-1]
    for ms in (head, rest, passed, near[1:], [0] + near[:1]):
        if ms == head:
            after = []
        elif ms == rest:
            straight = pl.pallas_call(
                join_kernel,
                out_shape=jax.ShapeDtypeStruct((len(far) * heads * rows_held, live), BF16),
                in_specs=[VMEM] * len(far) + [ANY],
                out_specs=VMEM,
                compiler_params=PARAMS,
                cost_estimate=measured(0.5),
            )(*[biases[m] for m in far], updates[head[0]])
            straight = swap(straight, 2)
            for m in passed:
                biases[m] = straight
            after = [updates[head[0]]] + [biases[m] for m in near]
        elif ms == passed:
            after = [updates[rest[0]]]
        elif ms == near[1:]:
            after = [updates[m] for m in passed]
        else:
            after = [updates[near[1]]] + [sent[m] for m in head]
        blocks = len(ms)
        first = [i * heads * rows_held if ms == passed else 0 for i in range(blocks)]
        rows = 2 * count * rows_held
        outs = pl.pallas_call(
            functools.partial(attention_kernel, heads, ms, first),
            out_shape=[jax.ShapeDtypeStruct((2 * count, rows_held, channels), BF16)] * blocks,
            in_specs=[SMEM, SMEM] + [VMEM] * (blocks + 10) + [ANY] * len(after),
            out_specs=[VMEM] * blocks,
            scratch_shapes=[
                pltpu.VMEM((rows, inner), BF16),
                pltpu.VMEM((rows, inner), F32),
                pltpu.VMEM((heads * rows_held, live), F32),
                pltpu.VMEM((rows, inner), BF16),
            ],
            compiler_params=PARAMS,
            cost_estimate=measured(2.2 * blocks),
        )(
            me,
            chain_bias,
            *[biases[m] for m in ms],
            own,
            other,
            keys,
            values,
            mask_row,
            chain_row,
            chain_live,
            w_project,
            gate_bias.reshape(1, inner),
            w_out,
            *after,
        )
        for m, out in zip(ms, outs):
            updates[m] = out
        for m, out in zip(ms, outs):
            sent[m] = out if m == 0 else swap(out, 2 * m)

    whole = []
    for order in (near[1:] + far + passed, [0] + near[:1]):
        placed = len(order)
        whole = [
            pl.pallas_call(
                functools.partial(gather_kernel, order),
                out_shape=jax.ShapeDtypeStruct((owners * 2 * count, rows_held, channels), BF16),
                in_specs=[SMEM] + [ANY] * (placed + len(whole)),
                out_specs=ANY,
                scratch_shapes=[pltpu.SemaphoreType.DMA((placed,))],
                input_output_aliases={placed + 1: 0} if whole else {},
                compiler_params=PARAMS,
                cost_estimate=measured(1),
            )(me, *[sent[m] for m in order], *whole)
        ]
    return whole[0]


def solution(mesh):
    placed = (
        P(("groups", "row"), None, None),
        P(("groups", "row")),
        P("groups"),
        P("groups"),
        P(),
        P(),
        P(),
        P(),
        P(),
        P(),
        P(),
    )
    return jax.shard_map(
        functools.partial(local, mesh.shape["row"]),
        mesh=mesh,
        in_specs=placed,
        out_specs=P("groups", "row", None),
        check_vma=False,
    )
```

```python
import functools

import jax
import jax.numpy as jnp
from jax import lax
from jax.experimental import pallas as pl
from jax.experimental.pallas import tpu as pltpu
from jax.sharding import PartitionSpec as P

F32, BF16 = jnp.float32, jnp.bfloat16
VMEM = pl.BlockSpec(memory_space=pltpu.VMEM)
SMEM = pl.BlockSpec(memory_space=pltpu.SMEM)
ANY = pl.BlockSpec(memory_space=pl.ANY)
NT = (((1,), (1,)), ((), ()))
PARAMS = pltpu.CompilerParams(vmem_limit_bytes=32 * 1024 * 1024)


def measured(microseconds):
    return pl.CostEstimate(
        flops=0, transcendentals=0, bytes_accessed=int(microseconds * 3.69e6)
    )


def normalised(rows, gain, shift):
    channels = rows.shape[-1]
    square = (channels, channels)
    diagonal = lax.broadcasted_iota(jnp.int32, square, 0) == lax.broadcasted_iota(
        jnp.int32, square, 1
    )
    centring = jnp.where(diagonal, 1.0 - 1.0 / channels, -1.0 / channels).astype(BF16)
    d = jnp.dot(rows, centring, preferred_element_type=F32)
    var = jnp.mean(d * d, axis=-1, keepdims=True)
    return (d * lax.rsqrt(var + 1e-05) * gain + shift).astype(BF16)


def live_ranks(mask_row):
    tokens = mask_row.shape[1]
    upper = lax.broadcasted_iota(jnp.int32, (tokens, tokens), 0) <= lax.broadcasted_iota(
        jnp.int32, (tokens, tokens), 1
    )
    ones = jnp.broadcast_to(mask_row.astype(F32), (8, tokens)).astype(BF16)
    running = jnp.dot(ones, upper.astype(F32).astype(BF16), preferred_element_type=F32)[0:1]
    return jnp.where(mask_row == 1, running - 1.0, -1.0)


def picking(mask_row, live):
    ranks = live_ranks(mask_row).astype(jnp.int32)
    wanted = lax.broadcasted_iota(jnp.int32, (live, mask_row.shape[1]), 0)
    return (wanted == ranks).astype(F32).astype(BF16)


def bias_kernel(
    me_ref,
    rows_ref,
    pair_ref,
    mask_ref,
    chain_ref,
    gain_ref,
    shift_ref,
    w_ref,
    out_ref,
    window_ref,
    pick_ref,
    chain_live_ref,
    acc,
    normed,
    rows_s,
    rows_sem,
):
    step = pl.program_id(0)
    rows, tokens, channels = pair_ref.shape
    columns, live = out_ref.shape
    held = rows * pl.num_programs(0)
    heads = w_ref.shape[0]
    row_of = columns // heads
    column = lax.broadcasted_iota(jnp.int32, (heads, columns), 1)
    spread = (column // row_of == lax.broadcasted_iota(jnp.int32, (heads, columns), 0)).astype(F32)
    w = lax.dot_general(
        w_ref[...], spread.astype(BF16), (((0,), (0,)), ((), ())), preferred_element_type=F32
    )
    row_column = lax.broadcasted_iota(jnp.int32, (channels, columns), 1) % row_of
    xs, ws = [], []
    for i in range(rows):
        xs.append(normalised(pair_ref[i], gain_ref[...], shift_ref[...]))
        ws.append(jnp.where(row_column == step * rows + i, w, 0.0).astype(BF16))
        normed[step * rows + i] = xs[i]
    part = jnp.dot(
        jnp.concatenate(xs, axis=1), jnp.concatenate(ws, axis=0), preferred_element_type=F32
    )

    @pl.when(step == 0)
    def _():
        pltpu.make_async_copy(rows_ref, rows_s, rows_sem).start()
        acc[...] = part
        pick = picking(mask_ref[...], live)
        pick_ref[...] = pick
        chain_row = jnp.broadcast_to(chain_ref[...].astype(F32), (8, tokens)).astype(BF16)
        chain_live_ref[...] = lax.dot_general(chain_row, pick, NT, preferred_element_type=F32)

    @pl.when(step > 0)
    def _():
        acc[...] += part

    @pl.when(step == pl.num_programs(0) - 1)
    def _():
        full = acc[...].astype(BF16)
        taken = jnp.dot(pick_ref[...], full, preferred_element_type=F32)
        out_ref[...] = taken.T.astype(BF16)
        pltpu.make_async_copy(rows_ref, rows_s, rows_sem).wait()
        for i in range(window_ref.shape[0]):
            window_ref[i] = normed[lax.rem(rows_s[i], held)]


def key_value_kernel(own_ref, other_ref, pick_ref, w_ref, k_ref, v_ref):
    count = own_ref.shape[0]
    live, inner = v_ref.shape[1:]
    for i in range(count):
        both = jnp.concatenate([own_ref[i], other_ref[i]], axis=1)
        taken = jnp.dot(pick_ref[...], both, preferred_element_type=F32).astype(BF16)
        c = own_ref.shape[2]
        for part in range(2):
            kv = jnp.dot(
                taken[:, part * c : (part + 1) * c],
                w_ref[:, inner : 3 * inner],
                preferred_element_type=F32,
            ).astype(BF16)
            k_ref[i + part * count] = kv[:, :inner].T
            v_ref[i + part * count] = kv[:, inner:]


def attention_kernel(heads, ms, first, me_ref, chain_bias_ref, *refs):
    blocks = len(ms)
    bias_refs, refs = refs[:blocks], refs[blocks:]
    own_ref, other_ref, k_ref, v_ref, mask_ref, chain_ref, chain_live_ref = refs[:7]
    w_ref, gate_bias_ref, w_out_ref = refs[7:10]
    out_refs, (q_s, gate_s, added_s, gated_s) = refs[-4 - blocks : -4], refs[-4:]
    windows, inner, live = k_ref.shape
    half = windows // 2
    block = own_ref.shape[3]
    tokens = mask_ref.shape[1]
    size = inner // heads
    core, chip = lax.rem(me_ref[0], 2), lax.div(me_ref[0], 2)
    chain_live = chain_live_ref[0:1, :]
    lane_head = lax.broadcasted_iota(jnp.int32, (block, inner), 1) // size
    w_q = w_ref[:, :inner]
    w_g = w_ref[:, 3 * inner :]
    for b in range(blocks):
        at = lax.bitwise_xor(chip, ms[b])
        here = (
            lax.broadcasted_iota(jnp.int32, (block, tokens), 1)
            == (at * 2 + core) * block + lax.broadcasted_iota(jnp.int32, (block, tokens), 0)
        ).astype(F32)
        chain_here = jnp.sum(here * chain_ref[...].astype(F32), axis=1, keepdims=True)
        keep = jnp.sum(here * mask_ref[...].astype(F32), axis=1, keepdims=True)
        same = (chain_here == chain_live).astype(F32)
        for h in range(heads):
            rows = slice(h * block, (h + 1) * block)
            taken = pl.ds(first[b] + h * block, block)
            added_s[rows, :] = bias_refs[b][taken, :].astype(F32) + chain_bias_ref[h] * same
        for part, ref in enumerate((own_ref, other_ref)):
            x = ref[:, at, core].reshape(half * block, inner)
            span = pl.ds(part * half * block, half * block)
            q_s[span, :] = (
                jnp.dot(x, w_q, preferred_element_type=F32) * size ** (-0.5)
            ).astype(BF16)
            gate_s[span, :] = jax.nn.sigmoid(
                jnp.dot(x, w_g, preferred_element_type=F32) + gate_bias_ref[...]
            )

        def some_windows(g):
            spans = [
                slice((g * half + i) * block, (g * half + i + 1) * block) for i in range(half)
            ]
            scores = []
            for i in range(half):
                q = q_s[spans[i], :].astype(F32)
                spread = jnp.concatenate(
                    [jnp.where(lane_head == h, q, 0.0) for h in range(heads)], axis=0
                ).astype(BF16)
                scores.append(
                    jnp.dot(spread, k_ref[g * half + i], preferred_element_type=F32) + added_s[...]
                )
            tops = [jnp.max(s, axis=1, keepdims=True) for s in scores]
            raised = [jnp.exp(s - top) for s, top in zip(scores, tops)]
            shares = [1.0 / jnp.sum(r, axis=1, keepdims=True) for r in raised]
            mixed = [
                jnp.dot(r.astype(BF16), v_ref[g * half + i], preferred_element_type=F32)
                for i, r in enumerate(raised)
            ]
            for i in range(half):
                m = mixed[i] * shares[i]
                attended = m[0:block]
                for h in range(1, heads):
                    attended = jnp.where(lane_head == h, m[h * block : (h + 1) * block], attended)
                gated_s[spans[i], :] = (gate_s[spans[i], :] * attended).astype(BF16)

        for g in range(2):
            some_windows(g)
        result = jnp.dot(gated_s[...], w_out_ref[...], preferred_element_type=F32)
        result = (result.reshape(windows, block, inner) * keep[None]).astype(BF16)
        out_refs[b][pl.ds(core * half, half)] = result[:half]
        out_refs[b][pl.ds((1 - core) * half, half)] = result[half:]


def join_kernel(*refs):
    parts, out_ref = refs[:-2], refs[-1]
    rows = parts[0].shape[0]
    for i, part in enumerate(parts):
        out_ref[i * rows : (i + 1) * rows, :] = part[...]


def gather_kernel(order, me_ref, *refs):
    parts, out_ref, sems = refs[: len(order)], refs[-2], refs[-1]
    count = parts[0].shape[0]
    chip = lax.div(me_ref[0], 2)
    copies = []
    for i, part in enumerate(parts):
        at = lax.bitwise_xor(chip, order[i]) * count
        copies.append(pltpu.make_async_copy(part, out_ref.at[pl.ds(at, count)], sems.at[i]))
        copies[-1].start()
    for copy in copies:
        copy.wait()


def local(
    devices,
    pair,
    window_rows,
    token_mask,
    chain_ids,
    ln_gain,
    ln_shift,
    w_project,
    gate_bias,
    w_bias,
    chain_bias,
    w_out,
):
    rows_held, tokens, channels = pair.shape
    heads = w_bias.shape[1]
    inner = w_out.shape[0]
    count = window_rows.shape[0]
    live = tokens * 3 // 4
    owners = devices // 2
    me = lax.axis_index("row").astype(jnp.int32).reshape(1)
    mask_row = token_mask.reshape(1, tokens)
    chain_row = chain_ids.reshape(1, tokens)
    gain = ln_gain.reshape(1, channels)
    shift = ln_shift.reshape(1, channels)

    def swap(x, bits):
        return lax.ppermute(x, "row", [(i, i ^ bits) for i in range(devices)])

    step_rows = 16
    bias, own, pick, chain_live = pl.pallas_call(
        bias_kernel,
        grid=(rows_held // step_rows,),
        out_shape=[
            jax.ShapeDtypeStruct((heads * rows_held, live), BF16),
            jax.ShapeDtypeStruct((count, tokens, channels), BF16),
            jax.ShapeDtypeStruct((live, tokens), BF16),
            jax.ShapeDtypeStruct((8, live), F32),
        ],
        in_specs=[
            ANY,
            ANY,
            pl.BlockSpec((step_rows, tokens, channels), lambda i: (i, 0, 0)),
            pl.BlockSpec((1, tokens), lambda i: (0, 0)),
            pl.BlockSpec((1, tokens), lambda i: (0, 0)),
            pl.BlockSpec((1, channels), lambda i: (0, 0)),
            pl.BlockSpec((1, channels), lambda i: (0, 0)),
            pl.BlockSpec((heads, channels), lambda i: (0, 0)),
        ],
        out_specs=[
            pl.BlockSpec((heads * rows_held, live), lambda i: (0, 0)),
            pl.BlockSpec((count, tokens, channels), lambda i: (0, 0, 0)),
            pl.BlockSpec((live, tokens), lambda i: (0, 0)),
            pl.BlockSpec((8, live), lambda i: (0, 0)),
        ],
        scratch_shapes=[
            pltpu.VMEM((tokens, heads * rows_held), F32),
            pltpu.VMEM((rows_held, tokens, channels), BF16),
            pltpu.SMEM((count,), jnp.int32),
            pltpu.SemaphoreType.DMA(()),
        ],
        compiler_params=PARAMS,
        cost_estimate=measured(6),
    )(
        me,
        *[
            pltpu.with_memory_space_constraint(x, pltpu.HBM)
            for x in (window_rows, pair, mask_row, chain_row, gain, shift, w_bias.T)
        ]
    )

    far = [m for m in range(owners // 2, owners) if m % 2 == 0]
    passed = [m + 1 for m in far]
    near = list(range(1, owners // 2))
    biases = {0: bias}
    for m in far[::-1] + near[::-1]:
        biases[m] = swap(bias, 2 * m)
    other = swap(own, 1)

    keys, values = pl.pallas_call(
        key_value_kernel,
        out_shape=[
            jax.ShapeDtypeStruct((2 * count, inner, live), BF16),
            jax.ShapeDtypeStruct((2 * count, live, inner), BF16),
        ],
        in_specs=[VMEM] * 4,
        out_specs=[VMEM] * 2,
        compiler_params=PARAMS,
        cost_estimate=measured(2),
    )(own, other, pick, w_project)

    split = (count, owners, 2, rows_held, channels)
    own, other = own.reshape(split), other.reshape(split)
    updates = {}
    sent = {}
    head, rest = far[-1:], far[:-1]
    for ms in (head, rest, passed, near[1:], [0] + near[:1]):
        if ms == head:
            after = []
        elif ms == rest:
            straight = pl.pallas_call(
                join_kernel,
                out_shape=jax.ShapeDtypeStruct((len(far) * heads * rows_held, live), BF16),
                in_specs=[VMEM] * len(far) + [ANY],
                out_specs=VMEM,
                compiler_params=PARAMS,
                cost_estimate=measured(0.5),
            )(*[biases[m] for m in far], updates[head[0]])
            straight = swap(straight, 2)
            for m in passed:
                biases[m] = straight
            after = [updates[head[0]]] + [biases[m] for m in near]
        elif ms == passed:
            after = [updates[rest[0]]]
        elif ms == near[1:]:
            after = [updates[m] for m in passed]
        else:
            after = [updates[near[1]]] + [sent[m] for m in head]
        blocks = len(ms)
        first = [i * heads * rows_held if ms == passed else 0 for i in range(blocks)]
        rows = 2 * count * rows_held
        outs = pl.pallas_call(
            functools.partial(attention_kernel, heads, ms, first),
            out_shape=[jax.ShapeDtypeStruct((2 * count, rows_held, channels), BF16)] * blocks,
            in_specs=[SMEM, SMEM] + [VMEM] * (blocks + 10) + [ANY] * len(after),
            out_specs=[VMEM] * blocks,
            scratch_shapes=[
                pltpu.VMEM((rows, inner), BF16),
                pltpu.VMEM((rows, inner), F32),
                pltpu.VMEM((heads * rows_held, live), F32),
                pltpu.VMEM((rows, inner), BF16),
            ],
            compiler_params=PARAMS,
            cost_estimate=measured(2.2 * blocks),
        )(
            me,
            chain_bias,
            *[biases[m] for m in ms],
            own,
            other,
            keys,
            values,
            mask_row,
            chain_row,
            chain_live,
            w_project,
            gate_bias.reshape(1, inner),
            w_out,
            *after,
        )
        for m, out in zip(ms, outs):
            updates[m] = out
        for m, out in zip(ms, outs):
            sent[m] = out if m == 0 else swap(out, 2 * m)

    whole = []
    for order in (near[1:] + far + passed, [0] + near[:1]):
        placed = len(order)
        whole = [
            pl.pallas_call(
                functools.partial(gather_kernel, order),
                out_shape=jax.ShapeDtypeStruct((owners * 2 * count, rows_held, channels), BF16),
                in_specs=[SMEM] + [ANY] * (placed + len(whole)),
                out_specs=ANY,
                scratch_shapes=[pltpu.SemaphoreType.DMA((placed,))],
                input_output_aliases={placed + 1: 0} if whole else {},
                compiler_params=PARAMS,
                cost_estimate=measured(1),
            )(me, *[sent[m] for m in order], *whole)
        ]
    return whole[0]


def solution(mesh):
    placed = (
        P(("groups", "row"), None, None),
        P(("groups", "row")),
        P("groups"),
        P("groups"),
        P(),
        P(),
        P(),
        P(),
        P(),
        P(),
        P(),
    )
    return jax.shard_map(
        functools.partial(local, mesh.shape["row"]),
        mesh=mesh,
        in_specs=placed,
        out_specs=P("groups", "row", None),
        check_vma=False,
    )
```

```python
import functools

import jax
import jax.numpy as jnp
from jax import lax
from jax.experimental import pallas as pl
from jax.experimental.pallas import tpu as pltpu
from jax.sharding import PartitionSpec as P

F32, BF16 = jnp.float32, jnp.bfloat16
VMEM = pl.BlockSpec(memory_space=pltpu.VMEM)
SMEM = pl.BlockSpec(memory_space=pltpu.SMEM)
ANY = pl.BlockSpec(memory_space=pl.ANY)
NT = (((1,), (1,)), ((), ()))
PARAMS = pltpu.CompilerParams(vmem_limit_bytes=32 * 1024 * 1024)


def measured(microseconds):
    return pl.CostEstimate(
        flops=0, transcendentals=0, bytes_accessed=int(microseconds * 3.69e6)
    )


def normalised(rows, gain, shift):
    channels = rows.shape[-1]
    square = (channels, channels)
    diagonal = lax.broadcasted_iota(jnp.int32, square, 0) == lax.broadcasted_iota(
        jnp.int32, square, 1
    )
    centring = jnp.where(diagonal, 1.0 - 1.0 / channels, -1.0 / channels).astype(BF16)
    d = jnp.dot(rows, centring, preferred_element_type=F32)
    var = jnp.mean(d * d, axis=-1, keepdims=True)
    return (d * lax.rsqrt(var + 1e-05) * gain + shift).astype(BF16)


def live_ranks(mask_row):
    tokens = mask_row.shape[1]
    upper = lax.broadcasted_iota(jnp.int32, (tokens, tokens), 0) <= lax.broadcasted_iota(
        jnp.int32, (tokens, tokens), 1
    )
    ones = jnp.broadcast_to(mask_row.astype(F32), (8, tokens)).astype(BF16)
    running = jnp.dot(ones, upper.astype(F32).astype(BF16), preferred_element_type=F32)[0:1]
    return jnp.where(mask_row == 1, running - 1.0, -1.0)


def picking(mask_row, live):
    ranks = live_ranks(mask_row).astype(jnp.int32)
    wanted = lax.broadcasted_iota(jnp.int32, (live, mask_row.shape[1]), 0)
    return (wanted == ranks).astype(F32).astype(BF16)


def bias_kernel(
    me_ref,
    rows_ref,
    pair_ref,
    mask_ref,
    chain_ref,
    gain_ref,
    shift_ref,
    w_ref,
    out_ref,
    window_ref,
    pick_ref,
    chain_live_ref,
    acc,
    normed,
    rows_s,
    rows_sem,
):
    step = pl.program_id(0)
    rows, tokens, channels = pair_ref.shape
    columns, live = out_ref.shape
    held = rows * pl.num_programs(0)
    heads = w_ref.shape[0]
    row_of = columns // heads
    column = lax.broadcasted_iota(jnp.int32, (heads, columns), 1)
    spread = (column // row_of == lax.broadcasted_iota(jnp.int32, (heads, columns), 0)).astype(F32)
    w = lax.dot_general(
        w_ref[...], spread.astype(BF16), (((0,), (0,)), ((), ())), preferred_element_type=F32
    )
    row_column = lax.broadcasted_iota(jnp.int32, (channels, columns), 1) % row_of
    xs, ws = [], []
    for i in range(rows):
        xs.append(normalised(pair_ref[i], gain_ref[...], shift_ref[...]))
        ws.append(jnp.where(row_column == step * rows + i, w, 0.0).astype(BF16))
        normed[step * rows + i] = xs[i]
    part = jnp.dot(
        jnp.concatenate(xs, axis=1), jnp.concatenate(ws, axis=0), preferred_element_type=F32
    )

    @pl.when(step == 0)
    def _():
        pltpu.make_async_copy(rows_ref, rows_s, rows_sem).start()
        acc[...] = part
        pick = picking(mask_ref[...], live)
        pick_ref[...] = pick
        chain_row = jnp.broadcast_to(chain_ref[...].astype(F32), (8, tokens)).astype(BF16)
        chain_live_ref[...] = lax.dot_general(chain_row, pick, NT, preferred_element_type=F32)

    @pl.when(step > 0)
    def _():
        acc[...] += part

    @pl.when(step == pl.num_programs(0) - 1)
    def _():
        full = acc[...].astype(BF16)
        taken = jnp.dot(pick_ref[...], full, preferred_element_type=F32)
        out_ref[...] = taken.T.astype(BF16)
        pltpu.make_async_copy(rows_ref, rows_s, rows_sem).wait()
        for i in range(window_ref.shape[0]):
            window_ref[i] = normed[lax.rem(rows_s[i], held)]


def key_value_kernel(own_ref, other_ref, pick_ref, w_ref, k_ref, v_ref):
    count = own_ref.shape[0]
    live, inner = v_ref.shape[1:]
    for i in range(count):
        both = jnp.concatenate([own_ref[i], other_ref[i]], axis=1)
        taken = jnp.dot(pick_ref[...], both, preferred_element_type=F32).astype(BF16)
        c = own_ref.shape[2]
        for part in range(2):
            kv = jnp.dot(
                taken[:, part * c : (part + 1) * c],
                w_ref[:, inner : 3 * inner],
                preferred_element_type=F32,
            ).astype(BF16)
            k_ref[i + part * count] = kv[:, :inner].T
            v_ref[i + part * count] = kv[:, inner:]


def attention_kernel(heads, ms, first, me_ref, chain_bias_ref, *refs):
    blocks = len(ms)
    bias_refs, refs = refs[:blocks], refs[blocks:]
    own_ref, other_ref, k_ref, v_ref, mask_ref, chain_ref, chain_live_ref = refs[:7]
    w_ref, gate_bias_ref, w_out_ref = refs[7:10]
    out_refs, (q_s, gate_s, added_s, gated_s) = refs[-4 - blocks : -4], refs[-4:]
    windows, inner, live = k_ref.shape
    half = windows // 2
    block = own_ref.shape[3]
    tokens = mask_ref.shape[1]
    size = inner // heads
    core, chip = lax.rem(me_ref[0], 2), lax.div(me_ref[0], 2)
    chain_live = chain_live_ref[0:1, :]
    lane_head = lax.broadcasted_iota(jnp.int32, (block, inner), 1) // size
    w_q = w_ref[:, :inner]
    w_g = w_ref[:, 3 * inner :]
    for b in range(blocks):
        at = lax.bitwise_xor(chip, ms[b])
        here = (
            lax.broadcasted_iota(jnp.int32, (block, tokens), 1)
            == (at * 2 + core) * block + lax.broadcasted_iota(jnp.int32, (block, tokens), 0)
        ).astype(F32)
        chain_here = jnp.sum(here * chain_ref[...].astype(F32), axis=1, keepdims=True)
        keep = jnp.sum(here * mask_ref[...].astype(F32), axis=1, keepdims=True)
        same = (chain_here == chain_live).astype(F32)
        for h in range(heads):
            rows = slice(h * block, (h + 1) * block)
            taken = pl.ds(first[b] + h * block, block)
            added_s[rows, :] = bias_refs[b][taken, :].astype(F32) + chain_bias_ref[h] * same
        for part, ref in enumerate((own_ref, other_ref)):
            x = ref[:, at, core].reshape(half * block, inner)
            span = pl.ds(part * half * block, half * block)
            q_s[span, :] = (
                jnp.dot(x, w_q, preferred_element_type=F32) * size ** (-0.5)
            ).astype(BF16)
            gate_s[span, :] = jax.nn.sigmoid(
                jnp.dot(x, w_g, preferred_element_type=F32) + gate_bias_ref[...]
            )

        def some_windows(g):
            spans = [
                slice((g * half + i) * block, (g * half + i + 1) * block) for i in range(half)
            ]
            scores = []
            for i in range(half):
                q = q_s[spans[i], :].astype(F32)
                spread = jnp.concatenate(
                    [jnp.where(lane_head == h, q, 0.0) for h in range(heads)], axis=0
                ).astype(BF16)
                scores.append(
                    jnp.dot(spread, k_ref[g * half + i], preferred_element_type=F32) + added_s[...]
                )
            tops = [jnp.max(s, axis=1, keepdims=True) for s in scores]
            raised = [jnp.exp(s - top) for s, top in zip(scores, tops)]
            shares = [1.0 / jnp.sum(r, axis=1, keepdims=True) for r in raised]
            mixed = [
                jnp.dot(r.astype(BF16), v_ref[g * half + i], preferred_element_type=F32)
                for i, r in enumerate(raised)
            ]
            for i in range(half):
                m = mixed[i] * shares[i]
                attended = m[0:block]
                for h in range(1, heads):
                    attended = jnp.where(lane_head == h, m[h * block : (h + 1) * block], attended)
                gated_s[spans[i], :] = (gate_s[spans[i], :] * attended).astype(BF16)

        for g in range(2):
            some_windows(g)
        result = jnp.dot(gated_s[...], w_out_ref[...], preferred_element_type=F32)
        result = (result.reshape(windows, block, inner) * keep[None]).astype(BF16)
        out_refs[b][pl.ds(core * half, half)] = result[:half]
        out_refs[b][pl.ds((1 - core) * half, half)] = result[half:]


def join_kernel(*refs):
    parts, out_ref = refs[:-2], refs[-1]
    rows = parts[0].shape[0]
    for i, part in enumerate(parts):
        out_ref[i * rows : (i + 1) * rows, :] = part[...]


def gather_kernel(order, me_ref, *refs):
    parts, out_ref, sems = refs[: len(order)], refs[-2], refs[-1]
    count = parts[0].shape[0]
    chip = lax.div(me_ref[0], 2)
    copies = []
    for i, part in enumerate(parts):
        at = lax.bitwise_xor(chip, order[i]) * count
        copies.append(pltpu.make_async_copy(part, out_ref.at[pl.ds(at, count)], sems.at[i]))
        copies[-1].start()
    for copy in copies:
        copy.wait()


def local(
    devices,
    pair,
    window_rows,
    token_mask,
    chain_ids,
    ln_gain,
    ln_shift,
    w_project,
    gate_bias,
    w_bias,
    chain_bias,
    w_out,
):
    rows_held, tokens, channels = pair.shape
    heads = w_bias.shape[1]
    inner = w_out.shape[0]
    count = window_rows.shape[0]
    live = tokens * 3 // 4
    owners = devices // 2
    me = lax.axis_index("row").astype(jnp.int32).reshape(1)
    mask_row = token_mask.reshape(1, tokens)
    chain_row = chain_ids.reshape(1, tokens)
    gain = ln_gain.reshape(1, channels)
    shift = ln_shift.reshape(1, channels)

    def swap(x, bits):
        return lax.ppermute(x, "row", [(i, i ^ bits) for i in range(devices)])

    step_rows = 16
    bias, own, pick, chain_live = pl.pallas_call(
        bias_kernel,
        grid=(rows_held // step_rows,),
        out_shape=[
            jax.ShapeDtypeStruct((heads * rows_held, live), BF16),
            jax.ShapeDtypeStruct((count, tokens, channels), BF16),
            jax.ShapeDtypeStruct((live, tokens), BF16),
            jax.ShapeDtypeStruct((8, live), F32),
        ],
        in_specs=[
            ANY,
            ANY,
            pl.BlockSpec((step_rows, tokens, channels), lambda i: (i, 0, 0)),
            pl.BlockSpec((1, tokens), lambda i: (0, 0)),
            pl.BlockSpec((1, tokens), lambda i: (0, 0)),
            pl.BlockSpec((1, channels), lambda i: (0, 0)),
            pl.BlockSpec((1, channels), lambda i: (0, 0)),
            pl.BlockSpec((heads, channels), lambda i: (0, 0)),
        ],
        out_specs=[
            pl.BlockSpec((heads * rows_held, live), lambda i: (0, 0)),
            pl.BlockSpec((count, tokens, channels), lambda i: (0, 0, 0)),
            pl.BlockSpec((live, tokens), lambda i: (0, 0)),
            pl.BlockSpec((8, live), lambda i: (0, 0)),
        ],
        scratch_shapes=[
            pltpu.VMEM((tokens, heads * rows_held), F32),
            pltpu.VMEM((rows_held, tokens, channels), BF16),
            pltpu.SMEM((count,), jnp.int32),
            pltpu.SemaphoreType.DMA(()),
        ],
        compiler_params=PARAMS,
        cost_estimate=measured(6),
    )(
        me,
        *[
            pltpu.with_memory_space_constraint(x, pltpu.HBM)
            for x in (window_rows, pair, mask_row, chain_row, gain, shift, w_bias.T)
        ]
    )

    far = [m for m in range(owners // 2, owners) if m % 2 == 0]
    passed = [m + 1 for m in far]
    near = list(range(1, owners // 2))
    biases = {0: bias}
    for m in far[::-1] + near[::-1]:
        biases[m] = swap(bias, 2 * m)
    other = swap(own, 1)

    keys, values = pl.pallas_call(
        key_value_kernel,
        out_shape=[
            jax.ShapeDtypeStruct((2 * count, inner, live), BF16),
            jax.ShapeDtypeStruct((2 * count, live, inner), BF16),
        ],
        in_specs=[VMEM] * 4,
        out_specs=[VMEM] * 2,
        compiler_params=PARAMS,
        cost_estimate=measured(2),
    )(own, other, pick, w_project)

    split = (count, owners, 2, rows_held, channels)
    own, other = own.reshape(split), other.reshape(split)
    updates = {}
    sent = {}
    head, rest = far[-1:], far[:-1]
    for ms in (head, rest, passed[-1:], passed[:-1], near[1:], [0] + near[:1]):
        if ms == head:
            after = []
        elif ms == rest:
            straight = pl.pallas_call(
                join_kernel,
                out_shape=jax.ShapeDtypeStruct((len(far) * heads * rows_held, live), BF16),
                in_specs=[VMEM] * len(far) + [ANY],
                out_specs=VMEM,
                compiler_params=PARAMS,
                cost_estimate=measured(0.5),
            )(*[biases[m] for m in far], updates[head[0]])
            straight = swap(straight, 2)
            for m in passed:
                biases[m] = straight
            after = [updates[head[0]]] + [biases[m] for m in near]
        elif ms == passed[-1:]:
            after = [updates[rest[0]]]
        elif ms == passed[:-1]:
            after = [updates[passed[-1]]]
        elif ms == near[1:]:
            after = [updates[m] for m in passed]
        else:
            after = [updates[near[1]]] + [sent[m] for m in head]
        blocks = len(ms)
        first = [passed.index(m) * heads * rows_held if m in passed else 0 for m in ms]
        rows = 2 * count * rows_held
        outs = pl.pallas_call(
            functools.partial(attention_kernel, heads, ms, first),
            out_shape=[jax.ShapeDtypeStruct((2 * count, rows_held, channels), BF16)] * blocks,
            in_specs=[SMEM, SMEM] + [VMEM] * (blocks + 10) + [ANY] * len(after),
            out_specs=[VMEM] * blocks,
            scratch_shapes=[
                pltpu.VMEM((rows, inner), BF16),
                pltpu.VMEM((rows, inner), F32),
                pltpu.VMEM((heads * rows_held, live), F32),
                pltpu.VMEM((rows, inner), BF16),
            ],
            compiler_params=PARAMS,
            cost_estimate=measured(2.2 * blocks),
        )(
            me,
            chain_bias,
            *[biases[m] for m in ms],
            own,
            other,
            keys,
            values,
            mask_row,
            chain_row,
            chain_live,
            w_project,
            gate_bias.reshape(1, inner),
            w_out,
            *after,
        )
        for m, out in zip(ms, outs):
            updates[m] = out
        for m, out in zip(ms, outs):
            sent[m] = out if m == 0 else swap(out, 2 * m)

    whole = []
    for order in (near[1:] + far + passed, [0] + near[:1]):
        placed = len(order)
        whole = [
            pl.pallas_call(
                functools.partial(gather_kernel, order),
                out_shape=jax.ShapeDtypeStruct((owners * 2 * count, rows_held, channels), BF16),
                in_specs=[SMEM] + [ANY] * (placed + len(whole)),
                out_specs=ANY,
                scratch_shapes=[pltpu.SemaphoreType.DMA((placed,))],
                input_output_aliases={placed + 1: 0} if whole else {},
                compiler_params=PARAMS,
                cost_estimate=measured(1),
            )(me, *[sent[m] for m in order], *whole)
        ]
    return whole[0]


def solution(mesh):
    placed = (
        P(("groups", "row"), None, None),
        P(("groups", "row")),
        P("groups"),
        P("groups"),
        P(),
        P(),
        P(),
        P(),
        P(),
        P(),
        P(),
    )
    return jax.shard_map(
        functools.partial(local, mesh.shape["row"]),
        mesh=mesh,
        in_specs=placed,
        out_specs=P("groups", "row", None),
        check_vma=False,
    )
```

```python
import functools

import jax
import jax.numpy as jnp
from jax import lax
from jax.experimental import pallas as pl
from jax.experimental.pallas import tpu as pltpu
from jax.sharding import PartitionSpec as P

F32, BF16 = jnp.float32, jnp.bfloat16
VMEM = pl.BlockSpec(memory_space=pltpu.VMEM)
SMEM = pl.BlockSpec(memory_space=pltpu.SMEM)
ANY = pl.BlockSpec(memory_space=pl.ANY)
NT = (((1,), (1,)), ((), ()))
PARAMS = pltpu.CompilerParams(vmem_limit_bytes=32 * 1024 * 1024)


def measured(microseconds):
    return pl.CostEstimate(
        flops=0, transcendentals=0, bytes_accessed=int(microseconds * 3.69e6)
    )


def normalised(rows, gain, shift):
    channels = rows.shape[-1]
    square = (channels, channels)
    diagonal = lax.broadcasted_iota(jnp.int32, square, 0) == lax.broadcasted_iota(
        jnp.int32, square, 1
    )
    centring = jnp.where(diagonal, 1.0 - 1.0 / channels, -1.0 / channels).astype(BF16)
    d = jnp.dot(rows, centring, preferred_element_type=F32)
    var = jnp.mean(d * d, axis=-1, keepdims=True)
    return (d * lax.rsqrt(var + 1e-05) * gain + shift).astype(BF16)


def live_ranks(mask_row):
    tokens = mask_row.shape[1]
    upper = lax.broadcasted_iota(jnp.int32, (tokens, tokens), 0) <= lax.broadcasted_iota(
        jnp.int32, (tokens, tokens), 1
    )
    ones = jnp.broadcast_to(mask_row.astype(F32), (8, tokens)).astype(BF16)
    running = jnp.dot(ones, upper.astype(F32).astype(BF16), preferred_element_type=F32)[0:1]
    return jnp.where(mask_row == 1, running - 1.0, -1.0)


def picking(mask_row, live):
    ranks = live_ranks(mask_row).astype(jnp.int32)
    wanted = lax.broadcasted_iota(jnp.int32, (live, mask_row.shape[1]), 0)
    return (wanted == ranks).astype(F32).astype(BF16)


def bias_kernel(
    me_ref,
    rows_ref,
    pair_ref,
    mask_ref,
    chain_ref,
    gain_ref,
    shift_ref,
    w_ref,
    out_ref,
    window_ref,
    pick_ref,
    chain_live_ref,
    acc,
    normed,
    rows_s,
    rows_sem,
):
    step = pl.program_id(0)
    rows, tokens, channels = pair_ref.shape
    columns, live = out_ref.shape
    held = rows * pl.num_programs(0)
    heads = w_ref.shape[0]
    row_of = columns // heads
    column = lax.broadcasted_iota(jnp.int32, (heads, columns), 1)
    spread = (column // row_of == lax.broadcasted_iota(jnp.int32, (heads, columns), 0)).astype(F32)
    w = lax.dot_general(
        w_ref[...], spread.astype(BF16), (((0,), (0,)), ((), ())), preferred_element_type=F32
    )
    row_column = lax.broadcasted_iota(jnp.int32, (channels, columns), 1) % row_of
    xs, ws = [], []
    for i in range(rows):
        xs.append(normalised(pair_ref[i], gain_ref[...], shift_ref[...]))
        ws.append(jnp.where(row_column == step * rows + i, w, 0.0).astype(BF16))
        normed[step * rows + i] = xs[i]
    part = jnp.dot(
        jnp.concatenate(xs, axis=1), jnp.concatenate(ws, axis=0), preferred_element_type=F32
    )

    @pl.when(step == 0)
    def _():
        pltpu.make_async_copy(rows_ref, rows_s, rows_sem).start()
        acc[...] = part
        pick = picking(mask_ref[...], live)
        pick_ref[...] = pick
        chain_row = jnp.broadcast_to(chain_ref[...].astype(F32), (8, tokens)).astype(BF16)
        chain_live_ref[...] = lax.dot_general(chain_row, pick, NT, preferred_element_type=F32)

    @pl.when(step > 0)
    def _():
        acc[...] += part

    @pl.when(step == pl.num_programs(0) - 1)
    def _():
        full = acc[...].astype(BF16)
        taken = jnp.dot(pick_ref[...], full, preferred_element_type=F32)
        out_ref[...] = taken.T.astype(BF16)
        pltpu.make_async_copy(rows_ref, rows_s, rows_sem).wait()
        for i in range(window_ref.shape[0]):
            window_ref[i] = normed[lax.rem(rows_s[i], held)]


def key_value_kernel(own_ref, other_ref, pick_ref, w_ref, k_ref, v_ref):
    count = own_ref.shape[0]
    live, inner = v_ref.shape[1:]
    for i in range(count):
        both = jnp.concatenate([own_ref[i], other_ref[i]], axis=1)
        taken = jnp.dot(pick_ref[...], both, preferred_element_type=F32).astype(BF16)
        c = own_ref.shape[2]
        for part in range(2):
            kv = jnp.dot(
                taken[:, part * c : (part + 1) * c],
                w_ref[:, inner : 3 * inner],
                preferred_element_type=F32,
            ).astype(BF16)
            k_ref[i + part * count] = kv[:, :inner].T
            v_ref[i + part * count] = kv[:, inner:]


def attention_kernel(heads, ms, first, me_ref, chain_bias_ref, *refs):
    blocks = len(ms)
    bias_refs, refs = refs[:blocks], refs[blocks:]
    own_ref, other_ref, k_ref, v_ref, mask_ref, chain_ref, chain_live_ref = refs[:7]
    w_ref, gate_bias_ref, w_out_ref = refs[7:10]
    out_refs, (q_s, gate_s, added_s, gated_s) = refs[-4 - blocks : -4], refs[-4:]
    windows, inner, live = k_ref.shape
    half = windows // 2
    block = own_ref.shape[3]
    tokens = mask_ref.shape[1]
    size = inner // heads
    core, chip = lax.rem(me_ref[0], 2), lax.div(me_ref[0], 2)
    chain_live = chain_live_ref[0:1, :]
    lane_head = lax.broadcasted_iota(jnp.int32, (block, inner), 1) // size
    w_q = w_ref[:, :inner]
    w_g = w_ref[:, 3 * inner :]
    for b in range(blocks):
        at = lax.bitwise_xor(chip, ms[b])
        here = (
            lax.broadcasted_iota(jnp.int32, (block, tokens), 1)
            == (at * 2 + core) * block + lax.broadcasted_iota(jnp.int32, (block, tokens), 0)
        ).astype(F32)
        chain_here = jnp.sum(here * chain_ref[...].astype(F32), axis=1, keepdims=True)
        keep = jnp.sum(here * mask_ref[...].astype(F32), axis=1, keepdims=True)
        same = (chain_here == chain_live).astype(F32)
        for h in range(heads):
            rows = slice(h * block, (h + 1) * block)
            taken = pl.ds(first[b] + h * block, block)
            added_s[rows, :] = bias_refs[b][taken, :].astype(F32) + chain_bias_ref[h] * same
        for part, ref in enumerate((own_ref, other_ref)):
            x = ref[:, at, core].reshape(half * block, inner)
            span = pl.ds(part * half * block, half * block)
            q_s[span, :] = (
                jnp.dot(x, w_q, preferred_element_type=F32) * size ** (-0.5)
            ).astype(BF16)
            gate_s[span, :] = jax.nn.sigmoid(
                jnp.dot(x, w_g, preferred_element_type=F32) + gate_bias_ref[...]
            )

        def some_windows(g):
            spans = [
                slice((g * half + i) * block, (g * half + i + 1) * block) for i in range(half)
            ]
            scores = []
            for i in range(half):
                q = q_s[spans[i], :].astype(F32)
                spread = jnp.concatenate(
                    [jnp.where(lane_head == h, q, 0.0) for h in range(heads)], axis=0
                ).astype(BF16)
                scores.append(
                    jnp.dot(spread, k_ref[g * half + i], preferred_element_type=F32) + added_s[...]
                )
            tops = [jnp.max(s, axis=1, keepdims=True) for s in scores]
            raised = [jnp.exp(s - top) for s, top in zip(scores, tops)]
            shares = [1.0 / jnp.sum(r, axis=1, keepdims=True) for r in raised]
            mixed = [
                jnp.dot(r.astype(BF16), v_ref[g * half + i], preferred_element_type=F32)
                for i, r in enumerate(raised)
            ]
            for i in range(half):
                m = mixed[i] * shares[i]
                attended = m[0:block]
                for h in range(1, heads):
                    attended = jnp.where(lane_head == h, m[h * block : (h + 1) * block], attended)
                gated_s[spans[i], :] = (gate_s[spans[i], :] * attended).astype(BF16)

        for g in range(2):
            some_windows(g)
        result = jnp.dot(gated_s[...], w_out_ref[...], preferred_element_type=F32)
        result = (result.reshape(windows, block, inner) * keep[None]).astype(BF16)
        out_refs[b][pl.ds(core * half, half)] = result[:half]
        out_refs[b][pl.ds((1 - core) * half, half)] = result[half:]


def join_kernel(*refs):
    parts, out_ref = refs[:-2], refs[-1]
    rows = parts[0].shape[0]
    for i, part in enumerate(parts):
        out_ref[i * rows : (i + 1) * rows, :] = part[...]


def gather_kernel(order, me_ref, *refs):
    parts, out_ref, sems = refs[: len(order)], refs[-2], refs[-1]
    count = parts[0].shape[0]
    chip = lax.div(me_ref[0], 2)
    copies = []
    for i, part in enumerate(parts):
        at = lax.bitwise_xor(chip, order[i]) * count
        copies.append(pltpu.make_async_copy(part, out_ref.at[pl.ds(at, count)], sems.at[i]))
        copies[-1].start()
    for copy in copies:
        copy.wait()


def local(
    devices,
    pair,
    window_rows,
    token_mask,
    chain_ids,
    ln_gain,
    ln_shift,
    w_project,
    gate_bias,
    w_bias,
    chain_bias,
    w_out,
):
    rows_held, tokens, channels = pair.shape
    heads = w_bias.shape[1]
    inner = w_out.shape[0]
    count = window_rows.shape[0]
    live = tokens * 3 // 4
    owners = devices // 2
    me = lax.axis_index("row").astype(jnp.int32).reshape(1)
    mask_row = token_mask.reshape(1, tokens)
    chain_row = chain_ids.reshape(1, tokens)
    gain = ln_gain.reshape(1, channels)
    shift = ln_shift.reshape(1, channels)

    def swap(x, bits):
        return lax.ppermute(x, "row", [(i, i ^ bits) for i in range(devices)])

    step_rows = 16
    bias, own, pick, chain_live = pl.pallas_call(
        bias_kernel,
        grid=(rows_held // step_rows,),
        out_shape=[
            jax.ShapeDtypeStruct((heads * rows_held, live), BF16),
            jax.ShapeDtypeStruct((count, tokens, channels), BF16),
            jax.ShapeDtypeStruct((live, tokens), BF16),
            jax.ShapeDtypeStruct((8, live), F32),
        ],
        in_specs=[
            ANY,
            ANY,
            pl.BlockSpec((step_rows, tokens, channels), lambda i: (i, 0, 0)),
            pl.BlockSpec((1, tokens), lambda i: (0, 0)),
            pl.BlockSpec((1, tokens), lambda i: (0, 0)),
            pl.BlockSpec((1, channels), lambda i: (0, 0)),
            pl.BlockSpec((1, channels), lambda i: (0, 0)),
            pl.BlockSpec((heads, channels), lambda i: (0, 0)),
        ],
        out_specs=[
            pl.BlockSpec((heads * rows_held, live), lambda i: (0, 0)),
            pl.BlockSpec((count, tokens, channels), lambda i: (0, 0, 0)),
            pl.BlockSpec((live, tokens), lambda i: (0, 0)),
            pl.BlockSpec((8, live), lambda i: (0, 0)),
        ],
        scratch_shapes=[
            pltpu.VMEM((tokens, heads * rows_held), F32),
            pltpu.VMEM((rows_held, tokens, channels), BF16),
            pltpu.SMEM((count,), jnp.int32),
            pltpu.SemaphoreType.DMA(()),
        ],
        compiler_params=PARAMS,
        cost_estimate=measured(6),
    )(
        me,
        *[
            pltpu.with_memory_space_constraint(x, pltpu.HBM)
            for x in (window_rows, pair, mask_row, chain_row, gain, shift, w_bias.T)
        ]
    )

    far = [m for m in range(owners // 2, owners) if m % 2 == 0]
    passed = [m + 1 for m in far]
    near = list(range(1, owners // 2))
    biases = {0: bias}
    for m in far[::-1] + near[::-1]:
        biases[m] = swap(bias, 2 * m)
    other = swap(own, 1)

    keys, values = pl.pallas_call(
        key_value_kernel,
        out_shape=[
            jax.ShapeDtypeStruct((2 * count, inner, live), BF16),
            jax.ShapeDtypeStruct((2 * count, live, inner), BF16),
        ],
        in_specs=[VMEM] * 4,
        out_specs=[VMEM] * 2,
        compiler_params=PARAMS,
        cost_estimate=measured(2),
    )(own, other, pick, w_project)

    split = (count, owners, 2, rows_held, channels)
    own, other = own.reshape(split), other.reshape(split)
    updates = {}
    sent = {}
    head, rest = far[:1], far[1:]
    for ms in (head, rest, passed, near[1:], [0] + near[:1]):
        if ms == head:
            after = []
        elif ms == rest:
            straight = pl.pallas_call(
                join_kernel,
                out_shape=jax.ShapeDtypeStruct((len(far) * heads * rows_held, live), BF16),
                in_specs=[VMEM] * len(far) + [ANY],
                out_specs=VMEM,
                compiler_params=PARAMS,
                cost_estimate=measured(0.5),
            )(*[biases[m] for m in far], updates[head[0]])
            straight = swap(straight, 2)
            for m in passed:
                biases[m] = straight
            after = [updates[head[0]]] + [biases[m] for m in near]
        elif ms == passed:
            after = [updates[rest[0]]]
        elif ms == near[1:]:
            after = [updates[m] for m in passed]
        else:
            after = [updates[near[1]]] + [sent[m] for m in head]
        blocks = len(ms)
        first = [i * heads * rows_held if ms == passed else 0 for i in range(blocks)]
        rows = 2 * count * rows_held
        outs = pl.pallas_call(
            functools.partial(attention_kernel, heads, ms, first),
            out_shape=[jax.ShapeDtypeStruct((2 * count, rows_held, channels), BF16)] * blocks,
            in_specs=[SMEM, SMEM] + [VMEM] * (blocks + 10) + [ANY] * len(after),
            out_specs=[VMEM] * blocks,
            scratch_shapes=[
                pltpu.VMEM((rows, inner), BF16),
                pltpu.VMEM((rows, inner), F32),
                pltpu.VMEM((heads * rows_held, live), F32),
                pltpu.VMEM((rows, inner), BF16),
            ],
            compiler_params=PARAMS,
            cost_estimate=measured(2.2 * blocks),
        )(
            me,
            chain_bias,
            *[biases[m] for m in ms],
            own,
            other,
            keys,
            values,
            mask_row,
            chain_row,
            chain_live,
            w_project,
            gate_bias.reshape(1, inner),
            w_out,
            *after,
        )
        for m, out in zip(ms, outs):
            updates[m] = out
        for m, out in zip(ms, outs):
            sent[m] = out if m == 0 else swap(out, 2 * m)

    whole = []
    for order in (near[1:] + far + passed, [0] + near[:1]):
        placed = len(order)
        whole = [
            pl.pallas_call(
                functools.partial(gather_kernel, order),
                out_shape=jax.ShapeDtypeStruct((owners * 2 * count, rows_held, channels), BF16),
                in_specs=[SMEM] + [ANY] * (placed + len(whole)),
                out_specs=ANY,
                scratch_shapes=[pltpu.SemaphoreType.DMA((placed,))],
                input_output_aliases={placed + 1: 0} if whole else {},
                compiler_params=PARAMS,
                cost_estimate=measured(1),
            )(me, *[sent[m] for m in order], *whole)
        ]
    return whole[0]


def solution(mesh):
    placed = (
        P(("groups", "row"), None, None),
        P(("groups", "row")),
        P("groups"),
        P("groups"),
        P(),
        P(),
        P(),
        P(),
        P(),
        P(),
        P(),
    )
    return jax.shard_map(
        functools.partial(local, mesh.shape["row"]),
        mesh=mesh,
        in_specs=placed,
        out_specs=P("groups", "row", None),
        check_vma=False,
    )
```

```python
import functools

import jax
import jax.numpy as jnp
from jax import lax
from jax.experimental import pallas as pl
from jax.experimental.pallas import tpu as pltpu
from jax.sharding import PartitionSpec as P

F32, BF16 = jnp.float32, jnp.bfloat16
VMEM = pl.BlockSpec(memory_space=pltpu.VMEM)
SMEM = pl.BlockSpec(memory_space=pltpu.SMEM)
ANY = pl.BlockSpec(memory_space=pl.ANY)
NT = (((1,), (1,)), ((), ()))
PARAMS = pltpu.CompilerParams(vmem_limit_bytes=32 * 1024 * 1024)


def measured(microseconds):
    return pl.CostEstimate(
        flops=0, transcendentals=0, bytes_accessed=int(microseconds * 3.69e6)
    )


def normalised(rows, gain, shift):
    channels = rows.shape[-1]
    square = (channels, channels)
    diagonal = lax.broadcasted_iota(jnp.int32, square, 0) == lax.broadcasted_iota(
        jnp.int32, square, 1
    )
    centring = jnp.where(diagonal, 1.0 - 1.0 / channels, -1.0 / channels).astype(BF16)
    d = jnp.dot(rows, centring, preferred_element_type=F32)
    var = jnp.mean(d * d, axis=-1, keepdims=True)
    return (d * lax.rsqrt(var + 1e-05) * gain + shift).astype(BF16)


def live_ranks(mask_row):
    tokens = mask_row.shape[1]
    upper = lax.broadcasted_iota(jnp.int32, (tokens, tokens), 0) <= lax.broadcasted_iota(
        jnp.int32, (tokens, tokens), 1
    )
    ones = jnp.broadcast_to(mask_row.astype(F32), (8, tokens)).astype(BF16)
    running = jnp.dot(ones, upper.astype(F32).astype(BF16), preferred_element_type=F32)[0:1]
    return jnp.where(mask_row == 1, running - 1.0, -1.0)


def picking(mask_row, live):
    ranks = live_ranks(mask_row).astype(jnp.int32)
    wanted = lax.broadcasted_iota(jnp.int32, (live, mask_row.shape[1]), 0)
    return (wanted == ranks).astype(F32).astype(BF16)


def bias_kernel(
    me_ref,
    rows_ref,
    pair_ref,
    mask_ref,
    chain_ref,
    gain_ref,
    shift_ref,
    w_ref,
    out_ref,
    window_ref,
    pick_ref,
    chain_live_ref,
    acc,
    normed,
    rows_s,
    rows_sem,
):
    step = pl.program_id(0)
    rows, tokens, channels = pair_ref.shape
    columns, live = out_ref.shape
    held = rows * pl.num_programs(0)
    heads = w_ref.shape[0]
    row_of = columns // heads
    column = lax.broadcasted_iota(jnp.int32, (heads, columns), 1)
    spread = (column // row_of == lax.broadcasted_iota(jnp.int32, (heads, columns), 0)).astype(F32)
    w = lax.dot_general(
        w_ref[...], spread.astype(BF16), (((0,), (0,)), ((), ())), preferred_element_type=F32
    )
    row_column = lax.broadcasted_iota(jnp.int32, (channels, columns), 1) % row_of
    xs, ws = [], []
    for i in range(rows):
        xs.append(normalised(pair_ref[i], gain_ref[...], shift_ref[...]))
        ws.append(jnp.where(row_column == step * rows + i, w, 0.0).astype(BF16))
        normed[step * rows + i] = xs[i]
    part = jnp.dot(
        jnp.concatenate(xs, axis=1), jnp.concatenate(ws, axis=0), preferred_element_type=F32
    )

    @pl.when(step == 0)
    def _():
        pltpu.make_async_copy(rows_ref, rows_s, rows_sem).start()
        acc[...] = part
        pick = picking(mask_ref[...], live)
        pick_ref[...] = pick
        chain_row = jnp.broadcast_to(chain_ref[...].astype(F32), (8, tokens)).astype(BF16)
        chain_live_ref[...] = lax.dot_general(chain_row, pick, NT, preferred_element_type=F32)

    @pl.when(step > 0)
    def _():
        acc[...] += part

    @pl.when(step == pl.num_programs(0) - 1)
    def _():
        full = acc[...].astype(BF16)
        taken = jnp.dot(pick_ref[...], full, preferred_element_type=F32)
        out_ref[...] = taken.T.astype(BF16)
        pltpu.make_async_copy(rows_ref, rows_s, rows_sem).wait()
        for i in range(window_ref.shape[0]):
            window_ref[i] = normed[lax.rem(rows_s[i], held)]


def key_value_kernel(own_ref, other_ref, pick_ref, w_ref, k_ref, v_ref):
    count = own_ref.shape[0]
    live, inner = v_ref.shape[1:]
    for i in range(count):
        both = jnp.concatenate([own_ref[i], other_ref[i]], axis=1)
        taken = jnp.dot(pick_ref[...], both, preferred_element_type=F32).astype(BF16)
        c = own_ref.shape[2]
        for part in range(2):
            kv = jnp.dot(
                taken[:, part * c : (part + 1) * c],
                w_ref[:, inner : 3 * inner],
                preferred_element_type=F32,
            ).astype(BF16)
            k_ref[i + part * count] = kv[:, :inner].T
            v_ref[i + part * count] = kv[:, inner:]


def attention_kernel(heads, ms, first, me_ref, chain_bias_ref, *refs):
    blocks = len(ms)
    bias_refs, refs = refs[:blocks], refs[blocks:]
    own_ref, other_ref, k_ref, v_ref, mask_ref, chain_ref, chain_live_ref = refs[:7]
    w_ref, gate_bias_ref, w_out_ref = refs[7:10]
    out_refs, (q_s, gate_s, added_s, gated_s) = refs[-4 - blocks : -4], refs[-4:]
    windows, inner, live = k_ref.shape
    half = windows // 2
    block = own_ref.shape[3]
    tokens = mask_ref.shape[1]
    size = inner // heads
    core, chip = lax.rem(me_ref[0], 2), lax.div(me_ref[0], 2)
    chain_live = chain_live_ref[0:1, :]
    lane_head = lax.broadcasted_iota(jnp.int32, (block, inner), 1) // size
    w_q = w_ref[:, :inner]
    w_g = w_ref[:, 3 * inner :]
    for b in range(blocks):
        at = lax.bitwise_xor(chip, ms[b])
        here = (
            lax.broadcasted_iota(jnp.int32, (block, tokens), 1)
            == (at * 2 + core) * block + lax.broadcasted_iota(jnp.int32, (block, tokens), 0)
        ).astype(F32)
        chain_here = jnp.sum(here * chain_ref[...].astype(F32), axis=1, keepdims=True)
        keep = jnp.sum(here * mask_ref[...].astype(F32), axis=1, keepdims=True)
        same = (chain_here == chain_live).astype(F32)
        for h in range(heads):
            rows = slice(h * block, (h + 1) * block)
            taken = pl.ds(first[b] + h * block, block)
            added_s[rows, :] = bias_refs[b][taken, :].astype(F32) + chain_bias_ref[h] * same
        for part, ref in enumerate((own_ref, other_ref)):
            x = ref[:, at, core].reshape(half * block, inner)
            span = pl.ds(part * half * block, half * block)
            q_s[span, :] = (
                jnp.dot(x, w_q, preferred_element_type=F32) * size ** (-0.5)
            ).astype(BF16)
            gate_s[span, :] = jax.nn.sigmoid(
                jnp.dot(x, w_g, preferred_element_type=F32) + gate_bias_ref[...]
            )

        def some_windows(g):
            spans = [
                slice((g * half + i) * block, (g * half + i + 1) * block) for i in range(half)
            ]
            scores = []
            for i in range(half):
                q = q_s[spans[i], :].astype(F32)
                spread = jnp.concatenate(
                    [jnp.where(lane_head == h, q, 0.0) for h in range(heads)], axis=0
                ).astype(BF16)
                scores.append(
                    jnp.dot(spread, k_ref[g * half + i], preferred_element_type=F32) + added_s[...]
                )
            tops = [jnp.max(s, axis=1, keepdims=True) for s in scores]
            raised = [jnp.exp(s - top) for s, top in zip(scores, tops)]
            shares = [1.0 / jnp.sum(r, axis=1, keepdims=True) for r in raised]
            mixed = [
                jnp.dot(r.astype(BF16), v_ref[g * half + i], preferred_element_type=F32)
                for i, r in enumerate(raised)
            ]
            for i in range(half):
                m = mixed[i] * shares[i]
                attended = m[0:block]
                for h in range(1, heads):
                    attended = jnp.where(lane_head == h, m[h * block : (h + 1) * block], attended)
                gated_s[spans[i], :] = (gate_s[spans[i], :] * attended).astype(BF16)

        for g in range(2):
            some_windows(g)
        result = jnp.dot(gated_s[...], w_out_ref[...], preferred_element_type=F32)
        result = (result.reshape(windows, block, inner) * keep[None]).astype(BF16)
        out_refs[b][pl.ds(core * half, half)] = result[:half]
        out_refs[b][pl.ds((1 - core) * half, half)] = result[half:]


def join_kernel(*refs):
    parts, out_ref = refs[:-2], refs[-1]
    rows = parts[0].shape[0]
    for i, part in enumerate(parts):
        out_ref[i * rows : (i + 1) * rows, :] = part[...]


def gather_kernel(order, me_ref, *refs):
    parts, out_ref, sems = refs[: len(order)], refs[-2], refs[-1]
    count = parts[0].shape[0]
    chip = lax.div(me_ref[0], 2)
    copies = []
    for i, part in enumerate(parts):
        at = lax.bitwise_xor(chip, order[i]) * count
        copies.append(pltpu.make_async_copy(part, out_ref.at[pl.ds(at, count)], sems.at[i]))
        copies[-1].start()
    for copy in copies:
        copy.wait()


def local(
    devices,
    pair,
    window_rows,
    token_mask,
    chain_ids,
    ln_gain,
    ln_shift,
    w_project,
    gate_bias,
    w_bias,
    chain_bias,
    w_out,
):
    rows_held, tokens, channels = pair.shape
    heads = w_bias.shape[1]
    inner = w_out.shape[0]
    count = window_rows.shape[0]
    live = tokens * 3 // 4
    owners = devices // 2
    me = lax.axis_index("row").astype(jnp.int32).reshape(1)
    mask_row = token_mask.reshape(1, tokens)
    chain_row = chain_ids.reshape(1, tokens)
    gain = ln_gain.reshape(1, channels)
    shift = ln_shift.reshape(1, channels)

    def swap(x, bits):
        return lax.ppermute(x, "row", [(i, i ^ bits) for i in range(devices)])

    step_rows = 16
    bias, own, pick, chain_live = pl.pallas_call(
        bias_kernel,
        grid=(rows_held // step_rows,),
        out_shape=[
            jax.ShapeDtypeStruct((heads * rows_held, live), BF16),
            jax.ShapeDtypeStruct((count, tokens, channels), BF16),
            jax.ShapeDtypeStruct((live, tokens), BF16),
            jax.ShapeDtypeStruct((8, live), F32),
        ],
        in_specs=[
            ANY,
            ANY,
            pl.BlockSpec((step_rows, tokens, channels), lambda i: (i, 0, 0)),
            pl.BlockSpec((1, tokens), lambda i: (0, 0)),
            pl.BlockSpec((1, tokens), lambda i: (0, 0)),
            pl.BlockSpec((1, channels), lambda i: (0, 0)),
            pl.BlockSpec((1, channels), lambda i: (0, 0)),
            pl.BlockSpec((heads, channels), lambda i: (0, 0)),
        ],
        out_specs=[
            pl.BlockSpec((heads * rows_held, live), lambda i: (0, 0)),
            pl.BlockSpec((count, tokens, channels), lambda i: (0, 0, 0)),
            pl.BlockSpec((live, tokens), lambda i: (0, 0)),
            pl.BlockSpec((8, live), lambda i: (0, 0)),
        ],
        scratch_shapes=[
            pltpu.VMEM((tokens, heads * rows_held), F32),
            pltpu.VMEM((rows_held, tokens, channels), BF16),
            pltpu.SMEM((count,), jnp.int32),
            pltpu.SemaphoreType.DMA(()),
        ],
        compiler_params=PARAMS,
        cost_estimate=measured(6),
    )(
        me,
        *[
            pltpu.with_memory_space_constraint(x, pltpu.HBM)
            for x in (window_rows, pair, mask_row, chain_row, gain, shift, w_bias.T)
        ]
    )

    far = [m for m in range(owners // 2, owners) if m % 2 == 0]
    passed = [m + 1 for m in far]
    near = list(range(1, owners // 2))
    biases = {0: bias}
    for m in far[::-1] + near[::-1]:
        biases[m] = swap(bias, 2 * m)
    other = swap(own, 1)

    keys, values = pl.pallas_call(
        key_value_kernel,
        out_shape=[
            jax.ShapeDtypeStruct((2 * count, inner, live), BF16),
            jax.ShapeDtypeStruct((2 * count, live, inner), BF16),
        ],
        in_specs=[VMEM] * 4,
        out_specs=[VMEM] * 2,
        compiler_params=PARAMS,
        cost_estimate=measured(2),
    )(own, other, pick, w_project)

    split = (count, owners, 2, rows_held, channels)
    own, other = own.reshape(split), other.reshape(split)
    updates = {}
    sent = {}
    head, rest = far[-1:], far[:-1]
    for ms in (head, rest, passed, near[1:], [0] + near[:1]):
        if ms == head:
            after = []
        elif ms == rest:
            straight = pl.pallas_call(
                join_kernel,
                out_shape=jax.ShapeDtypeStruct((len(far) * heads * rows_held, live), BF16),
                in_specs=[VMEM] * len(far) + [ANY],
                out_specs=VMEM,
                compiler_params=PARAMS,
                cost_estimate=measured(0.5),
            )(*[biases[m] for m in far], updates[head[0]])
            straight = swap(straight, 2)
            for m in passed:
                biases[m] = straight
            after = [updates[head[0]]] + [biases[m] for m in near]
        elif ms == passed:
            after = [updates[rest[0]]]
        elif ms == near[1:]:
            after = [updates[m] for m in passed] + [sent[m] for m in head]
        else:
            after = [updates[near[1]]] + [sent[m] for m in head]
        blocks = len(ms)
        first = [i * heads * rows_held if ms == passed else 0 for i in range(blocks)]
        rows = 2 * count * rows_held
        outs = pl.pallas_call(
            functools.partial(attention_kernel, heads, ms, first),
            out_shape=[jax.ShapeDtypeStruct((2 * count, rows_held, channels), BF16)] * blocks,
            in_specs=[SMEM, SMEM] + [VMEM] * (blocks + 10) + [ANY] * len(after),
            out_specs=[VMEM] * blocks,
            scratch_shapes=[
                pltpu.VMEM((rows, inner), BF16),
                pltpu.VMEM((rows, inner), F32),
                pltpu.VMEM((heads * rows_held, live), F32),
                pltpu.VMEM((rows, inner), BF16),
            ],
            compiler_params=PARAMS,
            cost_estimate=measured(0.2 * blocks),
        )(
            me,
            chain_bias,
            *[biases[m] for m in ms],
            own,
            other,
            keys,
            values,
            mask_row,
            chain_row,
            chain_live,
            w_project,
            gate_bias.reshape(1, inner),
            w_out,
            *after,
        )
        for m, out in zip(ms, outs):
            updates[m] = out
        for m, out in zip(ms, outs):
            sent[m] = out if m == 0 else swap(out, 2 * m)

    whole = []
    for order in (near[1:] + far + passed, [0] + near[:1]):
        placed = len(order)
        whole = [
            pl.pallas_call(
                functools.partial(gather_kernel, order),
                out_shape=jax.ShapeDtypeStruct((owners * 2 * count, rows_held, channels), BF16),
                in_specs=[SMEM] + [ANY] * (placed + len(whole)),
                out_specs=ANY,
                scratch_shapes=[pltpu.SemaphoreType.DMA((placed,))],
                input_output_aliases={placed + 1: 0} if whole else {},
                compiler_params=PARAMS,
                cost_estimate=measured(1),
            )(me, *[sent[m] for m in order], *whole)
        ]
    return whole[0]


def solution(mesh):
    placed = (
        P(("groups", "row"), None, None),
        P(("groups", "row")),
        P("groups"),
        P("groups"),
        P(),
        P(),
        P(),
        P(),
        P(),
        P(),
        P(),
    )
    return jax.shard_map(
        functools.partial(local, mesh.shape["row"]),
        mesh=mesh,
        in_specs=placed,
        out_specs=P("groups", "row", None),
        check_vma=False,
    )
```
